32 devices in a mesh: parts: 2 (over y), clus: 4 (over z), mem: 2 (over x), sub: 2 (over core).
Axes of the slice: x: 2, y: 2, z: 4, core: 2. Of those that a mesh axis runs over, the one named last changes fastest.
Arguments:
- embeddings: bfloat16 [4096, 1024], P(('parts', 'clus', 'mem', 'sub')), parts along dimension 0, as said below
- labels: int32 [4096], P(('parts', 'clus', 'mem', 'sub')), parts along dimension 0, may hold values from 0 to 15, as said below
- member_rank: int32 [4096], P(('parts', 'clus', 'mem', 'sub')), parts along dimension 0, may hold values from 0 to 2047, each once
Outputs:
- nearest: float32 [4096], P(('parts', 'clus', 'mem', 'sub')), parts along dimension 0
The draws below stay inside these ranges and needn't reach their ends.
There are 2 independent parts, one for each index of `parts`. The reference program is written for one: setup_inputs(seed, part) draws one part's arguments, and reference() takes and returns one part's arrays. A program takes and returns all parts, laid end to end along the dimension named above; each array names one. Nothing has to cross between parts.
Inputs may be any that keep to these rules, and one draw needn't show every extreme that they name: `embeddings`: each row has unit length up to rounding. Among the rows of one device, at most 32 have labels in any one group of 2 consecutive clusters (label // 2); on every device some group has exactly 32.
All inputs are finite; a program needn't handle non-finite values.
Results may differ from the reference program's by a relative error of at most 0.0003.
Values may be sent and summed in bfloat16 or wider, within the bound.
No kernel may reach another device: no remote copies, remote signals or barrier semaphores. Data moves between devices by JAX's collectives and lax.ppermute only.
A program may use at most 64 MiB of HBM per device.

```python
import jax
import jax.numpy as jnp
from jax import lax

D = 1024
ROWS_DEV = 128
CLUS_GROUP = 2
GROUPS = 8
CAPACITY = 32
SLOTS = 256
SHARDS = 16
MEMBERS = 2048
CLUSTERS = 16


def member_layout(key):
    base = jax.random.fold_in(key, 11)
    key_full, key_score, key_shuffle, key_first, key_second = jax.random.split(base, 5)
    full_group = jax.random.randint(key_full, (SHARDS,), 0, GROUPS)
    scores = jax.random.randint(key_score, (SHARDS, SLOTS), 0, 1 << 20)
    slot_group = jnp.arange(SLOTS, dtype=jnp.int32) // CAPACITY
    scores = jnp.where(slot_group[None, :] == full_group[:, None], -1, scores)
    chosen = jnp.argsort(scores, axis=1, stable=True)[:, :ROWS_DEV].astype(jnp.int32)
    shuffle_key = jax.random.randint(key_shuffle, (SHARDS, ROWS_DEV), 0, 1 << 20)
    shuffle_order = jnp.argsort(shuffle_key, axis=1, stable=True)
    chosen = jnp.take_along_axis(chosen, shuffle_order, axis=1)
    within = jnp.minimum(jax.random.randint(key_first, (SHARDS, ROWS_DEV), 0, CLUS_GROUP), jax.random.randint(key_second, (SHARDS, ROWS_DEV), 0, CLUS_GROUP))
    label_all = chosen // CAPACITY * CLUS_GROUP + within
    return label_all.reshape(-1).astype(jnp.int32)


def draw_labels(key, part):
    return member_layout(key)


def draw_embeddings(key, part):
    label_all = member_layout(key)
    key_centre, key_weight, key_noise = jax.random.split(jax.random.fold_in(key, 23), 3)
    centre = jax.random.normal(key_centre, (CLUSTERS, D), jnp.float32)
    centre = centre / jnp.sqrt(jnp.sum(centre * centre, axis=1, keepdims=True))
    weight = jax.random.uniform(key_weight, (MEMBERS, 1), jnp.float32, 0.2, 0.95)
    noise_vec = jax.random.normal(key_noise, (MEMBERS, D), jnp.float32)
    noise_vec = noise_vec / jnp.sqrt(jnp.sum(noise_vec * noise_vec, axis=1, keepdims=True))
    mixed_vec = weight * centre[label_all] + jnp.sqrt(1.0 - weight * weight) * noise_vec
    mixed_vec = mixed_vec / jnp.sqrt(jnp.sum(mixed_vec * mixed_vec, axis=1, keepdims=True))
    return mixed_vec.astype(jnp.bfloat16)


def setup_inputs(seed: int = 0, part: int = 0) -> dict:
    key_list = jax.random.split(jax.random.key(seed), 4)
    own_keys = jax.random.split(jax.random.fold_in(key_list[3], part), 4)
    embeddings = draw_embeddings(jax.random.fold_in(jax.random.fold_in(key_list[3], part), 71), part)
    labels = draw_labels(jax.random.fold_in(jax.random.fold_in(key_list[3], part), 71), part)
    member_rank = jax.random.permutation(own_keys[2], MEMBERS).astype(jnp.int32)
    return dict(embeddings=embeddings, labels=labels, member_rank=member_rank)


def reference(embeddings, labels, member_rank):
    group_of = labels // CLUS_GROUP
    member_count = embeddings.shape[0]
    group_width = SHARDS * CAPACITY

    def per_group(group_id):
        in_group = group_of == group_id
        member_idx = jnp.nonzero(in_group, size=group_width, fill_value=0)[0].astype(jnp.int32)
        live_slot = jnp.arange(group_width) < jnp.sum(in_group)
        slot_emb = embeddings[member_idx]
        slot_label = jnp.where(live_slot, labels[member_idx], -1)
        slot_rank = member_rank[member_idx]
        scores = jnp.dot(slot_emb, slot_emb.T, preferred_element_type=jnp.float32)
        allowed = (slot_label[:, None] == slot_label[None, :]) & (slot_label[:, None] >= 0)
        allowed = allowed & (slot_rank[None, :] < slot_rank[:, None])
        nearest = jnp.max(jnp.where(allowed, scores, jnp.float32(-1.0)), axis=1)
        return jnp.where(live_slot, member_idx, member_count), nearest

    all_idx, all_best = lax.map(per_group, jnp.arange(GROUPS, dtype=jnp.int32))
    result = jnp.full((member_count,), -1.0, jnp.float32)
    return result.at[all_idx.reshape(-1)].set(all_best.reshape(-1), mode="drop")
```

```python
import math

import jax
import jax.numpy as jnp
from jax import lax
from jax.experimental import pallas as pl
from jax.experimental.pallas import tpu as pltpu
from jax.sharding import PartitionSpec as P

CLUS_GROUP = 2
LANES = 128
META_ROWS = 16
DIGIT = 256
VMEM_LIMIT = 16 * 1024 * 1024
NT = (((1,), (1,)), ((), ()))


def swapped(value, axis, stride):
    mask = 2**stride
    pairs = [(source, source ^ mask) for source in range(lax.axis_size(axis))]
    return lax.ppermute(value, axis, pairs)


def masked_best(row_emb, row_label, row_rank, col_emb, col_label, col_rank, want_columns):
    col_count = col_emb.shape[0]
    block_size = math.gcd(512, col_count)
    block_count = col_count // block_size
    emb_blocks = col_emb.reshape(block_count, block_size, col_emb.shape[1])
    label_blocks = col_label.reshape(block_count, block_size)
    rank_blocks = col_rank.reshape(block_count, block_size)

    def visit_block(running, column_piece):
        piece_emb, piece_label, piece_rank = column_piece
        scores = lax.dot_general(
            row_emb, piece_emb, (((1,), (1,)), ((), ())), preferred_element_type=jnp.float32
        )
        same_cluster = (row_label[:, None] == piece_label[None, :]) & (row_label[:, None] >= 0)
        earlier = piece_rank[None, :] < row_rank[:, None]
        row_best = jnp.max(jnp.where(same_cluster & earlier, scores, jnp.float32(-1.0)), axis=1)
        if want_columns:
            later = same_cluster & jnp.logical_not(earlier)
            col_best = jnp.max(jnp.where(later, scores, jnp.float32(-1.0)), axis=0)
        else:
            col_best = jnp.zeros((0,), jnp.float32)
        return (jnp.maximum(running, row_best), col_best)

    initial = jnp.full((row_emb.shape[0],), -1.0, jnp.float32)
    row_best, col_blocks = lax.scan(visit_block, initial, (emb_blocks, label_blocks, rank_blocks))
    return (row_best, col_blocks.reshape(-1))


def narrow_body(embeddings, labels, member_rank):
    row_count = embeddings.shape[0]
    feature_count = embeddings.shape[1]
    group_count = lax.axis_size("clus") * lax.axis_size("mem")
    capacity = 2 * row_count // group_count
    slot_count = group_count * capacity
    group_of = labels // CLUS_GROUP
    one_hot = (group_of[:, None] == jnp.arange(group_count, dtype=jnp.int32)[None, :]).astype(
        jnp.int32
    )
    running_count = jnp.cumsum(one_hot, axis=0) - 1
    within_group = jnp.sum(one_hot * running_count, axis=1)
    slot_of = group_of * capacity + within_group
    send_emb = jnp.zeros((slot_count, feature_count), jnp.bfloat16).at[slot_of].set(embeddings)
    send_label = jnp.full((slot_count,), -1, jnp.int32).at[slot_of].set(labels)
    send_rank = jnp.zeros((slot_count,), jnp.int32).at[slot_of].set(member_rank)

    def exchanged(value):
        return lax.all_to_all(value, ("clus", "mem"), split_axis=0, concat_axis=0, tiled=True)

    own_emb = exchanged(send_emb.reshape(group_count, capacity, feature_count))
    own_emb = own_emb.reshape(slot_count, feature_count)
    own_label = exchanged(send_label.reshape(group_count, capacity)).reshape(slot_count)
    own_rank = exchanged(send_rank.reshape(group_count, capacity)).reshape(slot_count)
    other_emb, other_label, other_rank = swapped((own_emb, own_label, own_rank), "sub", 0)
    diag_best, ignored = masked_best(
        own_emb, own_label, own_rank, own_emb, own_label, own_rank, False
    )
    cross_best, ignored = masked_best(
        own_emb, own_label, own_rank, other_emb, other_label, other_rank, False
    )
    nearest = jnp.maximum(diag_best, cross_best)
    returned = exchanged(nearest.reshape(group_count, capacity))
    return returned.reshape(-1)[slot_of]


def one_hot_slots(slot_row, slot_count):
    slot_id = lax.broadcasted_iota(jnp.int32, (slot_count, slot_row.shape[1]), 0)
    return slot_id == slot_row


def route_kernel(group_count, capacity, me_ref, label_ref, rank_ref, emb_ref, slot_ref, *messages):
    row_count, feature_count = emb_ref.shape
    chunk_count = feature_count // LANES
    slot_count = group_count * capacity
    label = label_ref[...]
    rank = rank_ref[...]
    offset = (label // CLUS_GROUP) ^ me_ref[0]
    hot = lax.broadcasted_iota(jnp.int32, (group_count, row_count), 0) == offset
    hot = hot.astype(jnp.float32)
    before = lax.broadcasted_iota(jnp.int32, (row_count, row_count), 0) < (
        lax.broadcasted_iota(jnp.int32, (row_count, row_count), 1)
    )
    count = jnp.dot(
        hot.astype(jnp.bfloat16),
        before.astype(jnp.float32).astype(jnp.bfloat16),
        preferred_element_type=jnp.float32,
    )
    within = jnp.sum(hot * count, axis=0, keepdims=True).astype(jnp.int32)
    slot = offset * capacity + within
    slot_ref[...] = slot
    place = one_hot_slots(slot, slot_count).astype(jnp.float32).astype(jnp.bfloat16)
    kind = lax.broadcasted_iota(jnp.int32, (META_ROWS, row_count), 0)
    digits = jnp.where(
        kind == 0,
        label % CLUS_GROUP + 1,
        jnp.where(kind == 1, rank // DIGIT, jnp.where(kind == 2, rank % DIGIT, 0)),
    )
    digits = digits.astype(jnp.float32).astype(jnp.bfloat16)
    meta = lax.dot_general(digits, place, NT, preferred_element_type=jnp.float32)
    meta = meta.astype(jnp.bfloat16)
    for index, message in enumerate(messages):
        rows = place[index * capacity : (index + 1) * capacity]
        placed = jnp.dot(rows, emb_ref[...], preferred_element_type=jnp.float32)
        placed = placed.astype(jnp.bfloat16)
        for chunk in range(chunk_count):
            message[chunk * capacity : (chunk + 1) * capacity, :] = placed[
                :, chunk * LANES : (chunk + 1) * LANES
            ]
        lane_block = index * capacity // LANES
        message[chunk_count * capacity :, :] = meta[
            :, lane_block * LANES : (lane_block + 1) * LANES
        ]


def gathered_meta(messages, capacity):
    per_tile = LANES // capacity
    tiles = []
    lane = lax.broadcasted_iota(jnp.int32, (META_ROWS, LANES), 1) // capacity
    for first in range(0, len(messages), per_tile):
        tile = jnp.zeros((META_ROWS, LANES), jnp.float32)
        for step, message in enumerate(messages[first : first + per_tile]):
            piece = message[message.shape[0] - META_ROWS :, :].astype(jnp.float32)
            tile = jnp.where(lane == step, piece, tile)
        tiles.append(tile)
    return jnp.concatenate(tiles, axis=1)


def gathered_rows(messages, capacity):
    rows = []
    for message in messages:
        chunk_count = (message.shape[0] - META_ROWS) // capacity
        rows.append(
            jnp.concatenate(
                [message[c * capacity : (c + 1) * capacity, :] for c in range(chunk_count)], axis=1
            )
        )
    return jnp.concatenate(rows, axis=0)


def score_kernel(capacity, *refs):
    message_count = (len(refs) - 1) // 2
    own, other, best_ref = refs[:message_count], refs[message_count:-1], refs[-1]
    own_meta = gathered_meta(own, capacity)
    own_rows = gathered_rows(own, capacity)
    own_label = own_meta[0:1]
    own_rank = own_meta[1:2] * DIGIT + own_meta[2:3]
    best = jnp.full(own_label.shape, -1.0, jnp.float32)
    for messages in (own, other):
        if messages is own:
            meta, rows = own_meta, own_rows
        else:
            meta, rows = gathered_meta(messages, capacity), gathered_rows(messages, capacity)
        column = jnp.transpose(meta)
        label = column[:, 0:1]
        rank = column[:, 1:2] * DIGIT + column[:, 2:3]
        scores = lax.dot_general(rows, own_rows, NT, preferred_element_type=jnp.float32)
        allowed = (label == own_label) & (rank < own_rank)
        scores = jnp.where(allowed, scores, jnp.float32(-1.0))
        best = jnp.maximum(best, jnp.max(scores, axis=0, keepdims=True))
    best_ref[...] = best


def pick_kernel(capacity, slot_ref, *refs):
    returned, out_ref = refs[:-1], refs[-1]
    slot_count = returned[0].shape[1]
    lane = lax.broadcasted_iota(jnp.int32, (1, slot_count), 1) // capacity
    value = returned[0][...]
    for index in range(1, len(returned)):
        value = jnp.where(lane == index, returned[index][...], value)
    high = value.astype(jnp.bfloat16)
    rest = value - high.astype(jnp.float32)
    middle = rest.astype(jnp.bfloat16)
    low = (rest - middle.astype(jnp.float32)).astype(jnp.bfloat16)
    place = one_hot_slots(slot_ref[...], slot_count).astype(jnp.float32).astype(jnp.bfloat16)
    parts = [jnp.dot(p, place, preferred_element_type=jnp.float32) for p in (high, middle, low)]
    out_ref[...] = parts[0] + (parts[1] + parts[2])


def wide_body(embeddings, labels, member_rank):
    row_count, feature_count = embeddings.shape
    groups = ("clus", "mem")
    group_count = lax.axis_size("clus") * lax.axis_size("mem")
    capacity = 2 * row_count // group_count
    slot_count = group_count * capacity
    message_rows = feature_count // LANES * capacity + META_ROWS
    params = pltpu.CompilerParams(vmem_limit_bytes=VMEM_LIMIT)
    vmem = pl.BlockSpec(memory_space=pltpu.VMEM)
    smem = pl.BlockSpec(memory_space=pltpu.SMEM)
    me = lax.axis_index(groups).astype(jnp.int32).reshape(1)

    def moved(value, offset):
        return lax.ppermute(value, groups, [(s, s ^ offset) for s in range(group_count)])

    slot, *messages = pl.pallas_call(
        lambda *refs: route_kernel(group_count, capacity, *refs),
        out_shape=[jax.ShapeDtypeStruct((1, row_count), jnp.int32)]
        + [jax.ShapeDtypeStruct((message_rows, LANES), jnp.bfloat16)] * group_count,
        in_specs=[smem, vmem, vmem, vmem],
        out_specs=[vmem] * (group_count + 1),
        compiler_params=params,
        name="route",
    )(me, labels.reshape(1, row_count), member_rank.reshape(1, row_count), embeddings)

    own = [None] * group_count
    own[0] = messages[0]
    for offset in range(group_count - 1, 0, -1):
        own[offset] = moved(messages[offset], offset)
    other = [swapped(message, "sub", 0) for message in own]
    best = pl.pallas_call(
        lambda *refs: score_kernel(capacity, *refs),
        out_shape=jax.ShapeDtypeStruct((1, slot_count), jnp.float32),
        in_specs=[vmem] * (2 * group_count),
        out_specs=vmem,
        compiler_params=params,
        name="score",
    )(*own, *other)
    returned = [best] + [moved(best, offset) for offset in range(1, group_count)]
    nearest = pl.pallas_call(
        lambda *refs: pick_kernel(capacity, *refs),
        out_shape=jax.ShapeDtypeStruct((1, row_count), jnp.float32),
        in_specs=[vmem] * (group_count + 1),
        out_specs=vmem,
        compiler_params=params,
        name="pick",
    )(slot, *returned)
    return nearest.reshape(row_count)


def body(embeddings, labels, member_rank):
    row_count, feature_count = embeddings.shape
    group_count = lax.axis_size("clus") * lax.axis_size("mem")
    capacity = 2 * row_count // group_count
    member_count = row_count * group_count * lax.axis_size("sub")
    wide = (
        capacity % META_ROWS == 0
        and LANES % capacity == 0
        and group_count * capacity % LANES == 0
        and group_count & (group_count - 1) == 0
        and feature_count % LANES == 0
        and row_count % LANES == 0
        and member_count <= DIGIT * DIGIT
    )
    return (wide_body if wide else narrow_body)(embeddings, labels, member_rank)


def solution(mesh):
    placed = (
        P(("parts", "clus", "mem", "sub"), None),
        P(("parts", "clus", "mem", "sub")),
        P(("parts", "clus", "mem", "sub")),
    )
    return jax.shard_map(
        body,
        mesh=mesh,
        in_specs=placed,
        out_specs=P(("parts", "clus", "mem", "sub")),
        check_vma=False,
    )
```

```python
import math

import jax
import jax.numpy as jnp
from jax import lax
from jax.experimental import pallas as pl
from jax.experimental.pallas import tpu as pltpu
from jax.sharding import PartitionSpec as P

CLUS_GROUP = 2
LANES = 128
META_ROWS = 16
DIGIT = 256
VMEM_LIMIT = 16 * 1024 * 1024
NT = (((1,), (1,)), ((), ()))


def swapped(value, axis, stride):
    mask = 2**stride
    pairs = [(source, source ^ mask) for source in range(lax.axis_size(axis))]
    return lax.ppermute(value, axis, pairs)


def masked_best(row_emb, row_label, row_rank, col_emb, col_label, col_rank, want_columns):
    col_count = col_emb.shape[0]
    block_size = math.gcd(512, col_count)
    block_count = col_count // block_size
    emb_blocks = col_emb.reshape(block_count, block_size, col_emb.shape[1])
    label_blocks = col_label.reshape(block_count, block_size)
    rank_blocks = col_rank.reshape(block_count, block_size)

    def visit_block(running, column_piece):
        piece_emb, piece_label, piece_rank = column_piece
        scores = lax.dot_general(
            row_emb, piece_emb, (((1,), (1,)), ((), ())), preferred_element_type=jnp.float32
        )
        same_cluster = (row_label[:, None] == piece_label[None, :]) & (row_label[:, None] >= 0)
        earlier = piece_rank[None, :] < row_rank[:, None]
        row_best = jnp.max(jnp.where(same_cluster & earlier, scores, jnp.float32(-1.0)), axis=1)
        if want_columns:
            later = same_cluster & jnp.logical_not(earlier)
            col_best = jnp.max(jnp.where(later, scores, jnp.float32(-1.0)), axis=0)
        else:
            col_best = jnp.zeros((0,), jnp.float32)
        return (jnp.maximum(running, row_best), col_best)

    initial = jnp.full((row_emb.shape[0],), -1.0, jnp.float32)
    row_best, col_blocks = lax.scan(visit_block, initial, (emb_blocks, label_blocks, rank_blocks))
    return (row_best, col_blocks.reshape(-1))


def narrow_body(embeddings, labels, member_rank):
    row_count = embeddings.shape[0]
    feature_count = embeddings.shape[1]
    group_count = lax.axis_size("clus") * lax.axis_size("mem")
    capacity = 2 * row_count // group_count
    slot_count = group_count * capacity
    group_of = labels // CLUS_GROUP
    one_hot = (group_of[:, None] == jnp.arange(group_count, dtype=jnp.int32)[None, :]).astype(
        jnp.int32
    )
    running_count = jnp.cumsum(one_hot, axis=0) - 1
    within_group = jnp.sum(one_hot * running_count, axis=1)
    slot_of = group_of * capacity + within_group
    send_emb = jnp.zeros((slot_count, feature_count), jnp.bfloat16).at[slot_of].set(embeddings)
    send_label = jnp.full((slot_count,), -1, jnp.int32).at[slot_of].set(labels)
    send_rank = jnp.zeros((slot_count,), jnp.int32).at[slot_of].set(member_rank)

    def exchanged(value):
        return lax.all_to_all(value, ("clus", "mem"), split_axis=0, concat_axis=0, tiled=True)

    own_emb = exchanged(send_emb.reshape(group_count, capacity, feature_count))
    own_emb = own_emb.reshape(slot_count, feature_count)
    own_label = exchanged(send_label.reshape(group_count, capacity)).reshape(slot_count)
    own_rank = exchanged(send_rank.reshape(group_count, capacity)).reshape(slot_count)
    other_emb, other_label, other_rank = swapped((own_emb, own_label, own_rank), "sub", 0)
    diag_best, ignored = masked_best(
        own_emb, own_label, own_rank, own_emb, own_label, own_rank, False
    )
    cross_best, ignored = masked_best(
        own_emb, own_label, own_rank, other_emb, other_label, other_rank, False
    )
    nearest = jnp.maximum(diag_best, cross_best)
    returned = exchanged(nearest.reshape(group_count, capacity))
    return returned.reshape(-1)[slot_of]


def score_kernel(
    here_ref, plane_meta_ref, line_meta_ref, line_ref, plane_ref, best_ref
):
    block_rows = plane_meta_ref.shape[2]
    best = []
    line_label = []
    line_rank = []
    for block in range(line_meta_ref.shape[0]):
        column = jnp.transpose(line_meta_ref[block].astype(jnp.float32))
        line_label.append(column[:, 0:1])
        line_rank.append(column[:, 1:2])
    line_label = jnp.concatenate(line_label, axis=0)
    line_rank = jnp.concatenate(line_rank, axis=0)
    for block in range(plane_meta_ref.shape[0]):
        rows = plane_ref[block * block_rows : (block + 1) * block_rows, :]
        meta = plane_meta_ref[block].astype(jnp.float32)
        scores = lax.dot_general(line_ref[...], rows, NT, preferred_element_type=jnp.float32)
        allowed = (line_label == meta[0:1]) & (line_rank < meta[1:2])
        scores = jnp.where(allowed, scores, jnp.float32(-1.0))
        best.append(jnp.max(scores, axis=0, keepdims=True))
    best_ref[...] = jnp.concatenate(best, axis=1)


def wide_body(embeddings, labels, member_rank):
    row_count, feature_count = embeddings.shape
    plane_axes = ("mem", "sub")
    plane_count = lax.axis_size("mem") * lax.axis_size("sub")
    params = pltpu.CompilerParams(vmem_limit_bytes=VMEM_LIMIT)
    vmem = pl.BlockSpec(memory_space=pltpu.VMEM)
    smem = pl.BlockSpec(memory_space=pltpu.SMEM)
    here = lax.axis_index(plane_axes).astype(jnp.int32)
    meta = jnp.concatenate(
        [labels.reshape(1, row_count), member_rank.reshape(1, row_count)]
        + [jnp.zeros((6, row_count), jnp.int32)]
    )
    line = lax.all_gather(embeddings, "clus", axis=0, tiled=True)
    line_meta = lax.all_gather(meta, "clus", axis=0, tiled=False)
    plane = lax.all_gather(embeddings, plane_axes, axis=0, tiled=True)
    plane_meta = lax.all_gather(meta, plane_axes, axis=0, tiled=False)
    best = pl.pallas_call(
        score_kernel,
        out_shape=jax.ShapeDtypeStruct((1, plane_count * row_count), jnp.float32),
        in_specs=[smem] + [vmem] * 4,
        out_specs=vmem,
        compiler_params=params,
        name="score",
    )(here.reshape(1), plane_meta, line_meta, line, plane)
    best = jnp.maximum(best, swapped(best, "sub", 0))
    mem_count = lax.axis_size("mem")
    total = best
    for step in range(1, mem_count):
        shift = [(s, (s + step) % mem_count) for s in range(mem_count)]
        total = jnp.maximum(total, lax.ppermute(best, "mem", shift))
    return lax.dynamic_slice_in_dim(total.reshape(-1), here * row_count, row_count)


def body(embeddings, labels, member_rank):
    row_count, feature_count = embeddings.shape
    group_count = lax.axis_size("clus") * lax.axis_size("mem")
    capacity = 2 * row_count // group_count
    member_count = row_count * group_count * lax.axis_size("sub")
    wide = (
        capacity % META_ROWS == 0
        and LANES % capacity == 0
        and group_count * capacity % LANES == 0
        and group_count & (group_count - 1) == 0
        and feature_count % LANES == 0
        and row_count % LANES == 0
        and member_count <= DIGIT * DIGIT
    )
    return (wide_body if wide else narrow_body)(embeddings, labels, member_rank)


def solution(mesh):
    placed = (
        P(("parts", "clus", "mem", "sub"), None),
        P(("parts", "clus", "mem", "sub")),
        P(("parts", "clus", "mem", "sub")),
    )
    return jax.shard_map(
        body,
        mesh=mesh,
        in_specs=placed,
        out_specs=P(("parts", "clus", "mem", "sub")),
        check_vma=False,
    )
```

```python
import math

import jax
import jax.numpy as jnp
from jax import lax
from jax.experimental import pallas as pl
from jax.experimental.pallas import tpu as pltpu
from jax.sharding import PartitionSpec as P

CLUS_GROUP = 2
LANES = 128
META_ROWS = 16
DIGIT = 256
VMEM_LIMIT = 16 * 1024 * 1024
NT = (((1,), (1,)), ((), ()))


def swapped(value, axis, stride):
    mask = 2**stride
    pairs = [(source, source ^ mask) for source in range(lax.axis_size(axis))]
    return lax.ppermute(value, axis, pairs)


def masked_best(row_emb, row_label, row_rank, col_emb, col_label, col_rank, want_columns):
    col_count = col_emb.shape[0]
    block_size = math.gcd(512, col_count)
    block_count = col_count // block_size
    emb_blocks = col_emb.reshape(block_count, block_size, col_emb.shape[1])
    label_blocks = col_label.reshape(block_count, block_size)
    rank_blocks = col_rank.reshape(block_count, block_size)

    def visit_block(running, column_piece):
        piece_emb, piece_label, piece_rank = column_piece
        scores = lax.dot_general(
            row_emb, piece_emb, (((1,), (1,)), ((), ())), preferred_element_type=jnp.float32
        )
        same_cluster = (row_label[:, None] == piece_label[None, :]) & (row_label[:, None] >= 0)
        earlier = piece_rank[None, :] < row_rank[:, None]
        row_best = jnp.max(jnp.where(same_cluster & earlier, scores, jnp.float32(-1.0)), axis=1)
        if want_columns:
            later = same_cluster & jnp.logical_not(earlier)
            col_best = jnp.max(jnp.where(later, scores, jnp.float32(-1.0)), axis=0)
        else:
            col_best = jnp.zeros((0,), jnp.float32)
        return (jnp.maximum(running, row_best), col_best)

    initial = jnp.full((row_emb.shape[0],), -1.0, jnp.float32)
    row_best, col_blocks = lax.scan(visit_block, initial, (emb_blocks, label_blocks, rank_blocks))
    return (row_best, col_blocks.reshape(-1))


def narrow_body(embeddings, labels, member_rank):
    row_count = embeddings.shape[0]
    feature_count = embeddings.shape[1]
    group_count = lax.axis_size("clus") * lax.axis_size("mem")
    capacity = 2 * row_count // group_count
    slot_count = group_count * capacity
    group_of = labels // CLUS_GROUP
    one_hot = (group_of[:, None] == jnp.arange(group_count, dtype=jnp.int32)[None, :]).astype(
        jnp.int32
    )
    running_count = jnp.cumsum(one_hot, axis=0) - 1
    within_group = jnp.sum(one_hot * running_count, axis=1)
    slot_of = group_of * capacity + within_group
    send_emb = jnp.zeros((slot_count, feature_count), jnp.bfloat16).at[slot_of].set(embeddings)
    send_label = jnp.full((slot_count,), -1, jnp.int32).at[slot_of].set(labels)
    send_rank = jnp.zeros((slot_count,), jnp.int32).at[slot_of].set(member_rank)

    def exchanged(value):
        return lax.all_to_all(value, ("clus", "mem"), split_axis=0, concat_axis=0, tiled=True)

    own_emb = exchanged(send_emb.reshape(group_count, capacity, feature_count))
    own_emb = own_emb.reshape(slot_count, feature_count)
    own_label = exchanged(send_label.reshape(group_count, capacity)).reshape(slot_count)
    own_rank = exchanged(send_rank.reshape(group_count, capacity)).reshape(slot_count)
    other_emb, other_label, other_rank = swapped((own_emb, own_label, own_rank), "sub", 0)
    diag_best, ignored = masked_best(
        own_emb, own_label, own_rank, own_emb, own_label, own_rank, False
    )
    cross_best, ignored = masked_best(
        own_emb, own_label, own_rank, other_emb, other_label, other_rank, False
    )
    nearest = jnp.maximum(diag_best, cross_best)
    returned = exchanged(nearest.reshape(group_count, capacity))
    return returned.reshape(-1)[slot_of]


def best_kernel(
    line_count, plane_count, place_ref, meta_ref, *refs
):
    blocks, table_ref = refs[:-1], refs[-1]
    lines, others = blocks[:line_count], blocks[line_count:]
    rows = lines[0].shape[0]

    def meta_of(block):
        place = place_ref[block]
        meta = meta_ref[jnp.maximum(place, 0)]
        return jnp.where(place >= 0, meta[0:1], -1), meta[1:2]

    line_label, line_rank = [], []
    for block in range(line_count):
        label, rank = meta_of(block)
        pair = jnp.concatenate([label, rank] + [rank] * 6, axis=0).astype(jnp.float32)
        column = jnp.transpose(pair)
        line_label.append(column[:, 0:1])
        line_rank.append(column[:, 1:2])
    line_label = jnp.concatenate(line_label, axis=0)
    line_rank = jnp.concatenate(line_rank, axis=0)
    line_rows = jnp.concatenate([line[...] for line in lines], axis=0)

    table_ref[...] = jnp.full(table_ref.shape, -1.0, jnp.float32)

    def keep(block, value):
        place = pl.ds(jnp.maximum(place_ref[block], 0), 1)
        table_ref[place, :] = jnp.maximum(table_ref[place, :], value)

    line_best = jnp.full((line_count * rows, rows), -1.0, jnp.float32)
    for index, other in enumerate(others):
        block = line_count + index
        label, rank = meta_of(block)
        label, rank = label.astype(jnp.float32), rank.astype(jnp.float32)
        scores = lax.dot_general(line_rows, other[...], NT, preferred_element_type=jnp.float32)
        same = jnp.where((line_label == label) & (label >= 0), scores, jnp.float32(-1.0))
        forward = jnp.where(line_rank < rank, same, jnp.float32(-1.0))
        backward = jnp.where(line_rank > rank, same, jnp.float32(-1.0))
        keep(block, jnp.max(forward, axis=0, keepdims=True))
        line_best = jnp.maximum(line_best, backward)
    for block in range(line_count):
        piece = line_best[block * rows : (block + 1) * rows]
        keep(block, jnp.max(jnp.transpose(piece), axis=0, keepdims=True))


def blind_body(embeddings, labels, member_rank):
    row_count, feature_count = embeddings.shape
    slab_axes = ("clus", "mem", "sub")
    clus_count = lax.axis_size("clus")
    mem_count = lax.axis_size("mem")
    sub_count = lax.axis_size("sub")
    slab_count = clus_count * mem_count * sub_count
    hub = clus_count // 2
    clus = lax.axis_index("clus")
    mem = lax.axis_index("mem")
    sub = lax.axis_index("sub")

    def shifted(value, clus_pairs, mem_shift):
        pairs = [
            (source * mem_count + m, target * mem_count + (m + mem_shift) % mem_count)
            for source, target in clus_pairs
            for m in range(mem_count)
        ]
        return lax.ppermute(value, ("clus", "mem"), pairs)

    def placed(clus_from, mem_shift, sub_from, there):
        mem_from = (mem - mem_shift) % mem_count
        place = (clus_from * mem_count + mem_from) * sub_count + sub_from
        return jnp.where(there, place, -1).astype(jnp.int32)

    lines, line_places = [embeddings], [placed(clus, 0, sub, True)]
    for distance in range(1, hub + 1):
        pairs = [(z, z + distance) for z in range(hub + 1 - distance)]
        lines.append(shifted(embeddings, pairs, 0))
        there = (clus >= distance) & (clus <= hub)
        line_places.append(placed(clus - distance, 0, sub, there))

    others, other_places = [], []
    for shift in range(mem_count):
        if shift:
            other = shifted(embeddings, [(z, z) for z in range(clus_count)], shift)
        else:
            other = embeddings
        others.append(other)
        other_places.append(placed(clus, shift, sub, True))
        others.append(swapped(other, "sub", 0))
        other_places.append(placed(clus, shift, 1 - sub, True))
    for distance in range(1, clus_count - hub):
        for shift in range(mem_count):
            other = shifted(embeddings, [(hub + distance, hub)], shift)
            others.append(other)
            other_places.append(placed(clus + distance, shift, sub, clus == hub))
            others.append(swapped(other, "sub", 0))
            other_places.append(placed(clus + distance, shift, 1 - sub, clus == hub))

    meta = jnp.concatenate([labels.reshape(1, row_count), member_rank.reshape(1, row_count)])
    meta = lax.all_gather(meta, slab_axes, axis=0, tiled=False)
    vmem = pl.BlockSpec(memory_space=pltpu.VMEM)
    smem = pl.BlockSpec(memory_space=pltpu.SMEM)
    block_count = len(lines) + len(others)
    table = pl.pallas_call(
        lambda *refs: best_kernel(len(lines), mem_count * sub_count, *refs),
        out_shape=jax.ShapeDtypeStruct((slab_count, row_count), jnp.float32),
        in_specs=[smem] + [vmem] * (1 + block_count),
        out_specs=vmem,
        compiler_params=pltpu.CompilerParams(vmem_limit_bytes=VMEM_LIMIT),
        name="best",
    )(jnp.stack(line_places + other_places), meta, *lines, *others)
    table = lax.pmax(table, slab_axes)
    here = placed(clus, 0, sub, True)
    return lax.dynamic_slice_in_dim(table.reshape(-1), here * row_count, row_count)


def body(embeddings, labels, member_rank):
    row_count, feature_count = embeddings.shape
    blind = (
        lax.axis_size("clus") <= 4
        and lax.axis_size("sub") == 2
        and feature_count % LANES == 0
        and row_count == LANES
    )
    return (blind_body if blind else narrow_body)(embeddings, labels, member_rank)


def solution(mesh):
    placed = (
        P(("parts", "clus", "mem", "sub"), None),
        P(("parts", "clus", "mem", "sub")),
        P(("parts", "clus", "mem", "sub")),
    )
    return jax.shard_map(
        body,
        mesh=mesh,
        in_specs=placed,
        out_specs=P(("parts", "clus", "mem", "sub")),
        check_vma=False,
    )
```

```python
import jax
import jax.numpy as jnp
from jax import lax
from jax.experimental import pallas as pl
from jax.experimental.pallas import tpu as pltpu
from jax.sharding import PartitionSpec as P

LANES = 128
META_ROWS = 16
DIGIT = 256
VMEM_LIMIT = 24 * 1024 * 1024
NT = (((1,), (1,)), ((), ()))
NONE = -1.0


def pack_kernel(label_ref, rank_ref, emb_ref, message_ref, sems):
    rows, features = emb_ref.shape
    chunks = features // LANES
    copies = [
        pltpu.make_async_copy(
            emb_ref.at[:, pl.ds(chunk * LANES, LANES)],
            message_ref.at[pl.ds(chunk * rows, rows), :],
            sems.at[chunk],
        )
        for chunk in range(chunks)
    ]
    for copy in copies:
        copy.start()
    kind = lax.broadcasted_iota(jnp.int32, (META_ROWS, rows), 0)
    rank = rank_ref[...]
    meta = jnp.where(kind == 0, label_ref[...], 0)
    meta = jnp.where(kind == 1, rank // DIGIT, meta)
    meta = jnp.where(kind == 2, rank % DIGIT, meta)
    message_ref[pl.ds(chunks * rows, META_ROWS), :] = meta.astype(jnp.float32).astype(jnp.bfloat16)
    for copy in copies:
        copy.wait()


def rows_of(message):
    rows = message.shape[1]
    chunks = message.shape[0] // rows
    return jnp.concatenate([message[c * rows : (c + 1) * rows, :] for c in range(chunks)], axis=1)


def meta_of(message):
    meta = message[message.shape[0] - META_ROWS :, :].astype(jnp.float32)
    return meta[0:1], meta[1:2] * DIGIT + meta[2:3]


def best_kernel(line_count, back_count, mem_count, sub_count, *refs):
    plane_count = mem_count * sub_count
    lines = refs[:line_count]
    plane = refs[line_count : line_count + plane_count]
    outs = refs[line_count + plane_count :]
    plane_outs, back_outs = outs[:sub_count], outs[sub_count:]
    rows = lines[0].shape[1]

    line_rows = jnp.concatenate([rows_of(line) for line in lines], axis=0)
    columns = []
    for line in lines:
        label, rank = meta_of(line)
        columns.append(jnp.transpose(jnp.concatenate([label, rank] + [rank] * 6, axis=0)))
    columns = jnp.concatenate(columns, axis=0)
    line_label, line_rank = columns[:, 0:1], columns[:, 1:2]

    back = [None] * back_count
    for shift in range(mem_count):
        blocks = plane[shift * sub_count : (shift + 1) * sub_count]
        plane_rows = jnp.concatenate([rows_of(block) for block in blocks], axis=0)
        metas = [meta_of(block) for block in blocks]
        label = jnp.concatenate([meta[0] for meta in metas], axis=1)
        rank = jnp.concatenate([meta[1] for meta in metas], axis=1)
        scores = lax.dot_general(line_rows, plane_rows, NT, preferred_element_type=jnp.float32)
        scores = jnp.where(line_label == label, scores, NONE)
        forward = jnp.where(line_rank < rank, scores, NONE)
        best = jnp.max(forward, axis=0, keepdims=True)
        for turn in range(sub_count):
            plane_outs[turn][shift : shift + 1, :] = best[:, turn * rows : (turn + 1) * rows]
        for index in range(back_count):
            piece = slice((index + 1) * rows, (index + 2) * rows)
            backward = jnp.where(line_rank[piece] > rank, scores[piece], NONE)
            for turn in range(sub_count):
                part = backward[:, turn * rows : (turn + 1) * rows]
                back[index] = part if back[index] is None else jnp.maximum(back[index], part)
    for index in range(back_count):
        back_outs[index][...] = jnp.max(jnp.transpose(back[index]), axis=0, keepdims=True)


def body(embeddings, labels, member_rank):
    row_count, feature_count = embeddings.shape
    clus_count = lax.axis_size("clus")
    mem_count = lax.axis_size("mem")
    sub_count = lax.axis_size("sub")
    chunk_count = feature_count // LANES
    vmem = pl.BlockSpec(memory_space=pltpu.VMEM)
    params = pltpu.CompilerParams(vmem_limit_bytes=VMEM_LIMIT)

    def shifted(value, axis, order, distance):
        count = len(order)
        pairs = [(order[i], order[(i + distance) % count]) for i in range(count)]
        return lax.ppermute(value, axis, pairs)

    half = (clus_count + 1) // 2
    ring = [z for pair in zip(range(half), range(half, 2 * half)) for z in pair if z < clus_count]
    mem_order = list(range(mem_count))
    sub_order = list(range(sub_count))

    message = pl.pallas_call(
        pack_kernel,
        out_shape=jax.ShapeDtypeStruct((chunk_count * row_count + META_ROWS, LANES), jnp.bfloat16),
        in_specs=[vmem, vmem, pl.BlockSpec(memory_space=pl.ANY)],
        out_specs=vmem,
        scratch_shapes=[pltpu.SemaphoreType.DMA((chunk_count,))],
        compiler_params=params,
        name="pack",
    )(labels.reshape(1, row_count), member_rank.reshape(1, row_count), embeddings)

    distances = list(range(1, clus_count // 2 + 1))
    one_way = [d for d in distances if 2 * d != clus_count]
    lines = [message] + [shifted(message, "clus", ring, d) for d in distances]
    plane = []
    for shift in range(mem_count):
        block = shifted(message, "mem", mem_order, shift) if shift else message
        plane.append(block)
        plane.extend(shifted(block, "sub", sub_order, turn) for turn in range(1, sub_count))

    outs = pl.pallas_call(
        lambda *refs: best_kernel(len(lines), len(one_way), mem_count, sub_count, *refs),
        out_shape=[jax.ShapeDtypeStruct((mem_count, row_count), jnp.float32)] * sub_count
        + [jax.ShapeDtypeStruct((1, row_count), jnp.float32)] * len(one_way),
        in_specs=[vmem] * (len(lines) + len(plane)),
        out_specs=[vmem] * (sub_count + len(one_way)),
        compiler_params=params,
        name="best",
    )(*lines, *plane)
    table = outs[0]
    for turn in range(1, sub_count):
        table = jnp.maximum(table, shifted(outs[turn], "sub", sub_order, -turn))
    nearest = table[0:1]
    for distance, value in zip(one_way, outs[sub_count:]):
        nearest = jnp.maximum(nearest, shifted(value, "clus", ring, -distance))
    for shift in range(1, mem_count):
        part = shifted(table[shift : shift + 1], "mem", mem_order, -shift)
        nearest = jnp.maximum(nearest, part)
    return nearest.reshape(row_count)


def solution(mesh):
    placed = (
        P(("parts", "clus", "mem", "sub"), None),
        P(("parts", "clus", "mem", "sub")),
        P(("parts", "clus", "mem", "sub")),
    )
    return jax.shard_map(
        body,
        mesh=mesh,
        in_specs=placed,
        out_specs=P(("parts", "clus", "mem", "sub")),
        check_vma=False,
    )
```

```python
import jax
import jax.numpy as jnp
from jax import lax
from jax.experimental import pallas as pl
from jax.experimental.pallas import tpu as pltpu
from jax.sharding import PartitionSpec as P

LANES = 128
META_ROWS = 16
DIGIT = 256
VMEM_LIMIT = 24 * 1024 * 1024
PACK_VMEM_LIMIT = 60 * 1024 * 1024
NT = (((1,), (1,)), ((), ()))
NONE = -1.0


def pack_kernel(label_ref, rank_ref, emb_ref, message_ref, whole_ref, meta_ref, sems):
    rows, features = emb_ref.shape
    chunks = features // LANES
    wholes = [
        pltpu.make_async_copy(ref, whole_ref.at[index], sems.at[chunks + index])
        for index, ref in enumerate((label_ref, rank_ref))
    ]
    copies = [
        pltpu.make_async_copy(
            emb_ref.at[:, pl.ds(chunk * LANES, LANES)],
            message_ref.at[pl.ds(chunk * rows, rows), :],
            sems.at[chunk],
        )
        for chunk in range(chunks)
    ]
    for copy in wholes + copies:
        copy.start()
    for copy in wholes:
        copy.wait()
    kind = lax.broadcasted_iota(jnp.int32, (META_ROWS, rows), 0)
    rank = whole_ref[1]
    meta = jnp.where(kind == 0, whole_ref[0], 0)
    meta = jnp.where(kind == 1, rank // DIGIT, meta)
    meta = jnp.where(kind == 2, rank % DIGIT, meta)
    meta_ref[...] = meta.astype(jnp.float32).astype(jnp.bfloat16)
    copies.append(
        pltpu.make_async_copy(
            meta_ref, message_ref.at[pl.ds(chunks * rows, META_ROWS), :], sems.at[chunks + 2]
        )
    )
    copies[-1].start()
    for copy in copies:
        copy.wait()


def rows_of(message):
    rows = message.shape[1]
    chunks = message.shape[0] // rows
    return jnp.concatenate([message[c * rows : (c + 1) * rows, :] for c in range(chunks)], axis=1)


def meta_of(message):
    meta = message[message.shape[0] - META_ROWS :, :].astype(jnp.float32)
    return meta[0:1], meta[1:2] * DIGIT + meta[2:3]


def best_kernel(line_count, back_count, mem_count, sub_count, *refs):
    plane_count = mem_count * sub_count
    plane = refs[:plane_count]
    lines = refs[plane_count : plane_count + line_count][::-1]
    outs = refs[line_count + plane_count :]
    plane_outs, back_outs = outs[:mem_count], outs[mem_count:]
    rows = lines[0].shape[1]

    line_rows = jnp.concatenate([rows_of(line) for line in lines], axis=0)
    columns = []
    for line in lines:
        label, rank = meta_of(line)
        columns.append(jnp.transpose(jnp.concatenate([label, rank] + [rank] * 6, axis=0)))
    columns = jnp.concatenate(columns, axis=0)
    line_label, line_rank = columns[:, 0:1], columns[:, 1:2]

    back = [None] * back_count
    for shift in range(mem_count):
        blocks = plane[shift * sub_count : (shift + 1) * sub_count]
        plane_rows = jnp.concatenate([rows_of(block) for block in blocks], axis=0)
        metas = [meta_of(block) for block in blocks]
        label = jnp.concatenate([meta[0] for meta in metas], axis=1)
        rank = jnp.concatenate([meta[1] for meta in metas], axis=1)
        scores = lax.dot_general(line_rows, plane_rows, NT, preferred_element_type=jnp.float32)
        scores = jnp.where(line_label == label, scores, NONE)
        forward = jnp.where(line_rank < rank, scores, NONE)
        best = jnp.max(forward, axis=0, keepdims=True)
        for turn in range(sub_count):
            plane_outs[shift][turn : turn + 1, :] = best[:, turn * rows : (turn + 1) * rows]
        for index in range(back_count):
            piece = slice((index + 1) * rows, (index + 2) * rows)
            backward = jnp.where(line_rank[piece] > rank, scores[piece], NONE)
            for turn in range(sub_count):
                part = backward[:, turn * rows : (turn + 1) * rows]
                back[index] = part if back[index] is None else jnp.maximum(back[index], part)
    for index in range(back_count):
        back_outs[index][...] = jnp.max(jnp.transpose(back[index]), axis=0, keepdims=True)


def body(embeddings, labels, member_rank):
    row_count, feature_count = embeddings.shape
    clus_count = lax.axis_size("clus")
    mem_count = lax.axis_size("mem")
    sub_count = lax.axis_size("sub")
    chunk_count = feature_count // LANES
    vmem = pl.BlockSpec(memory_space=pltpu.VMEM)
    hbm = pl.BlockSpec(memory_space=pltpu.HBM)
    params = pltpu.CompilerParams(vmem_limit_bytes=VMEM_LIMIT)

    def shifted(value, axis, order, distance):
        count = len(order)
        pairs = [(order[i], order[(i + distance) % count]) for i in range(count)]
        return lax.ppermute(value, axis, pairs)

    half = (clus_count + 1) // 2
    ring = [z for pair in zip(range(half), range(half, 2 * half)) for z in pair if z < clus_count]
    mem_order = list(range(mem_count))
    sub_order = list(range(sub_count))

    message = pl.pallas_call(
        pack_kernel,
        out_shape=jax.ShapeDtypeStruct((chunk_count * row_count + META_ROWS, LANES), jnp.bfloat16),
        in_specs=[hbm] * 3,
        out_specs=hbm,
        scratch_shapes=[
            pltpu.VMEM((2, 1, row_count), jnp.int32),
            pltpu.VMEM((META_ROWS, LANES), jnp.bfloat16),
            pltpu.SemaphoreType.DMA((chunk_count + 3,)),
        ],
        compiler_params=pltpu.CompilerParams(vmem_limit_bytes=PACK_VMEM_LIMIT),
        name="pack",
    )(labels.reshape(1, row_count), member_rank.reshape(1, row_count), embeddings)

    distances = list(range(1, clus_count // 2 + 1))
    one_way = [d for d in distances if 2 * d != clus_count]
    lines = [message] + [shifted(message, "clus", ring, d) for d in distances]
    plane = []
    for shift in range(mem_count):
        block = shifted(message, "mem", mem_order, shift) if shift else message
        plane.append(block)
        plane.extend(shifted(block, "sub", sub_order, turn) for turn in range(1, sub_count))

    outs = pl.pallas_call(
        lambda *refs: best_kernel(len(lines), len(one_way), mem_count, sub_count, *refs),
        out_shape=[jax.ShapeDtypeStruct((sub_count, row_count), jnp.float32)] * mem_count
        + [jax.ShapeDtypeStruct((1, row_count), jnp.float32)] * len(one_way),
        in_specs=[vmem] * (len(lines) + len(plane)),
        out_specs=[vmem] * (mem_count + len(one_way)),
        compiler_params=params,
        name="best",
    )(*plane, *lines[::-1])
    table = outs[0]
    for shift in range(1, mem_count):
        table = jnp.maximum(table, shifted(outs[shift], "mem", mem_order, -shift))
    nearest = table[0:1]
    for turn in range(1, sub_count):
        part = shifted(table[turn : turn + 1], "sub", sub_order, -turn)
        nearest = jnp.maximum(nearest, part)
    for distance, value in zip(one_way, outs[mem_count:]):
        nearest = jnp.maximum(nearest, shifted(value, "clus", ring, -distance))
    return nearest.reshape(row_count)


def solution(mesh):
    placed = (
        P(("parts", "clus", "mem", "sub"), None),
        P(("parts", "clus", "mem", "sub")),
        P(("parts", "clus", "mem", "sub")),
    )
    return jax.shard_map(
        body,
        mesh=mesh,
        in_specs=placed,
        out_specs=P(("parts", "clus", "mem", "sub")),
        check_vma=False,
    )
```

```python
import jax
import jax.numpy as jnp
from jax import lax
from jax.experimental import pallas as pl
from jax.experimental.pallas import tpu as pltpu
from jax.sharding import PartitionSpec as P

LANES = 128
META_ROWS = 16
DIGIT = 256
VMEM_LIMIT = 24 * 1024 * 1024
NT = (((1,), (1,)), ((), ()))
NONE = -1.0


def pack_kernel(label_ref, rank_ref, emb_ref, message_ref, sems):
    rows, features = emb_ref.shape
    chunks = features // LANES
    copies = [
        pltpu.make_async_copy(
            emb_ref.at[:, pl.ds(chunk * LANES, LANES)],
            message_ref.at[pl.ds(chunk * rows, rows), :],
            sems.at[chunk],
        )
        for chunk in range(chunks)
    ]
    for copy in copies:
        copy.start()
    kind = lax.broadcasted_iota(jnp.int32, (META_ROWS, rows), 0)
    rank = rank_ref[...]
    meta = jnp.where(kind == 0, label_ref[...], 0)
    meta = jnp.where(kind == 1, rank // DIGIT, meta)
    meta = jnp.where(kind == 2, rank % DIGIT, meta)
    message_ref[pl.ds(chunks * rows, META_ROWS), :] = meta.astype(jnp.float32).astype(jnp.bfloat16)
    for copy in copies:
        copy.wait()


def rows_of(message):
    rows = message.shape[1]
    chunks = message.shape[0] // rows
    return jnp.concatenate([message[c * rows : (c + 1) * rows, :] for c in range(chunks)], axis=1)


def meta_of(message):
    meta = message[message.shape[0] - META_ROWS :, :].astype(jnp.float32)
    return meta[0:1], meta[1:2] * DIGIT + meta[2:3]


def best_kernel(line_count, back_count, mem_count, sub_count, *refs):
    plane_count = mem_count * sub_count
    plane = refs[:plane_count]
    lines = refs[plane_count : plane_count + line_count][::-1]
    outs = refs[line_count + plane_count :]
    plane_outs, back_outs = outs[:mem_count], outs[mem_count:]
    rows = lines[0].shape[1]

    line_rows = jnp.concatenate([rows_of(line) for line in lines], axis=0)
    columns = []
    for line in lines:
        label, rank = meta_of(line)
        columns.append(jnp.transpose(jnp.concatenate([label, rank] + [rank] * 6, axis=0)))
    columns = jnp.concatenate(columns, axis=0)
    line_label, line_rank = columns[:, 0:1], columns[:, 1:2]

    back = [None] * back_count
    for shift in range(mem_count):
        blocks = plane[shift * sub_count : (shift + 1) * sub_count]
        plane_rows = jnp.concatenate([rows_of(block) for block in blocks], axis=0)
        metas = [meta_of(block) for block in blocks]
        label = jnp.concatenate([meta[0] for meta in metas], axis=1)
        rank = jnp.concatenate([meta[1] for meta in metas], axis=1)
        scores = lax.dot_general(line_rows, plane_rows, NT, preferred_element_type=jnp.float32)
        scores = jnp.where(line_label == label, scores, NONE)
        forward = jnp.where(line_rank < rank, scores, NONE)
        best = jnp.max(forward, axis=0, keepdims=True)
        for turn in range(sub_count):
            plane_outs[shift][turn : turn + 1, :] = best[:, turn * rows : (turn + 1) * rows]
        for index in range(back_count):
            piece = slice((index + 1) * rows, (index + 2) * rows)
            backward = jnp.where(line_rank[piece] > rank, scores[piece], NONE)
            for turn in range(sub_count):
                part = backward[:, turn * rows : (turn + 1) * rows]
                back[index] = part if back[index] is None else jnp.maximum(back[index], part)
    for index in range(back_count):
        back_outs[index][...] = jnp.max(jnp.transpose(back[index]), axis=0, keepdims=True)


def body(embeddings, labels, member_rank):
    row_count, feature_count = embeddings.shape
    clus_count = lax.axis_size("clus")
    mem_count = lax.axis_size("mem")
    sub_count = lax.axis_size("sub")
    chunk_count = feature_count // LANES
    vmem = pl.BlockSpec(memory_space=pltpu.VMEM)
    params = pltpu.CompilerParams(vmem_limit_bytes=VMEM_LIMIT)

    def shifted(value, axis, order, distance):
        count = len(order)
        pairs = [(order[i], order[(i + distance) % count]) for i in range(count)]
        return lax.ppermute(value, axis, pairs)

    half = (clus_count + 1) // 2
    ring = [z for pair in zip(range(half), range(half, 2 * half)) for z in pair if z < clus_count]
    mem_order = list(range(mem_count))
    sub_order = list(range(sub_count))

    message = pl.pallas_call(
        pack_kernel,
        out_shape=jax.ShapeDtypeStruct((chunk_count * row_count + META_ROWS, LANES), jnp.bfloat16),
        in_specs=[vmem, vmem, pl.BlockSpec(memory_space=pl.ANY)],
        out_specs=vmem,
        scratch_shapes=[pltpu.SemaphoreType.DMA((chunk_count,))],
        compiler_params=params,
        name="pack",
    )(labels.reshape(1, row_count), member_rank.reshape(1, row_count), embeddings)

    distances = list(range(1, clus_count // 2 + 1))
    one_way = [d for d in distances if 2 * d != clus_count]
    lines = [message] + [shifted(message, "clus", ring, d) for d in distances]
    plane = []
    for shift in range(mem_count):
        block = shifted(message, "mem", mem_order, shift) if shift else message
        plane.append(block)
        plane.extend(shifted(block, "sub", sub_order, turn) for turn in range(1, sub_count))

    outs = pl.pallas_call(
        lambda *refs: best_kernel(len(lines), len(one_way), mem_count, sub_count, *refs),
        out_shape=[jax.ShapeDtypeStruct((sub_count, row_count), jnp.float32)] * mem_count
        + [jax.ShapeDtypeStruct((1, row_count), jnp.float32)] * len(one_way),
        in_specs=[vmem] * (len(lines) + len(plane)),
        out_specs=[vmem] * (mem_count + len(one_way)),
        compiler_params=params,
        name="best",
    )(*plane, *lines[::-1])
    table = outs[0]
    for shift in range(1, mem_count):
        table = jnp.maximum(table, shifted(outs[shift], "mem", mem_order, -shift))
    nearest = table[0:1]
    for turn in range(1, sub_count):
        part = shifted(table[turn : turn + 1], "sub", sub_order, -turn)
        nearest = jnp.maximum(nearest, part)
    for distance, value in zip(one_way, outs[mem_count:]):
        nearest = jnp.maximum(nearest, shifted(value, "clus", ring, -distance))
    return nearest.reshape(row_count)


def solution(mesh):
    placed = (
        P(("parts", "clus", "mem", "sub"), None),
        P(("parts", "clus", "mem", "sub")),
        P(("parts", "clus", "mem", "sub")),
    )
    return jax.shard_map(
        body,
        mesh=mesh,
        in_specs=placed,
        out_specs=P(("parts", "clus", "mem", "sub")),
        check_vma=False,
    )
```

```python
import jax
import jax.numpy as jnp
from jax import lax
from jax.experimental import pallas as pl
from jax.experimental.pallas import tpu as pltpu
from jax.sharding import PartitionSpec as P

LANES = 128
META_ROWS = 16
DIGIT = 256
VMEM_LIMIT = 24 * 1024 * 1024
NT = (((1,), (1,)), ((), ()))
NONE = -1.0


def pack_kernel(label_ref, rank_ref, emb_ref, message_ref, sems):
    rows, features = emb_ref.shape
    chunks = features // LANES
    copies = [
        pltpu.make_async_copy(
            emb_ref.at[:, pl.ds(chunk * LANES, LANES)],
            message_ref.at[pl.ds(chunk * rows, rows), :],
            sems.at[chunk],
        )
        for chunk in range(chunks)
    ]
    for copy in copies:
        copy.start()
    kind = lax.broadcasted_iota(jnp.int32, (META_ROWS, rows), 0)
    rank = rank_ref[...]
    meta = jnp.where(kind == 0, label_ref[...], 0)
    meta = jnp.where(kind == 1, rank // DIGIT, meta)
    meta = jnp.where(kind == 2, rank % DIGIT, meta)
    message_ref[pl.ds(chunks * rows, META_ROWS), :] = meta.astype(jnp.float32).astype(jnp.bfloat16)
    for copy in copies:
        copy.wait()


def rows_of(message):
    rows = message.shape[1]
    chunks = message.shape[0] // rows
    return jnp.concatenate([message[c * rows : (c + 1) * rows, :] for c in range(chunks)], axis=1)


def meta_of(message):
    meta = message[message.shape[0] - META_ROWS :, :].astype(jnp.float32)
    return meta[0:1], meta[1:2] * DIGIT + meta[2:3]


def best_kernel(line_count, back_count, mem_count, sub_count, *refs):
    plane_count = mem_count * sub_count
    plane = refs[:plane_count]
    lines = refs[plane_count : plane_count + line_count][::-1]
    outs = refs[line_count + plane_count :]
    plane_outs, back_outs = outs[:mem_count], outs[mem_count:]
    rows = lines[0].shape[1]

    line_rows = jnp.concatenate([rows_of(line) for line in lines], axis=0)
    columns = []
    for line in lines:
        label, rank = meta_of(line)
        columns.append(jnp.transpose(jnp.concatenate([label, rank] + [rank] * 6, axis=0)))
    columns = jnp.concatenate(columns, axis=0)
    line_label, line_rank = columns[:, 0:1], columns[:, 1:2]

    back = [None] * back_count
    for shift in range(mem_count):
        blocks = plane[shift * sub_count : (shift + 1) * sub_count]
        plane_rows = jnp.concatenate([rows_of(block) for block in blocks], axis=0)
        metas = [meta_of(block) for block in blocks]
        label = jnp.concatenate([meta[0] for meta in metas], axis=1)
        rank = jnp.concatenate([meta[1] for meta in metas], axis=1)
        scores = lax.dot_general(line_rows, plane_rows, NT, preferred_element_type=jnp.float32)
        scores = jnp.where(line_label == label, scores, NONE)
        forward = jnp.where(line_rank < rank, scores, NONE)
        best = jnp.max(forward, axis=0, keepdims=True)
        for turn in range(sub_count):
            plane_outs[shift][turn : turn + 1, :] = best[:, turn * rows : (turn + 1) * rows]
        for index in range(back_count):
            piece = slice((index + 1) * rows, (index + 2) * rows)
            backward = jnp.where(line_rank[piece] > rank, scores[piece], NONE)
            for turn in range(sub_count):
                part = backward[:, turn * rows : (turn + 1) * rows]
                back[index] = part if back[index] is None else jnp.maximum(back[index], part)
    for index in range(back_count):
        back_outs[index][...] = jnp.max(jnp.transpose(back[index]), axis=0, keepdims=True)


def body(embeddings, labels, member_rank):
    row_count, feature_count = embeddings.shape
    clus_count = lax.axis_size("clus")
    mem_count = lax.axis_size("mem")
    sub_count = lax.axis_size("sub")
    chunk_count = feature_count // LANES
    vmem = pl.BlockSpec(memory_space=pltpu.VMEM)
    params = pltpu.CompilerParams(vmem_limit_bytes=VMEM_LIMIT)

    def shifted(value, axis, order, distance):
        count = len(order)
        pairs = [(order[i], order[(i + distance) % count]) for i in range(count)]
        return lax.ppermute(value, axis, pairs)

    ring = list(range(clus_count))
    mem_order = list(range(mem_count))
    sub_order = list(range(sub_count))

    message = pl.pallas_call(
        pack_kernel,
        out_shape=jax.ShapeDtypeStruct((chunk_count * row_count + META_ROWS, LANES), jnp.bfloat16),
        in_specs=[vmem, vmem, pl.BlockSpec(memory_space=pl.ANY)],
        out_specs=vmem,
        scratch_shapes=[pltpu.SemaphoreType.DMA((chunk_count,))],
        compiler_params=params,
        name="pack",
    )(labels.reshape(1, row_count), member_rank.reshape(1, row_count), embeddings)

    distances = list(range(1, clus_count // 2 + 1))
    one_way = [d for d in distances if 2 * d != clus_count]
    lines = [message] + [shifted(message, "clus", ring, d) for d in distances]
    plane = []
    for shift in range(mem_count):
        block = shifted(message, "mem", mem_order, shift) if shift else message
        plane.append(block)
        plane.extend(shifted(block, "sub", sub_order, turn) for turn in range(1, sub_count))

    outs = pl.pallas_call(
        lambda *refs: best_kernel(len(lines), len(one_way), mem_count, sub_count, *refs),
        out_shape=[jax.ShapeDtypeStruct((sub_count, row_count), jnp.float32)] * mem_count
        + [jax.ShapeDtypeStruct((1, row_count), jnp.float32)] * len(one_way),
        in_specs=[vmem] * (len(lines) + len(plane)),
        out_specs=[vmem] * (mem_count + len(one_way)),
        compiler_params=params,
        name="best",
    )(*plane, *lines[::-1])
    table = outs[0]
    for shift in range(1, mem_count):
        table = jnp.maximum(table, shifted(outs[shift], "mem", mem_order, -shift))
    nearest = table[0:1]
    for turn in range(1, sub_count):
        part = shifted(table[turn : turn + 1], "sub", sub_order, -turn)
        nearest = jnp.maximum(nearest, part)
    for distance, value in zip(one_way, outs[mem_count:]):
        nearest = jnp.maximum(nearest, shifted(value, "clus", ring, -distance))
    return nearest.reshape(row_count)


def solution(mesh):
    placed = (
        P(("parts", "clus", "mem", "sub"), None),
        P(("parts", "clus", "mem", "sub")),
        P(("parts", "clus", "mem", "sub")),
    )
    return jax.shard_map(
        body,
        mesh=mesh,
        in_specs=placed,
        out_specs=P(("parts", "clus", "mem", "sub")),
        check_vma=False,
    )
```

```python
import jax
import jax.numpy as jnp
from jax import lax
from jax.experimental import pallas as pl
from jax.experimental.pallas import tpu as pltpu
from jax.sharding import PartitionSpec as P

LANES = 128
META_ROWS = 16
DIGIT = 256
VMEM_LIMIT = 24 * 1024 * 1024
NT = (((1,), (1,)), ((), ()))
NONE = -1.0


def pack_kernel(label_ref, rank_ref, chunks_ref, message_ref, sem):
    chunk_rows, rows = chunks_ref.shape[0], label_ref.shape[1]
    copy = pltpu.make_async_copy(chunks_ref, message_ref.at[pl.ds(0, chunk_rows), :], sem)
    copy.start()
    kind = lax.broadcasted_iota(jnp.int32, (META_ROWS, rows), 0)
    rank = rank_ref[...]
    meta = jnp.where(kind == 0, label_ref[...], 0)
    meta = jnp.where(kind == 1, rank // DIGIT, meta)
    meta = jnp.where(kind == 2, rank % DIGIT, meta)
    message_ref[pl.ds(chunk_rows, META_ROWS), :] = meta.astype(jnp.float32).astype(jnp.bfloat16)
    copy.wait()


def rows_of(message):
    rows = message.shape[1]
    chunks = message.shape[0] // rows
    return jnp.concatenate([message[c * rows : (c + 1) * rows, :] for c in range(chunks)], axis=1)


def meta_of(message):
    meta = message[message.shape[0] - META_ROWS :, :].astype(jnp.float32)
    return meta[0:1], meta[1:2] * DIGIT + meta[2:3]


def best_kernel(line_count, back_count, mem_count, sub_count, *refs):
    plane_count = mem_count * sub_count
    plane = refs[:plane_count]
    lines = refs[plane_count : plane_count + line_count][::-1]
    outs = refs[line_count + plane_count :]
    plane_outs, back_outs = outs[:mem_count], outs[mem_count:]
    rows = lines[0].shape[1]

    line_rows = jnp.concatenate([rows_of(line) for line in lines], axis=0)
    columns = []
    for line in lines:
        label, rank = meta_of(line)
        columns.append(jnp.transpose(jnp.concatenate([label, rank] + [rank] * 6, axis=0)))
    columns = jnp.concatenate(columns, axis=0)
    line_label, line_rank = columns[:, 0:1], columns[:, 1:2]

    back = [None] * back_count
    for shift in range(mem_count):
        blocks = plane[shift * sub_count : (shift + 1) * sub_count]
        plane_rows = jnp.concatenate([rows_of(block) for block in blocks], axis=0)
        metas = [meta_of(block) for block in blocks]
        label = jnp.concatenate([meta[0] for meta in metas], axis=1)
        rank = jnp.concatenate([meta[1] for meta in metas], axis=1)
        scores = lax.dot_general(line_rows, plane_rows, NT, preferred_element_type=jnp.float32)
        scores = jnp.where(line_label == label, scores, NONE)
        forward = jnp.where(line_rank < rank, scores, NONE)
        best = jnp.max(forward, axis=0, keepdims=True)
        for turn in range(sub_count):
            plane_outs[shift][turn : turn + 1, :] = best[:, turn * rows : (turn + 1) * rows]
        for index in range(back_count):
            piece = slice((index + 1) * rows, (index + 2) * rows)
            backward = jnp.where(line_rank[piece] > rank, scores[piece], NONE)
            for turn in range(sub_count):
                part = backward[:, turn * rows : (turn + 1) * rows]
                back[index] = part if back[index] is None else jnp.maximum(back[index], part)
    for index in range(back_count):
        back_outs[index][...] = jnp.max(jnp.transpose(back[index]), axis=0, keepdims=True)


def body(embeddings, labels, member_rank):
    row_count, feature_count = embeddings.shape
    clus_count = lax.axis_size("clus")
    mem_count = lax.axis_size("mem")
    sub_count = lax.axis_size("sub")
    chunk_count = feature_count // LANES
    vmem = pl.BlockSpec(memory_space=pltpu.VMEM)
    params = pltpu.CompilerParams(vmem_limit_bytes=VMEM_LIMIT)

    def shifted(value, axis, order, distance):
        count = len(order)
        pairs = [(order[i], order[(i + distance) % count]) for i in range(count)]
        return lax.ppermute(value, axis, pairs)

    half = (clus_count + 1) // 2
    ring = [z for pair in zip(range(half), range(half, 2 * half)) for z in pair if z < clus_count]
    mem_order = list(range(mem_count))
    sub_order = list(range(sub_count))

    chunks = embeddings.reshape(row_count, chunk_count, LANES).transpose(1, 0, 2)
    message = pl.pallas_call(
        pack_kernel,
        out_shape=jax.ShapeDtypeStruct((chunk_count * row_count + META_ROWS, LANES), jnp.bfloat16),
        in_specs=[vmem, vmem, pl.BlockSpec(memory_space=pl.ANY)],
        out_specs=vmem,
        scratch_shapes=[pltpu.SemaphoreType.DMA(())],
        compiler_params=params,
        name="pack",
    )(
        labels.reshape(1, row_count),
        member_rank.reshape(1, row_count),
        chunks.reshape(chunk_count * row_count, LANES),
    )

    distances = list(range(1, clus_count // 2 + 1))
    one_way = [d for d in distances if 2 * d != clus_count]
    lines = [message] + [shifted(message, "clus", ring, d) for d in distances]
    plane = []
    for shift in range(mem_count):
        block = shifted(message, "mem", mem_order, shift) if shift else message
        plane.append(block)
        plane.extend(shifted(block, "sub", sub_order, turn) for turn in range(1, sub_count))

    outs = pl.pallas_call(
        lambda *refs: best_kernel(len(lines), len(one_way), mem_count, sub_count, *refs),
        out_shape=[jax.ShapeDtypeStruct((sub_count, row_count), jnp.float32)] * mem_count
        + [jax.ShapeDtypeStruct((1, row_count), jnp.float32)] * len(one_way),
        in_specs=[vmem] * (len(lines) + len(plane)),
        out_specs=[vmem] * (mem_count + len(one_way)),
        compiler_params=params,
        name="best",
    )(*plane, *lines[::-1])
    table = outs[0]
    for shift in range(1, mem_count):
        table = jnp.maximum(table, shifted(outs[shift], "mem", mem_order, -shift))
    nearest = table[0:1]
    for turn in range(1, sub_count):
        part = shifted(table[turn : turn + 1], "sub", sub_order, -turn)
        nearest = jnp.maximum(nearest, part)
    for distance, value in zip(one_way, outs[mem_count:]):
        nearest = jnp.maximum(nearest, shifted(value, "clus", ring, -distance))
    return nearest.reshape(row_count)


def solution(mesh):
    placed = (
        P(("parts", "clus", "mem", "sub"), None),
        P(("parts", "clus", "mem", "sub")),
        P(("parts", "clus", "mem", "sub")),
    )
    return jax.shard_map(
        body,
        mesh=mesh,
        in_specs=placed,
        out_specs=P(("parts", "clus", "mem", "sub")),
        check_vma=False,
    )
```

```python
import jax
import jax.numpy as jnp
from jax import lax
from jax.experimental import pallas as pl
from jax.experimental.pallas import tpu as pltpu
from jax.sharding import PartitionSpec as P

LANES = 128
META_ROWS = 16
DIGIT = 256
VMEM_LIMIT = 24 * 1024 * 1024
NT = (((1,), (1,)), ((), ()))
NONE = -1.0


def meta_kernel(label_ref, rank_ref, meta_ref):
    kind = lax.broadcasted_iota(jnp.int32, meta_ref.shape, 0)
    rank = rank_ref[...]
    meta = jnp.where(kind == 0, label_ref[...], 0)
    meta = jnp.where(kind == 1, rank // DIGIT, meta)
    meta = jnp.where(kind == 2, rank % DIGIT, meta)
    meta_ref[...] = meta.astype(jnp.float32).astype(jnp.bfloat16)


def pack_kernel(meta_ref, chunks_ref, message_ref, sem):
    chunk_rows = chunks_ref.shape[0]
    copy = pltpu.make_async_copy(chunks_ref, message_ref.at[pl.ds(0, chunk_rows), :], sem)
    copy.start()
    message_ref[pl.ds(chunk_rows, META_ROWS), :] = meta_ref[...]
    copy.wait()


def rows_of(message):
    rows = message.shape[1]
    chunks = message.shape[0] // rows
    return jnp.concatenate([message[c * rows : (c + 1) * rows, :] for c in range(chunks)], axis=1)


def meta_of(message):
    meta = message[message.shape[0] - META_ROWS :, :].astype(jnp.float32)
    return meta[0:1], meta[1:2] * DIGIT + meta[2:3]


def best_kernel(line_count, back_count, mem_count, sub_count, *refs):
    plane_count = mem_count * sub_count
    plane = refs[:plane_count]
    lines = refs[plane_count : plane_count + line_count][::-1]
    outs = refs[line_count + plane_count :]
    plane_outs, back_outs = outs[:mem_count], outs[mem_count:]
    rows = lines[0].shape[1]

    line_rows = jnp.concatenate([rows_of(line) for line in lines], axis=0)
    columns = []
    for line in lines:
        label, rank = meta_of(line)
        columns.append(jnp.transpose(jnp.concatenate([label, rank] + [rank] * 6, axis=0)))
    columns = jnp.concatenate(columns, axis=0)
    line_label, line_rank = columns[:, 0:1], columns[:, 1:2]

    back = [None] * back_count
    for shift in range(mem_count):
        blocks = plane[shift * sub_count : (shift + 1) * sub_count]
        plane_rows = jnp.concatenate([rows_of(block) for block in blocks], axis=0)
        metas = [meta_of(block) for block in blocks]
        label = jnp.concatenate([meta[0] for meta in metas], axis=1)
        rank = jnp.concatenate([meta[1] for meta in metas], axis=1)
        scores = lax.dot_general(line_rows, plane_rows, NT, preferred_element_type=jnp.float32)
        scores = jnp.where(line_label == label, scores, NONE)
        forward = jnp.where(line_rank < rank, scores, NONE)
        best = jnp.max(forward, axis=0, keepdims=True)
        for turn in range(sub_count):
            plane_outs[shift][turn : turn + 1, :] = best[:, turn * rows : (turn + 1) * rows]
        for index in range(back_count):
            piece = slice((index + 1) * rows, (index + 2) * rows)
            backward = jnp.where(line_rank[piece] > rank, scores[piece], NONE)
            for turn in range(sub_count):
                part = backward[:, turn * rows : (turn + 1) * rows]
                back[index] = part if back[index] is None else jnp.maximum(back[index], part)
    for index in range(back_count):
        back_outs[index][...] = jnp.max(jnp.transpose(back[index]), axis=0, keepdims=True)


def body(embeddings, labels, member_rank):
    row_count, feature_count = embeddings.shape
    clus_count = lax.axis_size("clus")
    mem_count = lax.axis_size("mem")
    sub_count = lax.axis_size("sub")
    chunk_count = feature_count // LANES
    vmem = pl.BlockSpec(memory_space=pltpu.VMEM)
    params = pltpu.CompilerParams(vmem_limit_bytes=VMEM_LIMIT)

    def shifted(value, axis, order, distance):
        count = len(order)
        pairs = [(order[i], order[(i + distance) % count]) for i in range(count)]
        return lax.ppermute(value, axis, pairs)

    half = (clus_count + 1) // 2
    ring = [z for pair in zip(range(half), range(half, 2 * half)) for z in pair if z < clus_count]
    mem_order = list(range(mem_count))
    sub_order = list(range(sub_count))

    meta = pl.pallas_call(
        meta_kernel,
        out_shape=jax.ShapeDtypeStruct((META_ROWS, row_count), jnp.bfloat16),
        in_specs=[vmem, vmem],
        out_specs=vmem,
        compiler_params=params,
        name="meta",
    )(labels.reshape(1, row_count), member_rank.reshape(1, row_count))
    meta, rows = lax.optimization_barrier((meta, embeddings))
    chunks = rows.reshape(row_count, chunk_count, LANES).transpose(1, 0, 2)
    message = pl.pallas_call(
        pack_kernel,
        out_shape=jax.ShapeDtypeStruct((chunk_count * row_count + META_ROWS, LANES), jnp.bfloat16),
        in_specs=[vmem, pl.BlockSpec(memory_space=pl.ANY)],
        out_specs=vmem,
        scratch_shapes=[pltpu.SemaphoreType.DMA(())],
        compiler_params=params,
        name="pack",
    )(meta, chunks.reshape(chunk_count * row_count, LANES))

    distances = list(range(1, clus_count // 2 + 1))
    one_way = [d for d in distances if 2 * d != clus_count]
    lines = [message] + [shifted(message, "clus", ring, d) for d in distances]
    neighbours = [shifted(message, "mem", mem_order, shift) for shift in range(1, mem_count)]
    neighbours, arrived = lax.optimization_barrier((neighbours, lines[1 : 1 + len(one_way)]))
    lines[1 : 1 + len(one_way)] = arrived
    plane = []
    for block in [message] + neighbours:
        plane.append(block)
        plane.extend(shifted(block, "sub", sub_order, turn) for turn in range(1, sub_count))

    outs = pl.pallas_call(
        lambda *refs: best_kernel(len(lines), len(one_way), mem_count, sub_count, *refs),
        out_shape=[jax.ShapeDtypeStruct((sub_count, row_count), jnp.float32)] * mem_count
        + [jax.ShapeDtypeStruct((1, row_count), jnp.float32)] * len(one_way),
        in_specs=[vmem] * (len(lines) + len(plane)),
        out_specs=[vmem] * (mem_count + len(one_way)),
        compiler_params=params,
        name="best",
    )(*plane, *lines[::-1])
    table = outs[0]
    for shift in range(1, mem_count):
        table = jnp.maximum(table, shifted(outs[shift], "mem", mem_order, -shift))
    nearest = table[0:1]
    for turn in range(1, sub_count):
        part = shifted(table[turn : turn + 1], "sub", sub_order, -turn)
        nearest = jnp.maximum(nearest, part)
    for distance, value in zip(one_way, outs[mem_count:]):
        nearest = jnp.maximum(nearest, shifted(value, "clus", ring, -distance))
    return nearest.reshape(row_count)


def solution(mesh):
    placed = (
        P(("parts", "clus", "mem", "sub"), None),
        P(("parts", "clus", "mem", "sub")),
        P(("parts", "clus", "mem", "sub")),
    )
    return jax.shard_map(
        body,
        mesh=mesh,
        in_specs=placed,
        out_specs=P(("parts", "clus", "mem", "sub")),
        check_vma=False,
    )
```

```python
import jax
import jax.numpy as jnp
from jax import lax
from jax.experimental import pallas as pl
from jax.experimental.pallas import tpu as pltpu
from jax.sharding import PartitionSpec as P

LANES = 128
META_ROWS = 16
DIGIT = 256
VMEM_LIMIT = 24 * 1024 * 1024
NT = (((1,), (1,)), ((), ()))
NONE = -1.0


def meta_kernel(label_ref, rank_ref, meta_ref):
    kind = lax.broadcasted_iota(jnp.int32, meta_ref.shape, 0)
    rank = rank_ref[...]
    meta = jnp.where(kind == 0, label_ref[...], 0)
    meta = jnp.where(kind == 1, rank // DIGIT, meta)
    meta = jnp.where(kind == 2, rank % DIGIT, meta)
    meta_ref[...] = meta.astype(jnp.float32).astype(jnp.bfloat16)


def pack_kernel(meta_ref, chunks_ref, message_ref, sem):
    chunk_rows = chunks_ref.shape[0]
    copy = pltpu.make_async_copy(chunks_ref, message_ref.at[pl.ds(0, chunk_rows), :], sem)
    copy.start()
    message_ref[pl.ds(chunk_rows, META_ROWS), :] = meta_ref[...]
    copy.wait()


def rows_of(message):
    rows = message.shape[1]
    chunks = message.shape[0] // rows
    return jnp.concatenate([message[c * rows : (c + 1) * rows, :] for c in range(chunks)], axis=1)


def meta_of(message):
    meta = message[message.shape[0] - META_ROWS :, :].astype(jnp.float32)
    return meta[0:1], meta[1:2] * DIGIT + meta[2:3]


def best_kernel(line_count, back_count, mem_count, sub_count, *refs):
    plane_count = mem_count * sub_count
    plane = refs[:plane_count]
    lines = refs[plane_count : plane_count + line_count][::-1]
    outs = refs[line_count + plane_count :]
    plane_outs, back_outs = outs[:mem_count], outs[mem_count:]
    rows = lines[0].shape[1]

    line_rows = jnp.concatenate([rows_of(line) for line in lines], axis=0)
    columns = []
    for line in lines:
        label, rank = meta_of(line)
        columns.append(jnp.transpose(jnp.concatenate([label, rank] + [rank] * 6, axis=0)))
    columns = jnp.concatenate(columns, axis=0)
    line_label, line_rank = columns[:, 0:1], columns[:, 1:2]

    back = [None] * back_count
    for shift in range(mem_count):
        blocks = plane[shift * sub_count : (shift + 1) * sub_count]
        plane_rows = jnp.concatenate([rows_of(block) for block in blocks], axis=0)
        metas = [meta_of(block) for block in blocks]
        label = jnp.concatenate([meta[0] for meta in metas], axis=1)
        rank = jnp.concatenate([meta[1] for meta in metas], axis=1)
        scores = lax.dot_general(line_rows, plane_rows, NT, preferred_element_type=jnp.float32)
        scores = jnp.where(line_label == label, scores, NONE)
        forward = jnp.where(line_rank < rank, scores, NONE)
        best = jnp.max(forward, axis=0, keepdims=True)
        for turn in range(sub_count):
            plane_outs[shift][turn : turn + 1, :] = best[:, turn * rows : (turn + 1) * rows]
        for index in range(back_count):
            piece = slice((index + 1) * rows, (index + 2) * rows)
            backward = jnp.where(line_rank[piece] > rank, scores[piece], NONE)
            for turn in range(sub_count):
                part = backward[:, turn * rows : (turn + 1) * rows]
                back[index] = part if back[index] is None else jnp.maximum(back[index], part)
    for index in range(back_count):
        back_outs[index][...] = jnp.max(jnp.transpose(back[index]), axis=0, keepdims=True)


def body(embeddings, labels, member_rank):
    row_count, feature_count = embeddings.shape
    clus_count = lax.axis_size("clus")
    mem_count = lax.axis_size("mem")
    sub_count = lax.axis_size("sub")
    chunk_count = feature_count // LANES
    vmem = pl.BlockSpec(memory_space=pltpu.VMEM)
    params = pltpu.CompilerParams(vmem_limit_bytes=VMEM_LIMIT)

    def shifted(value, axis, order, distance):
        count = len(order)
        pairs = [(order[i], order[(i + distance) % count]) for i in range(count)]
        return lax.ppermute(value, axis, pairs)

    half = (clus_count + 1) // 2
    ring = [z for pair in zip(range(half), range(half, 2 * half)) for z in pair if z < clus_count]
    mem_order = list(range(mem_count))
    sub_order = list(range(sub_count))

    meta = pl.pallas_call(
        meta_kernel,
        out_shape=jax.ShapeDtypeStruct((META_ROWS, row_count), jnp.bfloat16),
        in_specs=[vmem, vmem],
        out_specs=vmem,
        compiler_params=params,
        name="meta",
    )(labels.reshape(1, row_count), member_rank.reshape(1, row_count))
    meta, rows = lax.optimization_barrier((meta, embeddings))
    chunks = rows.reshape(row_count, chunk_count, LANES).transpose(1, 0, 2)
    message = pl.pallas_call(
        pack_kernel,
        out_shape=jax.ShapeDtypeStruct((chunk_count * row_count + META_ROWS, LANES), jnp.bfloat16),
        in_specs=[vmem, pl.BlockSpec(memory_space=pl.ANY)],
        out_specs=vmem,
        scratch_shapes=[pltpu.SemaphoreType.DMA(())],
        compiler_params=params,
        name="pack",
    )(meta, chunks.reshape(chunk_count * row_count, LANES))

    distances = list(range(1, clus_count // 2 + 1))
    one_way = [d for d in distances if 2 * d != clus_count]
    lines = [message] + [shifted(message, "clus", ring, d) for d in distances]
    def from_plane(value, shift, turn):
        places = [(m, c) for m in range(mem_count) for c in range(sub_count)]
        pairs = [
            (m * sub_count + c, (m + shift) % mem_count * sub_count + (c + turn) % sub_count)
            for m, c in places
        ]
        return lax.ppermute(value, ("mem", "sub"), pairs) if shift or turn else value

    plane = [
        from_plane(message, shift, turn)
        for shift in range(mem_count)
        for turn in range(sub_count)
    ]

    outs = pl.pallas_call(
        lambda *refs: best_kernel(len(lines), len(one_way), mem_count, sub_count, *refs),
        out_shape=[jax.ShapeDtypeStruct((sub_count, row_count), jnp.float32)] * mem_count
        + [jax.ShapeDtypeStruct((1, row_count), jnp.float32)] * len(one_way),
        in_specs=[vmem] * (len(lines) + len(plane)),
        out_specs=[vmem] * (mem_count + len(one_way)),
        compiler_params=params,
        name="best",
    )(*plane, *lines[::-1])
    table = outs[0]
    for shift in range(1, mem_count):
        table = jnp.maximum(table, shifted(outs[shift], "mem", mem_order, -shift))
    nearest = table[0:1]
    for turn in range(1, sub_count):
        part = shifted(table[turn : turn + 1], "sub", sub_order, -turn)
        nearest = jnp.maximum(nearest, part)
    for distance, value in zip(one_way, outs[mem_count:]):
        nearest = jnp.maximum(nearest, shifted(value, "clus", ring, -distance))
    return nearest.reshape(row_count)


def solution(mesh):
    placed = (
        P(("parts", "clus", "mem", "sub"), None),
        P(("parts", "clus", "mem", "sub")),
        P(("parts", "clus", "mem", "sub")),
    )
    return jax.shard_map(
        body,
        mesh=mesh,
        in_specs=placed,
        out_specs=P(("parts", "clus", "mem", "sub")),
        check_vma=False,
    )
```

```python
import jax
import jax.numpy as jnp
from jax import lax
from jax.experimental import pallas as pl
from jax.experimental.pallas import tpu as pltpu
from jax.sharding import PartitionSpec as P

LANES = 128
META_ROWS = 16
DIGIT = 256
VMEM_LIMIT = 24 * 1024 * 1024
NT = (((1,), (1,)), ((), ()))
NONE = -1.0


def meta_kernel(label_ref, rank_ref, meta_ref):
    kind = lax.broadcasted_iota(jnp.int32, meta_ref.shape, 0)
    rank = rank_ref[...]
    meta = jnp.where(kind == 0, label_ref[...], 0)
    meta = jnp.where(kind == 1, rank // DIGIT, meta)
    meta = jnp.where(kind == 2, rank % DIGIT, meta)
    meta_ref[...] = meta.astype(jnp.float32).astype(jnp.bfloat16)


def pack_kernel(meta_ref, chunks_ref, message_ref, sem):
    chunk_rows = chunks_ref.shape[0]
    copy = pltpu.make_async_copy(chunks_ref, message_ref.at[pl.ds(0, chunk_rows), :], sem)
    copy.start()
    message_ref[pl.ds(chunk_rows, META_ROWS), :] = meta_ref[...]
    copy.wait()


def rows_of(message):
    rows = message.shape[1]
    chunks = message.shape[0] // rows
    return jnp.concatenate([message[c * rows : (c + 1) * rows, :] for c in range(chunks)], axis=1)


def meta_of(message):
    meta = message[message.shape[0] - META_ROWS :, :].astype(jnp.float32)
    return meta[0:1], meta[1:2] * DIGIT + meta[2:3]


def best_kernel(line_count, back_count, mem_count, sub_count, *refs):
    plane_count = mem_count * sub_count
    chip, rest = refs[:sub_count], refs[sub_count : plane_count + line_count - 1]
    both_ways, rest = rest[: line_count - 1 - back_count], rest[line_count - 1 - back_count :]
    neighbours, one_way = rest[: plane_count - sub_count], rest[plane_count - sub_count :]
    plane, lines = chip + neighbours, chip[:1] + one_way + both_ways
    outs = refs[line_count - 1 + plane_count :]
    plane_outs, back_outs = outs[:mem_count], outs[mem_count:]
    rows = lines[0].shape[1]

    line_rows = jnp.concatenate([rows_of(line) for line in lines], axis=0)
    columns = []
    for line in lines:
        label, rank = meta_of(line)
        columns.append(jnp.transpose(jnp.concatenate([label, rank] + [rank] * 6, axis=0)))
    columns = jnp.concatenate(columns, axis=0)
    line_label, line_rank = columns[:, 0:1], columns[:, 1:2]

    back = [None] * back_count
    for shift in range(mem_count):
        blocks = plane[shift * sub_count : (shift + 1) * sub_count]
        plane_rows = jnp.concatenate([rows_of(block) for block in blocks], axis=0)
        metas = [meta_of(block) for block in blocks]
        label = jnp.concatenate([meta[0] for meta in metas], axis=1)
        rank = jnp.concatenate([meta[1] for meta in metas], axis=1)
        scores = lax.dot_general(line_rows, plane_rows, NT, preferred_element_type=jnp.float32)
        scores = jnp.where(line_label == label, scores, NONE)
        forward = jnp.where(line_rank < rank, scores, NONE)
        best = jnp.max(forward, axis=0, keepdims=True)
        for turn in range(sub_count):
            plane_outs[shift][turn : turn + 1, :] = best[:, turn * rows : (turn + 1) * rows]
        for index in range(back_count):
            piece = slice((index + 1) * rows, (index + 2) * rows)
            backward = jnp.where(line_rank[piece] > rank, scores[piece], NONE)
            for turn in range(sub_count):
                part = backward[:, turn * rows : (turn + 1) * rows]
                back[index] = part if back[index] is None else jnp.maximum(back[index], part)
    for index in range(back_count):
        back_outs[index][...] = jnp.max(jnp.transpose(back[index]), axis=0, keepdims=True)


def body(embeddings, labels, member_rank):
    row_count, feature_count = embeddings.shape
    clus_count = lax.axis_size("clus")
    mem_count = lax.axis_size("mem")
    sub_count = lax.axis_size("sub")
    chunk_count = feature_count // LANES
    vmem = pl.BlockSpec(memory_space=pltpu.VMEM)
    params = pltpu.CompilerParams(vmem_limit_bytes=VMEM_LIMIT)

    def shifted(value, axis, order, distance):
        count = len(order)
        pairs = [(order[i], order[(i + distance) % count]) for i in range(count)]
        return lax.ppermute(value, axis, pairs)

    half = (clus_count + 1) // 2
    ring = [z for pair in zip(range(half), range(half, 2 * half)) for z in pair if z < clus_count]
    mem_order = list(range(mem_count))
    sub_order = list(range(sub_count))

    meta = pl.pallas_call(
        meta_kernel,
        out_shape=jax.ShapeDtypeStruct((META_ROWS, row_count), jnp.bfloat16),
        in_specs=[vmem, vmem],
        out_specs=vmem,
        compiler_params=params,
        name="meta",
    )(labels.reshape(1, row_count), member_rank.reshape(1, row_count))
    meta, rows = lax.optimization_barrier((meta, embeddings))
    chunks = rows.reshape(row_count, chunk_count, LANES).transpose(1, 0, 2)
    message = pl.pallas_call(
        pack_kernel,
        out_shape=jax.ShapeDtypeStruct((chunk_count * row_count + META_ROWS, LANES), jnp.bfloat16),
        in_specs=[vmem, pl.BlockSpec(memory_space=pl.ANY)],
        out_specs=vmem,
        scratch_shapes=[pltpu.SemaphoreType.DMA(())],
        compiler_params=params,
        name="pack",
    )(meta, chunks.reshape(chunk_count * row_count, LANES))

    distances = list(range(1, clus_count // 2 + 1))
    one_way = [d for d in distances if 2 * d != clus_count]
    lines = [shifted(message, "clus", ring, d) for d in distances]
    def from_plane(value, shift, turn):
        places = [(m, c) for m in range(mem_count) for c in range(sub_count)]
        pairs = [
            (m * sub_count + c, (m + shift) % mem_count * sub_count + (c + turn) % sub_count)
            for m, c in places
        ]
        return lax.ppermute(value, ("mem", "sub"), pairs) if shift or turn else value

    plane = [
        from_plane(message, shift, turn)
        for shift in range(mem_count)
        for turn in range(sub_count)
    ]

    outs = pl.pallas_call(
        lambda *refs: best_kernel(1 + len(lines), len(one_way), mem_count, sub_count, *refs),
        out_shape=[jax.ShapeDtypeStruct((sub_count, row_count), jnp.float32)] * mem_count
        + [jax.ShapeDtypeStruct((1, row_count), jnp.float32)] * len(one_way),
        in_specs=[vmem] * (len(lines) + len(plane)),
        out_specs=[vmem] * (mem_count + len(one_way)),
        compiler_params=params,
        name="best",
    )(*plane[:sub_count], *lines[len(one_way) :], *plane[sub_count:], *lines[: len(one_way)])
    table = outs[0]
    for shift in range(1, mem_count):
        table = jnp.maximum(table, shifted(outs[shift], "mem", mem_order, -shift))
    nearest = table[0:1]
    for turn in range(1, sub_count):
        part = shifted(table[turn : turn + 1], "sub", sub_order, -turn)
        nearest = jnp.maximum(nearest, part)
    for distance, value in zip(one_way, outs[mem_count:]):
        nearest = jnp.maximum(nearest, shifted(value, "clus", ring, -distance))
    return nearest.reshape(row_count)


def solution(mesh):
    placed = (
        P(("parts", "clus", "mem", "sub"), None),
        P(("parts", "clus", "mem", "sub")),
        P(("parts", "clus", "mem", "sub")),
    )
    return jax.shard_map(
        body,
        mesh=mesh,
        in_specs=placed,
        out_specs=P(("parts", "clus", "mem", "sub")),
        check_vma=False,
    )
```

```python
import jax
import jax.numpy as jnp
from jax import lax
from jax.experimental import pallas as pl
from jax.experimental.pallas import tpu as pltpu
from jax.sharding import PartitionSpec as P

LANES = 128
META_ROWS = 16
DIGIT = 256
VMEM_LIMIT = 24 * 1024 * 1024
NT = (((1,), (1,)), ((), ()))
NONE = -1.0


def meta_kernel(label_ref, rank_ref, meta_ref):
    kind = lax.broadcasted_iota(jnp.int32, meta_ref.shape, 0)
    rank = rank_ref[...]
    meta = jnp.where(kind == 0, label_ref[...], 0)
    meta = jnp.where(kind == 1, rank // DIGIT, meta)
    meta = jnp.where(kind == 2, rank % DIGIT, meta)
    meta_ref[...] = meta.astype(jnp.float32).astype(jnp.bfloat16)


def pack_kernel(meta_ref, chunks_ref, message_ref, sem):
    chunk_rows = chunks_ref.shape[0]
    copy = pltpu.make_async_copy(chunks_ref, message_ref.at[pl.ds(0, chunk_rows), :], sem)
    copy.start()
    message_ref[pl.ds(chunk_rows, META_ROWS), :] = meta_ref[...]
    copy.wait()


def label_and_rank(meta):
    meta = meta.astype(jnp.float32)
    return meta[0:1], meta[1:2] * DIGIT + meta[2:3]


def unpacked(message):
    rows = message.shape[1]
    chunks = message.shape[0] // rows
    pieces = [message[c * rows : (c + 1) * rows, :] for c in range(chunks)]
    return jnp.concatenate(pieces, axis=1), *label_and_rank(message[chunks * rows :, :])


def read_blocks(refs, kinds):
    refs = list(refs)
    blocks = []
    for packed in kinds:
        if packed:
            blocks.append(unpacked(refs.pop(0)))
        else:
            rows, meta = refs.pop(0)[...], refs.pop(0)[...]
            blocks.append((rows, *label_and_rank(meta)))
    return blocks


def best_kernel(plane_kinds, line_kinds, back_count, mem_count, sub_count, *refs):
    outs = refs[-mem_count - back_count :]
    plane_outs, back_outs = outs[:mem_count], outs[mem_count:]
    blocks = read_blocks(refs[: -mem_count - back_count], plane_kinds + line_kinds[::-1])
    plane, lines = blocks[: len(plane_kinds)], blocks[len(plane_kinds) :][::-1]
    rows = lines[0][0].shape[0]

    line_rows = jnp.concatenate([line[0] for line in lines], axis=0)
    columns = []
    for _, label, rank in lines:
        columns.append(jnp.transpose(jnp.concatenate([label, rank] + [rank] * 6, axis=0)))
    columns = jnp.concatenate(columns, axis=0)
    line_label, line_rank = columns[:, 0:1], columns[:, 1:2]

    back = [None] * back_count
    for shift in range(mem_count):
        chip = plane[shift * sub_count : (shift + 1) * sub_count]
        chip_rows, label, rank = [
            jnp.concatenate([block[part] for block in chip], axis=min(part, 1)) for part in range(3)
        ]
        scores = lax.dot_general(line_rows, chip_rows, NT, preferred_element_type=jnp.float32)
        scores = jnp.where(line_label == label, scores, NONE)
        forward = jnp.where(line_rank < rank, scores, NONE)
        best = jnp.max(forward, axis=0, keepdims=True)
        for turn in range(sub_count):
            plane_outs[shift][turn : turn + 1, :] = best[:, turn * rows : (turn + 1) * rows]
        for index in range(back_count):
            piece = slice((index + 1) * rows, (index + 2) * rows)
            backward = jnp.where(line_rank[piece] > rank, scores[piece], NONE)
            for turn in range(sub_count):
                part = backward[:, turn * rows : (turn + 1) * rows]
                back[index] = part if back[index] is None else jnp.maximum(back[index], part)
    for index in range(back_count):
        back_outs[index][...] = jnp.max(jnp.transpose(back[index]), axis=0, keepdims=True)


def body(embeddings, labels, member_rank):
    row_count, feature_count = embeddings.shape
    clus_count = lax.axis_size("clus")
    mem_count = lax.axis_size("mem")
    sub_count = lax.axis_size("sub")
    chunk_count = feature_count // LANES
    vmem = pl.BlockSpec(memory_space=pltpu.VMEM)
    params = pltpu.CompilerParams(vmem_limit_bytes=VMEM_LIMIT)

    def shifted(value, axis, order, distance):
        count = len(order)
        pairs = [(order[i], order[(i + distance) % count]) for i in range(count)]
        return lax.ppermute(value, axis, pairs)

    half = (clus_count + 1) // 2
    ring = [z for pair in zip(range(half), range(half, 2 * half)) for z in pair if z < clus_count]
    mem_order = list(range(mem_count))
    sub_order = list(range(sub_count))

    meta = pl.pallas_call(
        meta_kernel,
        out_shape=jax.ShapeDtypeStruct((META_ROWS, row_count), jnp.bfloat16),
        in_specs=[vmem, vmem],
        out_specs=vmem,
        compiler_params=params,
        name="meta",
    )(labels.reshape(1, row_count), member_rank.reshape(1, row_count))
    meta, rows = lax.optimization_barrier((meta, embeddings))
    chunks = rows.reshape(row_count, chunk_count, LANES).transpose(1, 0, 2)
    message = pl.pallas_call(
        pack_kernel,
        out_shape=jax.ShapeDtypeStruct((chunk_count * row_count + META_ROWS, LANES), jnp.bfloat16),
        in_specs=[vmem, pl.BlockSpec(memory_space=pl.ANY)],
        out_specs=vmem,
        scratch_shapes=[pltpu.SemaphoreType.DMA(())],
        compiler_params=params,
        name="pack",
    )(meta, chunks.reshape(chunk_count * row_count, LANES))

    distances = list(range(1, clus_count // 2 + 1))
    one_way = [d for d in distances if 2 * d != clus_count]
    def cores(block):
        return [block] + [shifted(block, "sub", sub_order, turn) for turn in range(1, sub_count)]

    lines = [[message]]
    far_rows = [shifted(embeddings, "clus", ring, d) for d in one_way]
    near_rows = [shifted(embeddings, "mem", mem_order, s) for s in range(1, mem_count)]
    far_metas = [shifted(meta, "clus", ring, d) for d in one_way]
    near_metas = [shifted(meta, "mem", mem_order, s) for s in range(1, mem_count)]
    near_rows, far_rows, near_metas, far_metas = lax.optimization_barrier(
        (near_rows, far_rows, near_metas, far_metas)
    )
    lines += [list(pair) for pair in zip(far_rows, far_metas)]
    both_ways = [shifted(message, "clus", ring, d) for d in distances if d not in one_way]
    near_metas, both_ways = lax.optimization_barrier((near_metas, both_ways))
    lines += [[block] for block in both_ways]
    plane = [[block] for block in cores(message)]
    for rows, whole in zip(near_rows, near_metas):
        plane.extend(list(pair) for pair in zip(cores(rows), cores(whole)))
    plane_kinds = [len(block) == 1 for block in plane]
    line_kinds = [len(block) == 1 for block in lines]
    operands = [value for block in plane + lines[::-1] for value in block]

    outs = pl.pallas_call(
        lambda *refs: best_kernel(
            plane_kinds, line_kinds, len(one_way), mem_count, sub_count, *refs
        ),
        out_shape=[jax.ShapeDtypeStruct((sub_count, row_count), jnp.float32)] * mem_count
        + [jax.ShapeDtypeStruct((1, row_count), jnp.float32)] * len(one_way),
        in_specs=[vmem] * len(operands),
        out_specs=[vmem] * (mem_count + len(one_way)),
        compiler_params=params,
        name="best",
    )(*operands)
    table = outs[0]
    for shift in range(1, mem_count):
        table = jnp.maximum(table, shifted(outs[shift], "mem", mem_order, -shift))
    nearest = table[0:1]
    for turn in range(1, sub_count):
        part = shifted(table[turn : turn + 1], "sub", sub_order, -turn)
        nearest = jnp.maximum(nearest, part)
    for distance, value in zip(one_way, outs[mem_count:]):
        nearest = jnp.maximum(nearest, shifted(value, "clus", ring, -distance))
    return nearest.reshape(row_count)


def solution(mesh):
    placed = (
        P(("parts", "clus", "mem", "sub"), None),
        P(("parts", "clus", "mem", "sub")),
        P(("parts", "clus", "mem", "sub")),
    )
    return jax.shard_map(
        body,
        mesh=mesh,
        in_specs=placed,
        out_specs=P(("parts", "clus", "mem", "sub")),
        check_vma=False,
    )
```

```python
import jax
import jax.numpy as jnp
from jax import lax
from jax.experimental import pallas as pl
from jax.experimental.pallas import tpu as pltpu
from jax.sharding import PartitionSpec as P

LANES = 128
META_ROWS = 16
DIGIT = 256
VMEM_LIMIT = 24 * 1024 * 1024
NT = (((1,), (1,)), ((), ()))
NONE = -1.0


def meta_kernel(label_ref, rank_ref, meta_ref):
    kind = lax.broadcasted_iota(jnp.int32, meta_ref.shape, 0)
    rank = rank_ref[...]
    meta = jnp.where(kind == 0, label_ref[...], 0)
    meta = jnp.where(kind == 1, rank // DIGIT, meta)
    meta = jnp.where(kind == 2, rank % DIGIT, meta)
    meta_ref[...] = meta.astype(jnp.float32).astype(jnp.bfloat16)


def pack_kernel(meta_ref, chunks_ref, message_ref, sem):
    chunk_rows = chunks_ref.shape[0]
    copy = pltpu.make_async_copy(chunks_ref, message_ref.at[pl.ds(0, chunk_rows), :], sem)
    copy.start()
    message_ref[pl.ds(chunk_rows, META_ROWS), :] = meta_ref[...]
    copy.wait()


def rows_of(message):
    rows = message.shape[1]
    chunks = message.shape[0] // rows
    return jnp.concatenate([message[c * rows : (c + 1) * rows, :] for c in range(chunks)], axis=1)


def meta_of(message):
    meta = message[message.shape[0] - META_ROWS :, :].astype(jnp.float32)
    return meta[0:1], meta[1:2] * DIGIT + meta[2:3]


def best_kernel(line_count, back_count, mem_count, sub_count, *refs):
    plane_count = mem_count * sub_count
    plane = refs[:plane_count]
    lines = refs[plane_count : plane_count + line_count][::-1]
    outs = refs[line_count + plane_count :]
    plane_outs, back_outs = outs[:mem_count], outs[mem_count:]
    rows = lines[0].shape[1]

    line_rows = jnp.concatenate([rows_of(line) for line in lines], axis=0)
    columns = []
    for line in lines:
        label, rank = meta_of(line)
        columns.append(jnp.transpose(jnp.concatenate([label, rank] + [rank] * 6, axis=0)))
    columns = jnp.concatenate(columns, axis=0)
    line_label, line_rank = columns[:, 0:1], columns[:, 1:2]

    back = [None] * back_count
    for shift in range(mem_count):
        blocks = plane[shift * sub_count : (shift + 1) * sub_count]
        plane_rows = jnp.concatenate([rows_of(block) for block in blocks], axis=0)
        metas = [meta_of(block) for block in blocks]
        label = jnp.concatenate([meta[0] for meta in metas], axis=1)
        rank = jnp.concatenate([meta[1] for meta in metas], axis=1)
        scores = lax.dot_general(line_rows, plane_rows, NT, preferred_element_type=jnp.float32)
        scores = jnp.where(line_label == label, scores, NONE)
        forward = jnp.where(line_rank < rank, scores, NONE)
        best = jnp.max(forward, axis=0, keepdims=True)
        for turn in range(sub_count):
            plane_outs[shift][turn : turn + 1, :] = best[:, turn * rows : (turn + 1) * rows]
        for index in range(back_count):
            piece = slice((index + 1) * rows, (index + 2) * rows)
            backward = jnp.where(line_rank[piece] > rank, scores[piece], NONE)
            for turn in range(sub_count):
                part = backward[:, turn * rows : (turn + 1) * rows]
                back[index] = part if back[index] is None else jnp.maximum(back[index], part)
    for index in range(back_count):
        back_outs[index][...] = jnp.max(jnp.transpose(back[index]), axis=0, keepdims=True)


def body(embeddings, labels, member_rank):
    row_count, feature_count = embeddings.shape
    clus_count = lax.axis_size("clus")
    mem_count = lax.axis_size("mem")
    sub_count = lax.axis_size("sub")
    chunk_count = feature_count // LANES
    vmem = pl.BlockSpec(memory_space=pltpu.VMEM)
    params = pltpu.CompilerParams(vmem_limit_bytes=VMEM_LIMIT)

    def shifted(value, axis, order, distance):
        count = len(order)
        pairs = [(order[i], order[(i + distance) % count]) for i in range(count)]
        return lax.ppermute(value, axis, pairs)

    half = (clus_count + 1) // 2
    ring = [z for pair in zip(range(half), range(half, 2 * half)) for z in pair if z < clus_count]
    ring.reverse()
    mem_order = list(range(mem_count))
    sub_order = list(range(sub_count))

    meta = pl.pallas_call(
        meta_kernel,
        out_shape=jax.ShapeDtypeStruct((META_ROWS, row_count), jnp.bfloat16),
        in_specs=[vmem, vmem],
        out_specs=vmem,
        compiler_params=params,
        name="meta",
    )(labels.reshape(1, row_count), member_rank.reshape(1, row_count))
    meta, rows = lax.optimization_barrier((meta, embeddings))
    chunks = rows.reshape(row_count, chunk_count, LANES).transpose(1, 0, 2)
    message = pl.pallas_call(
        pack_kernel,
        out_shape=jax.ShapeDtypeStruct((chunk_count * row_count + META_ROWS, LANES), jnp.bfloat16),
        in_specs=[vmem, pl.BlockSpec(memory_space=pl.ANY)],
        out_specs=vmem,
        scratch_shapes=[pltpu.SemaphoreType.DMA(())],
        compiler_params=params,
        name="pack",
    )(meta, chunks.reshape(chunk_count * row_count, LANES))

    distances = list(range(1, clus_count // 2 + 1))
    one_way = [d for d in distances if 2 * d != clus_count]
    lines = [message] + [shifted(message, "clus", ring, d) for d in distances]
    neighbours = [shifted(message, "mem", mem_order, shift) for shift in range(1, mem_count)]
    neighbours, arrived = lax.optimization_barrier((neighbours, lines[1 : 1 + len(one_way)]))
    lines[1 : 1 + len(one_way)] = arrived
    plane = []
    for block in [message] + neighbours:
        plane.append(block)
        plane.extend(shifted(block, "sub", sub_order, turn) for turn in range(1, sub_count))

    outs = pl.pallas_call(
        lambda *refs: best_kernel(len(lines), len(one_way), mem_count, sub_count, *refs),
        out_shape=[jax.ShapeDtypeStruct((sub_count, row_count), jnp.float32)] * mem_count
        + [jax.ShapeDtypeStruct((1, row_count), jnp.float32)] * len(one_way),
        in_specs=[vmem] * (len(lines) + len(plane)),
        out_specs=[vmem] * (mem_count + len(one_way)),
        compiler_params=params,
        name="best",
    )(*plane, *lines[::-1])
    table = outs[0]
    for shift in range(1, mem_count):
        table = jnp.maximum(table, shifted(outs[shift], "mem", mem_order, -shift))
    nearest = table[0:1]
    for turn in range(1, sub_count):
        part = shifted(table[turn : turn + 1], "sub", sub_order, -turn)
        nearest = jnp.maximum(nearest, part)
    for distance, value in zip(one_way, outs[mem_count:]):
        nearest = jnp.maximum(nearest, shifted(value, "clus", ring, -distance))
    return nearest.reshape(row_count)


def solution(mesh):
    placed = (
        P(("parts", "clus", "mem", "sub"), None),
        P(("parts", "clus", "mem", "sub")),
        P(("parts", "clus", "mem", "sub")),
    )
    return jax.shard_map(
        body,
        mesh=mesh,
        in_specs=placed,
        out_specs=P(("parts", "clus", "mem", "sub")),
        check_vma=False,
    )
```

```python
import jax
import jax.numpy as jnp
from jax import lax
from jax.experimental import pallas as pl
from jax.experimental.pallas import tpu as pltpu
from jax.sharding import PartitionSpec as P

LANES = 128
META_ROWS = 16
DIGIT = 256
VMEM_LIMIT = 24 * 1024 * 1024
NT = (((1,), (1,)), ((), ()))
NONE = -1.0


def meta_kernel(label_ref, rank_ref, meta_ref):
    kind = lax.broadcasted_iota(jnp.int32, meta_ref.shape, 0)
    rank = rank_ref[...]
    meta = jnp.where(kind == 0, label_ref[...] + 1, 0)
    meta = jnp.where(kind == 1, rank // DIGIT, meta)
    meta = jnp.where(kind == 2, rank % DIGIT, meta)
    meta_ref[...] = meta.astype(jnp.float32).astype(jnp.bfloat16)


def pack_kernel(meta_ref, chunks_ref, message_ref, sem):
    chunk_rows = chunks_ref.shape[0]
    copy = pltpu.make_async_copy(chunks_ref, message_ref.at[pl.ds(0, chunk_rows), :], sem)
    copy.start()
    message_ref[pl.ds(chunk_rows, META_ROWS), :] = meta_ref[...]
    copy.wait()


def rows_of(message):
    rows = message.shape[1]
    chunks = message.shape[0] // rows
    return jnp.concatenate([message[c * rows : (c + 1) * rows, :] for c in range(chunks)], axis=1)


def meta_of(message):
    meta = message[message.shape[0] - META_ROWS :, :].astype(jnp.float32)
    return meta[0:1], meta[1:2] * DIGIT + meta[2:3]


def best_kernel(line_count, back_count, mem_count, sub_count, *refs):
    plane_count = mem_count * sub_count
    plane = refs[:plane_count]
    lines = refs[plane_count : plane_count + line_count][::-1]
    outs = refs[line_count + plane_count :]
    plane_outs, back_outs = outs[:mem_count], outs[mem_count:]
    rows = lines[0].shape[1]

    line_rows = jnp.concatenate([rows_of(line) for line in lines], axis=0)
    columns = []
    for line in lines:
        label, rank = meta_of(line)
        columns.append(jnp.transpose(jnp.concatenate([label, rank] + [rank] * 6, axis=0)))
    columns = jnp.concatenate(columns, axis=0)
    line_label, line_rank = columns[:, 0:1], columns[:, 1:2]

    back = [None] * back_count
    for shift in range(mem_count):
        blocks = plane[shift * sub_count : (shift + 1) * sub_count]
        plane_rows = jnp.concatenate([rows_of(block) for block in blocks], axis=0)
        metas = [meta_of(block) for block in blocks]
        label = jnp.concatenate([meta[0] for meta in metas], axis=1)
        rank = jnp.concatenate([meta[1] for meta in metas], axis=1)
        scores = lax.dot_general(line_rows, plane_rows, NT, preferred_element_type=jnp.float32)
        scores = jnp.where(line_label == label, scores, NONE)
        forward = jnp.where(line_rank < rank, scores, NONE)
        best = jnp.max(forward, axis=0, keepdims=True)
        for turn in range(sub_count):
            plane_outs[shift][turn : turn + 1, :] = best[:, turn * rows : (turn + 1) * rows]
        for index in range(back_count):
            piece = slice((index + 1) * rows, (index + 2) * rows)
            backward = jnp.where(line_rank[piece] > rank, scores[piece], NONE)
            for turn in range(sub_count):
                part = backward[:, turn * rows : (turn + 1) * rows]
                back[index] = part if back[index] is None else jnp.maximum(back[index], part)
    for index in range(back_count):
        back_outs[index][...] = jnp.max(jnp.transpose(back[index]), axis=0, keepdims=True)


def body(embeddings, labels, member_rank):
    row_count, feature_count = embeddings.shape
    clus_count = lax.axis_size("clus")
    mem_count = lax.axis_size("mem")
    sub_count = lax.axis_size("sub")
    chunk_count = feature_count // LANES
    vmem = pl.BlockSpec(memory_space=pltpu.VMEM)
    params = pltpu.CompilerParams(vmem_limit_bytes=VMEM_LIMIT)

    def shifted(value, axis, order, distance):
        count = len(order)
        pairs = [(order[i], order[(i + distance) % count]) for i in range(count)]
        return lax.ppermute(value, axis, pairs)

    half = (clus_count + 1) // 2
    ring = [z for pair in zip(range(half), range(half, 2 * half)) for z in pair if z < clus_count]
    mem_order = list(range(mem_count))
    sub_order = list(range(sub_count))

    meta = pl.pallas_call(
        meta_kernel,
        out_shape=jax.ShapeDtypeStruct((META_ROWS, row_count), jnp.bfloat16),
        in_specs=[vmem, vmem],
        out_specs=vmem,
        compiler_params=params,
        name="meta",
    )(labels.reshape(1, row_count), member_rank.reshape(1, row_count))
    meta, rows = lax.optimization_barrier((meta, embeddings))
    chunks = rows.reshape(row_count, chunk_count, LANES).transpose(1, 0, 2)
    message = pl.pallas_call(
        pack_kernel,
        out_shape=jax.ShapeDtypeStruct((chunk_count * row_count + META_ROWS, LANES), jnp.bfloat16),
        in_specs=[vmem, pl.BlockSpec(memory_space=pl.ANY)],
        out_specs=vmem,
        scratch_shapes=[pltpu.SemaphoreType.DMA(())],
        compiler_params=params,
        name="pack",
    )(meta, chunks.reshape(chunk_count * row_count, LANES))

    distances = list(range(1, clus_count // 2 + 1))
    one_way = [d for d in distances if 2 * d != clus_count]
    inner = sorted(range(clus_count), key=lambda z: abs(2 * z - clus_count + 1))
    opposite = {z: ring[(ring.index(z) + clus_count // 2) % clus_count] for z in ring}
    outward = [(z, opposite[z]) for z in inner if inner.index(z) < inner.index(opposite[z])]
    lines = [message]
    for distance in distances:
        if distance in one_way:
            lines.append(shifted(message, "clus", ring, distance))
        else:
            lines.append(lax.ppermute(message, "clus", outward))
    neighbours = [shifted(message, "mem", mem_order, shift) for shift in range(1, mem_count)]
    neighbours, arrived = lax.optimization_barrier((neighbours, lines[1 : 1 + len(one_way)]))
    lines[1 : 1 + len(one_way)] = arrived
    plane = []
    for block in [message] + neighbours:
        plane.append(block)
        plane.extend(shifted(block, "sub", sub_order, turn) for turn in range(1, sub_count))

    outs = pl.pallas_call(
        lambda *refs: best_kernel(len(lines), len(distances), mem_count, sub_count, *refs),
        out_shape=[jax.ShapeDtypeStruct((sub_count, row_count), jnp.float32)] * mem_count
        + [jax.ShapeDtypeStruct((1, row_count), jnp.float32)] * len(distances),
        in_specs=[vmem] * (len(lines) + len(plane)),
        out_specs=[vmem] * (mem_count + len(distances)),
        compiler_params=params,
        name="best",
    )(*plane, *lines[::-1])
    table = outs[0]
    for shift in range(1, mem_count):
        table = jnp.maximum(table, shifted(outs[shift], "mem", mem_order, -shift))
    nearest = table[0:1]
    for turn in range(1, sub_count):
        part = shifted(table[turn : turn + 1], "sub", sub_order, -turn)
        nearest = jnp.maximum(nearest, part)
    for distance, value in zip(distances, outs[mem_count:]):
        nearest = jnp.maximum(nearest, shifted(value, "clus", ring, -distance))
    return nearest.reshape(row_count)


def solution(mesh):
    placed = (
        P(("parts", "clus", "mem", "sub"), None),
        P(("parts", "clus", "mem", "sub")),
        P(("parts", "clus", "mem", "sub")),
    )
    return jax.shard_map(
        body,
        mesh=mesh,
        in_specs=placed,
        out_specs=P(("parts", "clus", "mem", "sub")),
        check_vma=False,
    )
```

```python
import jax
import jax.numpy as jnp
from jax import lax
from jax.experimental import pallas as pl
from jax.experimental.pallas import tpu as pltpu
from jax.sharding import PartitionSpec as P

LANES = 128
META_ROWS = 16
DIGIT = 256
VMEM_LIMIT = 24 * 1024 * 1024
NT = (((1,), (1,)), ((), ()))
NONE = -1.0


def meta_kernel(label_ref, rank_ref, meta_ref):
    kind = lax.broadcasted_iota(jnp.int32, meta_ref.shape, 0)
    rank = rank_ref[...]
    meta = jnp.where(kind == 0, label_ref[...], 0)
    meta = jnp.where(kind == 1, rank // DIGIT, meta)
    meta = jnp.where(kind == 2, rank % DIGIT, meta)
    meta_ref[...] = meta.astype(jnp.float32).astype(jnp.bfloat16)


def pack_kernel(meta_ref, chunks_ref, message_ref, sem):
    chunk_rows = chunks_ref.shape[0]
    copy = pltpu.make_async_copy(chunks_ref, message_ref.at[pl.ds(0, chunk_rows), :], sem)
    copy.start()
    message_ref[pl.ds(chunk_rows, META_ROWS), :] = meta_ref[...]
    copy.wait()


def rows_of(message):
    rows = message.shape[1]
    chunks = message.shape[0] // rows
    return jnp.concatenate([message[c * rows : (c + 1) * rows, :] for c in range(chunks)], axis=1)


def meta_of(message):
    meta = message[message.shape[0] - META_ROWS :, :].astype(jnp.float32)
    return meta[0:1], meta[1:2] * DIGIT + meta[2:3]


def best_kernel(line_count, back_count, mem_count, sub_count, *refs):
    plane_count = mem_count * sub_count
    plane = refs[:plane_count]
    lines = refs[plane_count : plane_count + line_count][::-1]
    outs = refs[line_count + plane_count :]
    plane_outs, back_outs = outs[:mem_count], outs[mem_count:]
    rows = lines[0].shape[1]

    line_rows = jnp.concatenate([rows_of(line) for line in lines], axis=0)
    columns = []
    for line in lines:
        label, rank = meta_of(line)
        columns.append(jnp.transpose(jnp.concatenate([label, rank] + [rank] * 6, axis=0)))
    columns = jnp.concatenate(columns, axis=0)
    line_label, line_rank = columns[:, 0:1], columns[:, 1:2]

    back = [None] * back_count
    for shift in range(mem_count):
        blocks = plane[shift * sub_count : (shift + 1) * sub_count]
        plane_rows = jnp.concatenate([rows_of(block) for block in blocks], axis=0)
        metas = [meta_of(block) for block in blocks]
        label = jnp.concatenate([meta[0] for meta in metas], axis=1)
        rank = jnp.concatenate([meta[1] for meta in metas], axis=1)
        scores = lax.dot_general(line_rows, plane_rows, NT, preferred_element_type=jnp.float32)
        scores = jnp.where(line_label == label, scores, NONE)
        forward = jnp.where(line_rank < rank, scores, NONE)
        best = jnp.max(forward, axis=0, keepdims=True)
        for turn in range(sub_count):
            plane_outs[shift][turn : turn + 1, :] = best[:, turn * rows : (turn + 1) * rows]
        for index in range(back_count):
            piece = slice((index + 1) * rows, (index + 2) * rows)
            backward = jnp.where(line_rank[piece] > rank, scores[piece], NONE)
            for turn in range(sub_count):
                part = backward[:, turn * rows : (turn + 1) * rows]
                back[index] = part if back[index] is None else jnp.maximum(back[index], part)
    for index in range(back_count):
        back_outs[index][...] = jnp.max(jnp.transpose(back[index]), axis=0, keepdims=True)


def body(embeddings, labels, member_rank):
    row_count, feature_count = embeddings.shape
    clus_count = lax.axis_size("clus")
    mem_count = lax.axis_size("mem")
    sub_count = lax.axis_size("sub")
    chunk_count = feature_count // LANES
    vmem = pl.BlockSpec(memory_space=pltpu.VMEM)
    params = pltpu.CompilerParams(vmem_limit_bytes=VMEM_LIMIT)

    def shifted(value, axis, order, distance):
        count = len(order)
        pairs = [(order[i], order[(i + distance) % count]) for i in range(count)]
        return lax.ppermute(value, axis, pairs)

    half = (clus_count + 1) // 2
    ring = [z for pair in zip(range(half), range(half, 2 * half)) for z in pair if z < clus_count]
    mem_order = list(range(mem_count))
    sub_order = list(range(sub_count))

    meta = pl.pallas_call(
        meta_kernel,
        out_shape=jax.ShapeDtypeStruct((META_ROWS, row_count), jnp.bfloat16),
        in_specs=[vmem, vmem],
        out_specs=vmem,
        compiler_params=params,
        name="meta",
    )(labels.reshape(1, row_count), member_rank.reshape(1, row_count))
    meta, rows = lax.optimization_barrier((meta, embeddings))
    chunks = rows.reshape(row_count, chunk_count, LANES).transpose(1, 0, 2)
    message = pl.pallas_call(
        pack_kernel,
        out_shape=jax.ShapeDtypeStruct((chunk_count * row_count + META_ROWS, LANES), jnp.bfloat16),
        in_specs=[vmem, pl.BlockSpec(memory_space=pl.ANY)],
        out_specs=vmem,
        scratch_shapes=[pltpu.SemaphoreType.DMA(())],
        compiler_params=params,
        name="pack",
    )(meta, chunks.reshape(chunk_count * row_count, LANES))

    distances = list(range(1, clus_count // 2 + 1))
    one_way = [d for d in distances if 2 * d != clus_count]
    lines = [message] + [shifted(message, "clus", ring, d) for d in distances]
    neighbours = [shifted(message, "mem", mem_order, shift) for shift in range(1, mem_count)]
    neighbours, arrived = lax.optimization_barrier((neighbours, lines[1:]))
    lines[1:] = arrived
    plane = []
    for block in [message] + neighbours:
        plane.append(block)
        plane.extend(shifted(block, "sub", sub_order, turn) for turn in range(1, sub_count))

    outs = pl.pallas_call(
        lambda *refs: best_kernel(len(lines), len(one_way), mem_count, sub_count, *refs),
        out_shape=[jax.ShapeDtypeStruct((sub_count, row_count), jnp.float32)] * mem_count
        + [jax.ShapeDtypeStruct((1, row_count), jnp.float32)] * len(one_way),
        in_specs=[vmem] * (len(lines) + len(plane)),
        out_specs=[vmem] * (mem_count + len(one_way)),
        compiler_params=params,
        name="best",
    )(*plane, *lines[::-1])
    table = outs[0]
    for shift in range(1, mem_count):
        table = jnp.maximum(table, shifted(outs[shift], "mem", mem_order, -shift))
    nearest = table[0:1]
    for turn in range(1, sub_count):
        part = shifted(table[turn : turn + 1], "sub", sub_order, -turn)
        nearest = jnp.maximum(nearest, part)
    for distance, value in zip(one_way, outs[mem_count:]):
        nearest = jnp.maximum(nearest, shifted(value, "clus", ring, -distance))
    return nearest.reshape(row_count)


def solution(mesh):
    placed = (
        P(("parts", "clus", "mem", "sub"), None),
        P(("parts", "clus", "mem", "sub")),
        P(("parts", "clus", "mem", "sub")),
    )
    return jax.shard_map(
        body,
        mesh=mesh,
        in_specs=placed,
        out_specs=P(("parts", "clus", "mem", "sub")),
        check_vma=False,
    )
```

```python
import jax
import jax.numpy as jnp
from jax import lax
from jax.experimental import pallas as pl
from jax.experimental.pallas import tpu as pltpu
from jax.sharding import PartitionSpec as P

LANES = 128
META_ROWS = 16
DIGIT = 256
VMEM_LIMIT = 24 * 1024 * 1024
NT = (((1,), (1,)), ((), ()))
NONE = -1.0


def meta_kernel(label_ref, rank_ref, meta_ref):
    kind = lax.broadcasted_iota(jnp.int32, meta_ref.shape, 0)
    rank = rank_ref[...]
    meta = jnp.where(kind == 0, label_ref[...], 0)
    meta = jnp.where(kind == 1, rank // DIGIT, meta)
    meta = jnp.where(kind == 2, rank % DIGIT, meta)
    meta_ref[...] = meta.astype(jnp.float32).astype(jnp.bfloat16)


def pack_kernel(meta_ref, chunks_ref, message_ref, sem):
    chunk_rows = chunks_ref.shape[0]
    copy = pltpu.make_async_copy(chunks_ref, message_ref.at[pl.ds(0, chunk_rows), :], sem)
    copy.start()
    message_ref[pl.ds(chunk_rows, META_ROWS), :] = meta_ref[...]
    copy.wait()


def rows_of(message):
    rows = message.shape[1]
    chunks = message.shape[0] // rows
    return jnp.concatenate([message[c * rows : (c + 1) * rows, :] for c in range(chunks)], axis=1)


def meta_of(message):
    meta = message[message.shape[0] - META_ROWS :, :].astype(jnp.float32)
    return meta[0:1], meta[1:2] * DIGIT + meta[2:3]


def best_kernel(line_count, back_count, mem_count, sub_count, *refs):
    plane_count = mem_count * sub_count
    plane = refs[:plane_count]
    lines = refs[plane_count : plane_count + line_count][::-1]
    outs = refs[line_count + plane_count :]
    plane_outs, back_outs = outs[:mem_count], outs[mem_count:]
    rows = lines[0].shape[1]

    line_rows = jnp.concatenate([rows_of(line) for line in lines], axis=0)
    columns = []
    for line in lines:
        label, rank = meta_of(line)
        columns.append(jnp.transpose(jnp.concatenate([label, rank] + [rank] * 6, axis=0)))
    columns = jnp.concatenate(columns, axis=0)
    line_label, line_rank = columns[:, 0:1], columns[:, 1:2]

    back = [None] * back_count
    for shift in range(mem_count):
        blocks = plane[shift * sub_count : (shift + 1) * sub_count]
        plane_rows = jnp.concatenate([rows_of(block) for block in blocks], axis=0)
        metas = [meta_of(block) for block in blocks]
        label = jnp.concatenate([meta[0] for meta in metas], axis=1)
        rank = jnp.concatenate([meta[1] for meta in metas], axis=1)
        scores = lax.dot_general(line_rows, plane_rows, NT, preferred_element_type=jnp.float32)
        scores = jnp.where(line_label == label, scores, NONE)
        forward = jnp.where(line_rank < rank, scores, NONE)
        best = jnp.max(forward, axis=0, keepdims=True)
        for turn in range(sub_count):
            plane_outs[shift][turn : turn + 1, :] = best[:, turn * rows : (turn + 1) * rows]
        for index in range(back_count):
            piece = slice((index + 1) * rows, (index + 2) * rows)
            backward = jnp.where(line_rank[piece] > rank, scores[piece], NONE)
            for turn in range(sub_count):
                part = backward[:, turn * rows : (turn + 1) * rows]
                back[index] = part if back[index] is None else jnp.maximum(back[index], part)
    for index in range(back_count):
        back_outs[index][...] = jnp.max(jnp.transpose(back[index]), axis=0, keepdims=True)


def body(embeddings, labels, member_rank):
    row_count, feature_count = embeddings.shape
    clus_count = lax.axis_size("clus")
    mem_count = lax.axis_size("mem")
    sub_count = lax.axis_size("sub")
    chunk_count = feature_count // LANES
    vmem = pl.BlockSpec(memory_space=pltpu.VMEM)
    params = pltpu.CompilerParams(vmem_limit_bytes=VMEM_LIMIT)

    def shifted(value, axis, order, distance):
        count = len(order)
        pairs = [(order[i], order[(i + distance) % count]) for i in range(count)]
        return lax.ppermute(value, axis, pairs)

    half = (clus_count + 1) // 2
    ring = [z for pair in zip(range(half), range(half, 2 * half)) for z in pair if z < clus_count]
    mem_order = list(range(mem_count))
    sub_order = list(range(sub_count))

    meta = pl.pallas_call(
        meta_kernel,
        out_shape=jax.ShapeDtypeStruct((META_ROWS, row_count), jnp.bfloat16),
        in_specs=[vmem, vmem],
        out_specs=vmem,
        compiler_params=params,
        name="meta",
    )(labels.reshape(1, row_count), member_rank.reshape(1, row_count))
    meta, rows = lax.optimization_barrier((meta, embeddings))
    chunks = rows.reshape(row_count, chunk_count, LANES).transpose(1, 0, 2)
    message = pl.pallas_call(
        pack_kernel,
        out_shape=jax.ShapeDtypeStruct((chunk_count * row_count + META_ROWS, LANES), jnp.bfloat16),
        in_specs=[vmem, pl.BlockSpec(memory_space=pl.ANY)],
        out_specs=vmem,
        scratch_shapes=[pltpu.SemaphoreType.DMA(())],
        compiler_params=params,
        name="pack",
    )(meta, chunks.reshape(chunk_count * row_count, LANES))

    distances = list(range(1, clus_count // 2 + 1))
    one_way = [d for d in distances if 2 * d != clus_count]
    lines = [message] + [shifted(message, "clus", ring, d) for d in distances]
    plane = []
    for shift in range(mem_count):
        block = shifted(message, "mem", mem_order, shift) if shift else message
        plane.append(block)
        plane.extend(shifted(block, "sub", sub_order, turn) for turn in range(1, sub_count))

    outs = pl.pallas_call(
        lambda *refs: best_kernel(len(lines), len(one_way), mem_count, sub_count, *refs),
        out_shape=[jax.ShapeDtypeStruct((sub_count, row_count), jnp.float32)] * mem_count
        + [jax.ShapeDtypeStruct((1, row_count), jnp.float32)] * len(one_way),
        in_specs=[vmem] * (len(lines) + len(plane)),
        out_specs=[vmem] * (mem_count + len(one_way)),
        compiler_params=params,
        name="best",
    )(*plane, *lines[::-1])
    table = outs[0]
    for shift in range(1, mem_count):
        table = jnp.maximum(table, shifted(outs[shift], "mem", mem_order, -shift))
    nearest = table[0:1]
    for turn in range(1, sub_count):
        part = shifted(table[turn : turn + 1], "sub", sub_order, -turn)
        nearest = jnp.maximum(nearest, part)
    for distance, value in zip(one_way, outs[mem_count:]):
        nearest = jnp.maximum(nearest, shifted(value, "clus", ring, -distance))
    return nearest.reshape(row_count)


def solution(mesh):
    placed = (
        P(("parts", "clus", "mem", "sub"), None),
        P(("parts", "clus", "mem", "sub")),
        P(("parts", "clus", "mem", "sub")),
    )
    return jax.shard_map(
        body,
        mesh=mesh,
        in_specs=placed,
        out_specs=P(("parts", "clus", "mem", "sub")),
        check_vma=False,
    )
```

```python
import jax
import jax.numpy as jnp
from jax import lax
from jax.experimental import pallas as pl
from jax.experimental.pallas import tpu as pltpu
from jax.sharding import PartitionSpec as P

LANES = 128
META_ROWS = 16
DIGIT = 256
VMEM_LIMIT = 24 * 1024 * 1024
NT = (((1,), (1,)), ((), ()))
NONE = -1.0


def meta_kernel(label_ref, rank_ref, meta_ref):
    kind = lax.broadcasted_iota(jnp.int32, meta_ref.shape, 0)
    rank = rank_ref[...]
    meta = jnp.where(kind == 0, label_ref[...], 0)
    meta = jnp.where(kind == 1, rank // DIGIT, meta)
    meta = jnp.where(kind == 2, rank % DIGIT, meta)
    meta_ref[...] = meta.astype(jnp.float32).astype(jnp.bfloat16)


def pack_kernel(meta_ref, chunks_ref, message_ref, sem):
    chunk_rows = chunks_ref.shape[0]
    copy = pltpu.make_async_copy(chunks_ref, message_ref.at[pl.ds(0, chunk_rows), :], sem)
    copy.start()
    message_ref[pl.ds(chunk_rows, META_ROWS), :] = meta_ref[...]
    copy.wait()


def rows_of(message):
    rows = message.shape[1]
    chunks = message.shape[0] // rows
    return jnp.concatenate([message[c * rows : (c + 1) * rows, :] for c in range(chunks)], axis=1)


def meta_of(message):
    meta = message[message.shape[0] - META_ROWS :, :].astype(jnp.float32)
    return meta[0:1], meta[1:2] * DIGIT + meta[2:3]


def best_kernel(line_count, back_count, mem_count, sub_count, *refs):
    plane_count = mem_count * sub_count
    plane = refs[:plane_count]
    lines = refs[plane_count : plane_count + line_count]
    outs = refs[line_count + plane_count :]
    plane_outs, back_outs = outs[:mem_count], outs[mem_count:]
    rows = lines[0].shape[1]

    line_rows = jnp.concatenate([rows_of(line) for line in lines], axis=0)
    columns = []
    for line in lines:
        label, rank = meta_of(line)
        columns.append(jnp.transpose(jnp.concatenate([label, rank] + [rank] * 6, axis=0)))
    columns = jnp.concatenate(columns, axis=0)
    line_label, line_rank = columns[:, 0:1], columns[:, 1:2]

    back = [None] * back_count
    for shift in range(mem_count):
        blocks = plane[shift * sub_count : (shift + 1) * sub_count]
        plane_rows = jnp.concatenate([rows_of(block) for block in blocks], axis=0)
        metas = [meta_of(block) for block in blocks]
        label = jnp.concatenate([meta[0] for meta in metas], axis=1)
        rank = jnp.concatenate([meta[1] for meta in metas], axis=1)
        scores = lax.dot_general(line_rows, plane_rows, NT, preferred_element_type=jnp.float32)
        scores = jnp.where(line_label == label, scores, NONE)
        forward = jnp.where(line_rank < rank, scores, NONE)
        best = jnp.max(forward, axis=0, keepdims=True)
        for turn in range(sub_count):
            plane_outs[shift][turn : turn + 1, :] = best[:, turn * rows : (turn + 1) * rows]
        for index in range(back_count):
            piece = slice((index + 1) * rows, (index + 2) * rows)
            backward = jnp.where(line_rank[piece] > rank, scores[piece], NONE)
            for turn in range(sub_count):
                part = backward[:, turn * rows : (turn + 1) * rows]
                back[index] = part if back[index] is None else jnp.maximum(back[index], part)
    for index in range(back_count):
        back_outs[index][...] = jnp.max(jnp.transpose(back[index]), axis=0, keepdims=True)


def body(embeddings, labels, member_rank):
    row_count, feature_count = embeddings.shape
    clus_count = lax.axis_size("clus")
    mem_count = lax.axis_size("mem")
    sub_count = lax.axis_size("sub")
    chunk_count = feature_count // LANES
    vmem = pl.BlockSpec(memory_space=pltpu.VMEM)
    params = pltpu.CompilerParams(vmem_limit_bytes=VMEM_LIMIT)

    def shifted(value, axis, order, distance):
        count = len(order)
        pairs = [(order[i], order[(i + distance) % count]) for i in range(count)]
        return lax.ppermute(value, axis, pairs)

    half = (clus_count + 1) // 2
    ring = [z for pair in zip(range(half), range(half, 2 * half)) for z in pair if z < clus_count]
    mem_order = list(range(mem_count))
    sub_order = list(range(sub_count))

    meta = pl.pallas_call(
        meta_kernel,
        out_shape=jax.ShapeDtypeStruct((META_ROWS, row_count), jnp.bfloat16),
        in_specs=[vmem, vmem],
        out_specs=vmem,
        compiler_params=params,
        name="meta",
    )(labels.reshape(1, row_count), member_rank.reshape(1, row_count))
    meta, rows = lax.optimization_barrier((meta, embeddings))
    chunks = rows.reshape(row_count, chunk_count, LANES).transpose(1, 0, 2)
    message = pl.pallas_call(
        pack_kernel,
        out_shape=jax.ShapeDtypeStruct((chunk_count * row_count + META_ROWS, LANES), jnp.bfloat16),
        in_specs=[vmem, pl.BlockSpec(memory_space=pl.ANY)],
        out_specs=vmem,
        scratch_shapes=[pltpu.SemaphoreType.DMA(())],
        compiler_params=params,
        name="pack",
    )(meta, chunks.reshape(chunk_count * row_count, LANES))

    distances = list(range(1, clus_count // 2 + 1))
    one_way = [d for d in distances if 2 * d != clus_count]
    lines = [message] + [shifted(message, "clus", ring, d) for d in distances]
    plane = []
    for shift in range(mem_count):
        block = shifted(message, "mem", mem_order, shift) if shift else message
        plane.append(block)
        plane.extend(shifted(block, "sub", sub_order, turn) for turn in range(1, sub_count))

    outs = pl.pallas_call(
        lambda *refs: best_kernel(len(lines), len(one_way), mem_count, sub_count, *refs),
        out_shape=[jax.ShapeDtypeStruct((sub_count, row_count), jnp.float32)] * mem_count
        + [jax.ShapeDtypeStruct((1, row_count), jnp.float32)] * len(one_way),
        in_specs=[vmem] * (len(lines) + len(plane)),
        out_specs=[vmem] * (mem_count + len(one_way)),
        compiler_params=params,
        name="best",
    )(*plane, *lines)
    table = outs[0]
    for shift in range(1, mem_count):
        table = jnp.maximum(table, shifted(outs[shift], "mem", mem_order, -shift))
    nearest = table[0:1]
    for turn in range(1, sub_count):
        part = shifted(table[turn : turn + 1], "sub", sub_order, -turn)
        nearest = jnp.maximum(nearest, part)
    for distance, value in zip(one_way, outs[mem_count:]):
        nearest = jnp.maximum(nearest, shifted(value, "clus", ring, -distance))
    return nearest.reshape(row_count)


def solution(mesh):
    placed = (
        P(("parts", "clus", "mem", "sub"), None),
        P(("parts", "clus", "mem", "sub")),
        P(("parts", "clus", "mem", "sub")),
    )
    return jax.shard_map(
        body,
        mesh=mesh,
        in_specs=placed,
        out_specs=P(("parts", "clus", "mem", "sub")),
        check_vma=False,
    )
```

```python
import jax
import jax.numpy as jnp
from jax import lax
from jax.experimental import pallas as pl
from jax.experimental.pallas import tpu as pltpu
from jax.sharding import PartitionSpec as P

LANES = 128
META_ROWS = 16
DIGIT = 256
VMEM_LIMIT = 24 * 1024 * 1024
NT = (((1,), (1,)), ((), ()))
NONE = -1.0


def meta_kernel(label_ref, rank_ref, meta_ref):
    kind = lax.broadcasted_iota(jnp.int32, meta_ref.shape, 0)
    rank = rank_ref[...]
    meta = jnp.where(kind == 0, label_ref[...], 0)
    meta = jnp.where(kind == 1, rank // DIGIT, meta)
    meta = jnp.where(kind == 2, rank % DIGIT, meta)
    meta_ref[...] = meta.astype(jnp.float32).astype(jnp.bfloat16)


def pack_kernel(meta_ref, chunks_ref, message_ref, sem):
    chunk_rows = chunks_ref.shape[0]
    copy = pltpu.make_async_copy(chunks_ref, message_ref.at[pl.ds(0, chunk_rows), :], sem)
    copy.start()
    message_ref[pl.ds(chunk_rows, META_ROWS), :] = meta_ref[...]
    copy.wait()


def rows_of(message):
    rows = message.shape[1]
    chunks = message.shape[0] // rows
    return jnp.concatenate([message[c * rows : (c + 1) * rows, :] for c in range(chunks)], axis=1)


def meta_of(message):
    meta = message[message.shape[0] - META_ROWS :, :].astype(jnp.float32)
    return meta[0:1], meta[1:2] * DIGIT + meta[2:3]


def best_kernel(line_count, back_count, mem_count, sub_count, *refs):
    plane_count = mem_count * sub_count
    plane = refs[:plane_count]
    lines = refs[plane_count : plane_count + line_count][::-1]
    outs = refs[line_count + plane_count :]
    plane_outs, back_outs = outs[:mem_count], outs[mem_count:]
    rows = lines[0].shape[1]

    line_rows = jnp.concatenate([rows_of(line) for line in lines], axis=0)
    columns = []
    for line in lines:
        label, rank = meta_of(line)
        columns.append(jnp.transpose(jnp.concatenate([label, rank] + [rank] * 6, axis=0)))
    columns = jnp.concatenate(columns, axis=0)
    line_label, line_rank = columns[:, 0:1], columns[:, 1:2]

    back = [None] * back_count
    for shift in range(mem_count):
        blocks = plane[shift * sub_count : (shift + 1) * sub_count]
        plane_rows = jnp.concatenate([rows_of(block) for block in blocks], axis=0)
        metas = [meta_of(block) for block in blocks]
        label = jnp.concatenate([meta[0] for meta in metas], axis=1)
        rank = jnp.concatenate([meta[1] for meta in metas], axis=1)
        scores = lax.dot_general(line_rows, plane_rows, NT, preferred_element_type=jnp.float32)
        scores = jnp.where(line_label == label, scores, NONE)
        forward = jnp.where(line_rank < rank, scores, NONE)
        best = jnp.max(forward, axis=0, keepdims=True)
        for turn in range(sub_count):
            plane_outs[shift][turn : turn + 1, :] = best[:, turn * rows : (turn + 1) * rows]
        for index in range(back_count):
            piece = slice((index + 1) * rows, (index + 2) * rows)
            backward = jnp.where(line_rank[piece] > rank, scores[piece], NONE)
            for turn in range(sub_count):
                part = backward[:, turn * rows : (turn + 1) * rows]
                back[index] = part if back[index] is None else jnp.maximum(back[index], part)
    for index in range(back_count):
        back_outs[index][...] = jnp.max(jnp.transpose(back[index]), axis=0, keepdims=True)


def body(embeddings, labels, member_rank):
    row_count, feature_count = embeddings.shape
    clus_count = lax.axis_size("clus")
    mem_count = lax.axis_size("mem")
    sub_count = lax.axis_size("sub")
    chunk_count = feature_count // LANES
    vmem = pl.BlockSpec(memory_space=pltpu.VMEM)
    params = pltpu.CompilerParams(vmem_limit_bytes=VMEM_LIMIT)

    def shifted(value, axis, order, distance):
        count = len(order)
        pairs = [(order[i], order[(i + distance) % count]) for i in range(count)]
        return lax.ppermute(value, axis, pairs)

    half = (clus_count + 1) // 2
    ring = [z for pair in zip(range(half), range(half, 2 * half)) for z in pair if z < clus_count]
    mem_order = list(range(mem_count))
    sub_order = list(range(sub_count))

    meta = pl.pallas_call(
        meta_kernel,
        out_shape=jax.ShapeDtypeStruct((META_ROWS, row_count), jnp.bfloat16),
        in_specs=[vmem, vmem],
        out_specs=vmem,
        compiler_params=params,
        name="meta",
    )(labels.reshape(1, row_count), member_rank.reshape(1, row_count))
    meta, rows = lax.optimization_barrier((meta, embeddings))
    chunks = rows.reshape(row_count, chunk_count, LANES).transpose(1, 0, 2)
    message = pl.pallas_call(
        pack_kernel,
        out_shape=jax.ShapeDtypeStruct((chunk_count * row_count + META_ROWS, LANES), jnp.bfloat16),
        in_specs=[vmem, pl.BlockSpec(memory_space=pl.ANY)],
        out_specs=vmem,
        scratch_shapes=[pltpu.SemaphoreType.DMA(())],
        compiler_params=params,
        name="pack",
    )(meta, chunks.reshape(chunk_count * row_count, LANES))

    distances = list(range(1, clus_count // 2 + 1))
    one_way = [d for d in distances if 2 * d != clus_count]
    def crossed(value, distance):
        pairs = [
            (
                z * mem_count + m,
                ring[(ring.index(z) + distance) % clus_count] * mem_count
                + (m + mem_count // 2) % mem_count,
            )
            for z in range(clus_count)
            for m in range(mem_count)
        ]
        return lax.ppermute(value, ("clus", "mem"), pairs)

    lines = [message]
    for distance in distances:
        if distance in one_way:
            lines.append(shifted(message, "clus", ring, distance))
        else:
            lines.append(crossed(message, distance))
    plane = []
    for shift in range(mem_count):
        block = shifted(message, "mem", mem_order, shift) if shift else message
        plane.append(block)
        plane.extend(shifted(block, "sub", sub_order, turn) for turn in range(1, sub_count))

    outs = pl.pallas_call(
        lambda *refs: best_kernel(len(lines), len(one_way), mem_count, sub_count, *refs),
        out_shape=[jax.ShapeDtypeStruct((sub_count, row_count), jnp.float32)] * mem_count
        + [jax.ShapeDtypeStruct((1, row_count), jnp.float32)] * len(one_way),
        in_specs=[vmem] * (len(lines) + len(plane)),
        out_specs=[vmem] * (mem_count + len(one_way)),
        compiler_params=params,
        name="best",
    )(*plane, *lines[::-1])
    table = outs[0]
    for shift in range(1, mem_count):
        table = jnp.maximum(table, shifted(outs[shift], "mem", mem_order, -shift))
    nearest = table[0:1]
    for turn in range(1, sub_count):
        part = shifted(table[turn : turn + 1], "sub", sub_order, -turn)
        nearest = jnp.maximum(nearest, part)
    for distance, value in zip(one_way, outs[mem_count:]):
        nearest = jnp.maximum(nearest, shifted(value, "clus", ring, -distance))
    return nearest.reshape(row_count)


def solution(mesh):
    placed = (
        P(("parts", "clus", "mem", "sub"), None),
        P(("parts", "clus", "mem", "sub")),
        P(("parts", "clus", "mem", "sub")),
    )
    return jax.shard_map(
        body,
        mesh=mesh,
        in_specs=placed,
        out_specs=P(("parts", "clus", "mem", "sub")),
        check_vma=False,
    )
```

```python
import jax
import jax.numpy as jnp
from jax import lax
from jax.experimental import pallas as pl
from jax.experimental.pallas import tpu as pltpu
from jax.sharding import PartitionSpec as P

LANES = 128
META_ROWS = 16
DIGIT = 256
VMEM_LIMIT = 24 * 1024 * 1024
NT = (((1,), (1,)), ((), ()))
NONE = -1.0


def meta_kernel(label_ref, rank_ref, meta_ref):
    kind = lax.broadcasted_iota(jnp.int32, meta_ref.shape, 0)
    rank = rank_ref[...]
    meta = jnp.where(kind == 0, label_ref[...], 0)
    meta = jnp.where(kind == 1, rank // DIGIT, meta)
    meta = jnp.where(kind == 2, rank % DIGIT, meta)
    meta_ref[...] = meta.astype(jnp.float32).astype(jnp.bfloat16)


def pack_kernel(meta_ref, chunks_ref, message_ref, sem):
    chunk_rows = chunks_ref.shape[0]
    copy = pltpu.make_async_copy(chunks_ref, message_ref.at[pl.ds(0, chunk_rows), :], sem)
    copy.start()
    message_ref[pl.ds(chunk_rows, META_ROWS), :] = meta_ref[...]
    copy.wait()


def rows_of(message):
    rows = message.shape[1]
    chunks = message.shape[0] // rows
    return jnp.concatenate([message[c * rows : (c + 1) * rows, :] for c in range(chunks)], axis=1)


def meta_of(message):
    meta = message[message.shape[0] - META_ROWS :, :].astype(jnp.float32)
    return meta[0:1], meta[1:2] * DIGIT + meta[2:3]


def best_kernel(counts, line_count, back_count, with_earlier, *refs):
    refs = list(refs)

    def taken(count):
        return [refs.pop(0) for _ in range(count)]

    blocks = taken(sum(counts))
    lines = taken(line_count)[::-1]
    first_rows = taken(len(counts) if with_earlier else 0)
    earlier_backs = taken(back_count if with_earlier else 0)
    outs, back_outs = taken(len(counts)), refs
    rows = lines[0].shape[1]

    line_rows = jnp.concatenate([rows_of(line) for line in lines], axis=0)
    columns = []
    for line in lines:
        label, rank = meta_of(line)
        columns.append(jnp.transpose(jnp.concatenate([label, rank] + [rank] * 6, axis=0)))
    columns = jnp.concatenate(columns, axis=0)
    line_label, line_rank = columns[:, 0:1], columns[:, 1:2]

    back = [None] * back_count
    for result, count in enumerate(counts):
        group, blocks = blocks[:count], blocks[count:]
        other_rows = jnp.concatenate([rows_of(block) for block in group], axis=0)
        metas = [meta_of(block) for block in group]
        label = jnp.concatenate([meta[0] for meta in metas], axis=1)
        rank = jnp.concatenate([meta[1] for meta in metas], axis=1)
        scores = lax.dot_general(line_rows, other_rows, NT, preferred_element_type=jnp.float32)
        scores = jnp.where(line_label == label, scores, NONE)
        forward = jnp.where(line_rank < rank, scores, NONE)
        best = jnp.max(forward, axis=0, keepdims=True)
        best = [best[:, turn * rows : (turn + 1) * rows] for turn in range(count)]
        if with_earlier:
            best = [first_rows[result][...]] + best
        for turn, row in enumerate(best):
            outs[result][turn : turn + 1, :] = row
        for index in range(back_count):
            piece = slice((index + 1) * rows, (index + 2) * rows)
            backward = jnp.where(line_rank[piece] > rank, scores[piece], NONE)
            for turn in range(count):
                part = backward[:, turn * rows : (turn + 1) * rows]
                back[index] = part if back[index] is None else jnp.maximum(back[index], part)
    for index in range(back_count):
        best = jnp.max(jnp.transpose(back[index]), axis=0, keepdims=True)
        if with_earlier:
            best = jnp.maximum(best, earlier_backs[index][...])
        back_outs[index][...] = best


def body(embeddings, labels, member_rank):
    row_count, feature_count = embeddings.shape
    clus_count = lax.axis_size("clus")
    mem_count = lax.axis_size("mem")
    sub_count = lax.axis_size("sub")
    chunk_count = feature_count // LANES
    vmem = pl.BlockSpec(memory_space=pltpu.VMEM)
    params = pltpu.CompilerParams(vmem_limit_bytes=VMEM_LIMIT)

    def shifted(value, axis, order, distance):
        count = len(order)
        pairs = [(order[i], order[(i + distance) % count]) for i in range(count)]
        return lax.ppermute(value, axis, pairs)

    half = (clus_count + 1) // 2
    ring = [z for pair in zip(range(half), range(half, 2 * half)) for z in pair if z < clus_count]
    mem_order = list(range(mem_count))
    sub_order = list(range(sub_count))

    meta = pl.pallas_call(
        meta_kernel,
        out_shape=jax.ShapeDtypeStruct((META_ROWS, row_count), jnp.bfloat16),
        in_specs=[vmem, vmem],
        out_specs=vmem,
        compiler_params=params,
        name="meta",
    )(labels.reshape(1, row_count), member_rank.reshape(1, row_count))
    meta, rows = lax.optimization_barrier((meta, embeddings))
    chunks = rows.reshape(row_count, chunk_count, LANES).transpose(1, 0, 2)
    message = pl.pallas_call(
        pack_kernel,
        out_shape=jax.ShapeDtypeStruct((chunk_count * row_count + META_ROWS, LANES), jnp.bfloat16),
        in_specs=[vmem, pl.BlockSpec(memory_space=pl.ANY)],
        out_specs=vmem,
        scratch_shapes=[pltpu.SemaphoreType.DMA(())],
        compiler_params=params,
        name="pack",
    )(meta, chunks.reshape(chunk_count * row_count, LANES))

    distances = list(range(1, clus_count // 2 + 1))
    one_way = [d for d in distances if 2 * d != clus_count]
    lines = [message] + [shifted(message, "clus", ring, d) for d in distances]
    neighbours = [shifted(message, "mem", mem_order, shift) for shift in range(1, mem_count)]
    arrived, neighbours = lax.optimization_barrier((lines[1 : 1 + len(one_way)], neighbours))
    lines[1 : 1 + len(one_way)] = arrived
    def cores(block):
        return [shifted(block, "sub", sub_order, turn) for turn in range(1, sub_count)]

    def best_of(groups, earlier):
        counts = [len(group) for group in groups]
        first = bool(earlier)
        operands = [block for group in groups for block in group] + lines[::-1] + earlier
        outs = pl.pallas_call(
            lambda *refs: best_kernel(counts, len(lines), len(one_way), first, *refs),
            out_shape=[
                jax.ShapeDtypeStruct((first + count, row_count), jnp.float32) for count in counts
            ]
            + [jax.ShapeDtypeStruct((1, row_count), jnp.float32)] * len(one_way),
            in_specs=[vmem] * len(operands),
            out_specs=[vmem] * (len(counts) + len(one_way)),
            compiler_params=params,
            name="best",
        )(*operands)
        return outs[: len(counts)], outs[len(counts) :]

    chip = [message] + cores(message)
    tables, backs = best_of([chip] + [[block] for block in neighbours], [])
    if neighbours and sub_count > 1:
        turned = [cores(block) for block in neighbours]
        later, backs = best_of(turned, [*tables[1:], *backs])
        tables = tables[:1] + later
    table = tables[0]
    for shift in range(1, mem_count):
        table = jnp.maximum(table, shifted(tables[shift], "mem", mem_order, -shift))
    nearest = table[0:1]
    for turn in range(1, sub_count):
        part = shifted(table[turn : turn + 1], "sub", sub_order, -turn)
        nearest = jnp.maximum(nearest, part)
    for distance, value in zip(one_way, backs):
        nearest = jnp.maximum(nearest, shifted(value, "clus", ring, -distance))
    return nearest.reshape(row_count)


def solution(mesh):
    placed = (
        P(("parts", "clus", "mem", "sub"), None),
        P(("parts", "clus", "mem", "sub")),
        P(("parts", "clus", "mem", "sub")),
    )
    return jax.shard_map(
        body,
        mesh=mesh,
        in_specs=placed,
        out_specs=P(("parts", "clus", "mem", "sub")),
        check_vma=False,
    )
```

```python
import jax
import jax.numpy as jnp
from jax import lax
from jax.experimental import pallas as pl
from jax.experimental.pallas import tpu as pltpu
from jax.sharding import PartitionSpec as P

LANES = 128
META_ROWS = 16
DIGIT = 256
VMEM_LIMIT = 24 * 1024 * 1024
NT = (((1,), (1,)), ((), ()))
NONE = -1.0


def meta_kernel(label_ref, rank_ref, meta_ref):
    kind = lax.broadcasted_iota(jnp.int32, meta_ref.shape, 0)
    rank = rank_ref[...]
    meta = jnp.where(kind == 0, label_ref[...], 0)
    meta = jnp.where(kind == 1, rank // DIGIT, meta)
    meta = jnp.where(kind == 2, rank % DIGIT, meta)
    meta_ref[...] = meta.astype(jnp.float32).astype(jnp.bfloat16)


def pack_kernel(meta_ref, chunks_ref, message_ref, sem):
    chunk_rows = chunks_ref.shape[0]
    copy = pltpu.make_async_copy(chunks_ref, message_ref.at[pl.ds(0, chunk_rows), :], sem)
    copy.start()
    message_ref[pl.ds(chunk_rows, META_ROWS), :] = meta_ref[...]
    copy.wait()


def rows_of(message):
    rows = message.shape[1]
    chunks = message.shape[0] // rows
    return jnp.concatenate([message[c * rows : (c + 1) * rows, :] for c in range(chunks)], axis=1)


def meta_of(message):
    meta = message[message.shape[0] - META_ROWS :, :].astype(jnp.float32)
    return meta[0:1], meta[1:2] * DIGIT + meta[2:3]


def best_kernel(line_count, back_count, mem_count, sub_count, *refs):
    plane_count = mem_count * sub_count
    plane = refs[:plane_count]
    lines = refs[plane_count : plane_count + line_count]
    outs = refs[line_count + plane_count :]
    plane_outs, back_outs = outs[:mem_count], outs[mem_count:]
    rows = lines[0].shape[1]

    line_rows = jnp.concatenate([rows_of(line) for line in lines], axis=0)
    columns = []
    for line in lines:
        label, rank = meta_of(line)
        columns.append(jnp.transpose(jnp.concatenate([label, rank] + [rank] * 6, axis=0)))
    columns = jnp.concatenate(columns, axis=0)
    line_label, line_rank = columns[:, 0:1], columns[:, 1:2]

    back = [None] * back_count
    for shift in range(mem_count):
        blocks = plane[shift * sub_count : (shift + 1) * sub_count]
        plane_rows = jnp.concatenate([rows_of(block) for block in blocks], axis=0)
        metas = [meta_of(block) for block in blocks]
        label = jnp.concatenate([meta[0] for meta in metas], axis=1)
        rank = jnp.concatenate([meta[1] for meta in metas], axis=1)
        scores = lax.dot_general(line_rows, plane_rows, NT, preferred_element_type=jnp.float32)
        scores = jnp.where(line_label == label, scores, NONE)
        forward = jnp.where(line_rank < rank, scores, NONE)
        best = jnp.max(forward, axis=0, keepdims=True)
        for turn in range(sub_count):
            plane_outs[shift][turn : turn + 1, :] = best[:, turn * rows : (turn + 1) * rows]
        for index in range(back_count):
            piece = slice((index + 1) * rows, (index + 2) * rows)
            backward = jnp.where(line_rank[piece] > rank, scores[piece], NONE)
            for turn in range(sub_count):
                part = backward[:, turn * rows : (turn + 1) * rows]
                back[index] = part if back[index] is None else jnp.maximum(back[index], part)
    for index in range(back_count):
        back_outs[index][...] = jnp.max(jnp.transpose(back[index]), axis=0, keepdims=True)


def body(embeddings, labels, member_rank):
    row_count, feature_count = embeddings.shape
    clus_count = lax.axis_size("clus")
    mem_count = lax.axis_size("mem")
    sub_count = lax.axis_size("sub")
    chunk_count = feature_count // LANES
    vmem = pl.BlockSpec(memory_space=pltpu.VMEM)
    params = pltpu.CompilerParams(vmem_limit_bytes=VMEM_LIMIT)

    def shifted(value, axis, order, distance):
        count = len(order)
        pairs = [(order[i], order[(i + distance) % count]) for i in range(count)]
        return lax.ppermute(value, axis, pairs)

    ring = list(range(clus_count))[::-1]
    mem_order = list(range(mem_count))
    sub_order = list(range(sub_count))

    meta = pl.pallas_call(
        meta_kernel,
        out_shape=jax.ShapeDtypeStruct((META_ROWS, row_count), jnp.bfloat16),
        in_specs=[vmem, vmem],
        out_specs=vmem,
        compiler_params=params,
        name="meta",
    )(labels.reshape(1, row_count), member_rank.reshape(1, row_count))
    meta, rows = lax.optimization_barrier((meta, embeddings))
    chunks = rows.reshape(row_count, chunk_count, LANES).transpose(1, 0, 2)
    message = pl.pallas_call(
        pack_kernel,
        out_shape=jax.ShapeDtypeStruct((chunk_count * row_count + META_ROWS, LANES), jnp.bfloat16),
        in_specs=[vmem, pl.BlockSpec(memory_space=pl.ANY)],
        out_specs=vmem,
        scratch_shapes=[pltpu.SemaphoreType.DMA(())],
        compiler_params=params,
        name="pack",
    )(meta, chunks.reshape(chunk_count * row_count, LANES))

    distances = list(range(1, clus_count // 2 + 1))
    one_way = [d for d in distances if 2 * d != clus_count]
    lines = [message] + [shifted(message, "clus", ring, d) for d in distances]
    plane = []
    for shift in range(mem_count):
        block = shifted(message, "mem", mem_order, shift) if shift else message
        plane.append(block)
        plane.extend(shifted(block, "sub", sub_order, turn) for turn in range(1, sub_count))

    outs = pl.pallas_call(
        lambda *refs: best_kernel(len(lines), len(one_way), mem_count, sub_count, *refs),
        out_shape=[jax.ShapeDtypeStruct((sub_count, row_count), jnp.float32)] * mem_count
        + [jax.ShapeDtypeStruct((1, row_count), jnp.float32)] * len(one_way),
        in_specs=[vmem] * (len(lines) + len(plane)),
        out_specs=[vmem] * (mem_count + len(one_way)),
        compiler_params=params,
        name="best",
    )(*plane, *lines)
    table = outs[0]
    for shift in range(1, mem_count):
        table = jnp.maximum(table, shifted(outs[shift], "mem", mem_order, -shift))
    nearest = table[0:1]
    for turn in range(1, sub_count):
        part = shifted(table[turn : turn + 1], "sub", sub_order, -turn)
        nearest = jnp.maximum(nearest, part)
    for distance, value in zip(one_way, outs[mem_count:]):
        nearest = jnp.maximum(nearest, shifted(value, "clus", ring, -distance))
    return nearest.reshape(row_count)


def solution(mesh):
    placed = (
        P(("parts", "clus", "mem", "sub"), None),
        P(("parts", "clus", "mem", "sub")),
        P(("parts", "clus", "mem", "sub")),
    )
    return jax.shard_map(
        body,
        mesh=mesh,
        in_specs=placed,
        out_specs=P(("parts", "clus", "mem", "sub")),
        check_vma=False,
    )
```

```python
import jax
import jax.numpy as jnp
from jax import lax
from jax.experimental import pallas as pl
from jax.experimental.pallas import tpu as pltpu
from jax.sharding import PartitionSpec as P

LANES = 128
META_ROWS = 16
DIGIT = 256
VMEM_LIMIT = 24 * 1024 * 1024
NT = (((1,), (1,)), ((), ()))
NONE = -1.0


def meta_kernel(label_ref, rank_ref, meta_ref):
    kind = lax.broadcasted_iota(jnp.int32, meta_ref.shape, 0)
    rank = rank_ref[...]
    meta = jnp.where(kind == 0, label_ref[...], 0)
    meta = jnp.where(kind == 1, rank // DIGIT, meta)
    meta = jnp.where(kind == 2, rank % DIGIT, meta)
    meta_ref[...] = meta.astype(jnp.float32).astype(jnp.bfloat16)


def pack_kernel(meta_ref, chunks_ref, message_ref, sem):
    chunk_rows = chunks_ref.shape[0]
    copy = pltpu.make_async_copy(chunks_ref, message_ref.at[pl.ds(0, chunk_rows), :], sem)
    copy.start()
    message_ref[pl.ds(chunk_rows, META_ROWS), :] = meta_ref[...]
    copy.wait()


def rows_of(message):
    rows = message.shape[1]
    chunks = message.shape[0] // rows
    return jnp.concatenate([message[c * rows : (c + 1) * rows, :] for c in range(chunks)], axis=1)


def meta_of(message):
    meta = message[message.shape[0] - META_ROWS :, :].astype(jnp.float32)
    return meta[0:1], meta[1:2] * DIGIT + meta[2:3]


def best_kernel(line_count, back_count, mem_count, sub_count, *refs):
    plane_count = mem_count * sub_count
    plane = refs[:plane_count]
    lines = refs[plane_count : plane_count + line_count]
    outs = refs[line_count + plane_count :]
    plane_outs, back_outs = outs[:mem_count], outs[mem_count:]
    rows = lines[0].shape[1]

    line_rows = jnp.concatenate([rows_of(line) for line in lines], axis=0)
    columns = []
    for line in lines:
        label, rank = meta_of(line)
        columns.append(jnp.transpose(jnp.concatenate([label, rank] + [rank] * 6, axis=0)))
    columns = jnp.concatenate(columns, axis=0)
    line_label, line_rank = columns[:, 0:1], columns[:, 1:2]

    back = [None] * back_count
    for shift in range(mem_count):
        blocks = plane[shift * sub_count : (shift + 1) * sub_count]
        plane_rows = jnp.concatenate([rows_of(block) for block in blocks], axis=0)
        metas = [meta_of(block) for block in blocks]
        label = jnp.concatenate([meta[0] for meta in metas], axis=1)
        rank = jnp.concatenate([meta[1] for meta in metas], axis=1)
        scores = lax.dot_general(line_rows, plane_rows, NT, preferred_element_type=jnp.float32)
        scores = jnp.where(line_label == label, scores, NONE)
        forward = jnp.where(line_rank < rank, scores, NONE)
        best = jnp.max(forward, axis=0, keepdims=True)
        for turn in range(sub_count):
            plane_outs[shift][turn : turn + 1, :] = best[:, turn * rows : (turn + 1) * rows]
        for index in range(back_count):
            piece = slice((index + 1) * rows, (index + 2) * rows)
            backward = jnp.where(line_rank[piece] > rank, scores[piece], NONE)
            for turn in range(sub_count):
                part = backward[:, turn * rows : (turn + 1) * rows]
                back[index] = part if back[index] is None else jnp.maximum(back[index], part)
    for index in range(back_count):
        back_outs[index][...] = jnp.max(jnp.transpose(back[index]), axis=0, keepdims=True)


def body(embeddings, labels, member_rank):
    row_count, feature_count = embeddings.shape
    clus_count = lax.axis_size("clus")
    mem_count = lax.axis_size("mem")
    sub_count = lax.axis_size("sub")
    chunk_count = feature_count // LANES
    vmem = pl.BlockSpec(memory_space=pltpu.VMEM)
    params = pltpu.CompilerParams(vmem_limit_bytes=VMEM_LIMIT)

    def shifted(value, axis, order, distance):
        count = len(order)
        pairs = [(order[i], order[(i + distance) % count]) for i in range(count)]
        return lax.ppermute(value, axis, pairs)

    half = (clus_count + 1) // 2
    ring = [z for pair in zip(range(half), range(half, 2 * half)) for z in pair if z < clus_count]
    ring.reverse()
    mem_order = list(range(mem_count))
    sub_order = list(range(sub_count))

    meta = pl.pallas_call(
        meta_kernel,
        out_shape=jax.ShapeDtypeStruct((META_ROWS, row_count), jnp.bfloat16),
        in_specs=[vmem, vmem],
        out_specs=vmem,
        compiler_params=params,
        name="meta",
    )(labels.reshape(1, row_count), member_rank.reshape(1, row_count))
    meta, rows = lax.optimization_barrier((meta, embeddings))
    chunks = rows.reshape(row_count, chunk_count, LANES).transpose(1, 0, 2)
    message = pl.pallas_call(
        pack_kernel,
        out_shape=jax.ShapeDtypeStruct((chunk_count * row_count + META_ROWS, LANES), jnp.bfloat16),
        in_specs=[vmem, pl.BlockSpec(memory_space=pl.ANY)],
        out_specs=vmem,
        scratch_shapes=[pltpu.SemaphoreType.DMA(())],
        compiler_params=params,
        name="pack",
    )(meta, chunks.reshape(chunk_count * row_count, LANES))

    distances = list(range(1, clus_count // 2 + 1))
    one_way = [d for d in distances if 2 * d != clus_count]
    lines = [message] + [shifted(message, "clus", ring, d) for d in distances]
    plane = []
    for shift in range(mem_count):
        block = shifted(message, "mem", mem_order, shift) if shift else message
        plane.append(block)
        plane.extend(shifted(block, "sub", sub_order, turn) for turn in range(1, sub_count))

    outs = pl.pallas_call(
        lambda *refs: best_kernel(len(lines), len(one_way), mem_count, sub_count, *refs),
        out_shape=[jax.ShapeDtypeStruct((sub_count, row_count), jnp.float32)] * mem_count
        + [jax.ShapeDtypeStruct((1, row_count), jnp.float32)] * len(one_way),
        in_specs=[vmem] * (len(lines) + len(plane)),
        out_specs=[vmem] * (mem_count + len(one_way)),
        compiler_params=params,
        name="best",
    )(*plane, *lines)
    table = outs[0]
    for shift in range(1, mem_count):
        table = jnp.maximum(table, shifted(outs[shift], "mem", mem_order, -shift))
    nearest = table[0:1]
    for turn in range(1, sub_count):
        part = shifted(table[turn : turn + 1], "sub", sub_order, -turn)
        nearest = jnp.maximum(nearest, part)
    for distance, value in zip(one_way, outs[mem_count:]):
        nearest = jnp.maximum(nearest, shifted(value, "clus", ring, -distance))
    return nearest.reshape(row_count)


def solution(mesh):
    placed = (
        P(("parts", "clus", "mem", "sub"), None),
        P(("parts", "clus", "mem", "sub")),
        P(("parts", "clus", "mem", "sub")),
    )
    return jax.shard_map(
        body,
        mesh=mesh,
        in_specs=placed,
        out_specs=P(("parts", "clus", "mem", "sub")),
        check_vma=False,
    )
```

```python
import jax
import jax.numpy as jnp
from jax import lax
from jax.experimental import pallas as pl
from jax.experimental.pallas import tpu as pltpu
from jax.sharding import PartitionSpec as P

LANES = 128
SUBLANES = 8
META_ROWS = 16
DIGIT = 256
VMEM_LIMIT = 24 * 1024 * 1024
NT = (((1,), (1,)), ((), ()))
NONE = -1.0


def meta_kernel(label_ref, rank_ref, meta_ref):
    kind = lax.broadcasted_iota(jnp.int32, meta_ref.shape, 0)
    rank = rank_ref[...]
    meta = jnp.where(kind == 0, label_ref[...], 0)
    meta = jnp.where(kind == 1, rank // DIGIT, meta)
    meta = jnp.where(kind == 2, rank % DIGIT, meta)
    meta_ref[...] = meta.astype(jnp.float32).astype(jnp.bfloat16)


def pack_kernel(meta_ref, chunks_ref, message_ref, sem):
    chunk_rows = chunks_ref.shape[0]
    copy = pltpu.make_async_copy(chunks_ref, message_ref.at[pl.ds(0, chunk_rows), :], sem)
    copy.start()
    message_ref[pl.ds(chunk_rows, META_ROWS), :] = meta_ref[...]
    copy.wait()


def rows_of(message):
    rows = message.shape[1]
    chunks = message.shape[0] // rows
    return jnp.concatenate([message[c * rows : (c + 1) * rows, :] for c in range(chunks)], axis=1)


def meta_of(message):
    meta = message[message.shape[0] - META_ROWS :, :].astype(jnp.float32)
    return meta[0:1], meta[1:2] * DIGIT + meta[2:3]


def best_kernel(line_count, back_count, mem_count, sub_count, *refs):
    plane_count = mem_count * sub_count
    plane = refs[:plane_count]
    lines = refs[plane_count : plane_count + line_count]
    outs = refs[line_count + plane_count :]
    plane_outs, back_outs = outs[:mem_count], outs[mem_count:]
    rows = lines[0].shape[1]

    line_rows = jnp.concatenate([rows_of(line) for line in lines], axis=0)
    plane_rows = jnp.concatenate([rows_of(block) for block in plane], axis=0)
    metas = [part for line in lines for part in meta_of(line)]
    metas += [metas[-1]] * (-len(metas) % SUBLANES)
    columns = jnp.transpose(jnp.concatenate(metas, axis=0))
    line_label, line_rank = [
        jnp.concatenate(
            [columns[:, 2 * index + part : 2 * index + part + 1] for index in range(line_count)],
            axis=0,
        )
        for part in range(2)
    ]
    label, rank = [jnp.concatenate(parts, axis=1) for parts in zip(*map(meta_of, plane))]

    scores = lax.dot_general(line_rows, plane_rows, NT, preferred_element_type=jnp.float32)
    scores = jnp.where(line_label == label, scores, NONE)
    forward = jnp.where(line_rank < rank, scores, NONE)
    best = jnp.max(forward, axis=0, keepdims=True)
    for block in range(plane_count):
        shift, turn = block // sub_count, block % sub_count
        plane_outs[shift][turn : turn + 1, :] = best[:, block * rows : (block + 1) * rows]
    for index in range(back_count):
        piece = slice((index + 1) * rows, (index + 2) * rows)
        backward = jnp.where(line_rank[piece] > rank, scores[piece], NONE)
        back = backward[:, :rows]
        for block in range(1, plane_count):
            back = jnp.maximum(back, backward[:, block * rows : (block + 1) * rows])
        back_outs[index][...] = jnp.max(jnp.transpose(back), axis=0, keepdims=True)


def body(embeddings, labels, member_rank):
    row_count, feature_count = embeddings.shape
    clus_count = lax.axis_size("clus")
    mem_count = lax.axis_size("mem")
    sub_count = lax.axis_size("sub")
    chunk_count = feature_count // LANES
    vmem = pl.BlockSpec(memory_space=pltpu.VMEM)
    params = pltpu.CompilerParams(vmem_limit_bytes=VMEM_LIMIT)

    def shifted(value, axis, order, distance):
        count = len(order)
        pairs = [(order[i], order[(i + distance) % count]) for i in range(count)]
        return lax.ppermute(value, axis, pairs)

    half = (clus_count + 1) // 2
    ring = [z for pair in zip(range(half), range(half, 2 * half)) for z in pair if z < clus_count]
    mem_order = list(range(mem_count))
    sub_order = list(range(sub_count))

    meta = pl.pallas_call(
        meta_kernel,
        out_shape=jax.ShapeDtypeStruct((META_ROWS, row_count), jnp.bfloat16),
        in_specs=[vmem, vmem],
        out_specs=vmem,
        compiler_params=params,
        name="meta",
    )(labels.reshape(1, row_count), member_rank.reshape(1, row_count))
    meta, rows = lax.optimization_barrier((meta, embeddings))
    chunks = rows.reshape(row_count, chunk_count, LANES).transpose(1, 0, 2)
    message = pl.pallas_call(
        pack_kernel,
        out_shape=jax.ShapeDtypeStruct((chunk_count * row_count + META_ROWS, LANES), jnp.bfloat16),
        in_specs=[vmem, pl.BlockSpec(memory_space=pl.ANY)],
        out_specs=vmem,
        scratch_shapes=[pltpu.SemaphoreType.DMA(())],
        compiler_params=params,
        name="pack",
    )(meta, chunks.reshape(chunk_count * row_count, LANES))

    distances = list(range(1, clus_count // 2 + 1))
    one_way = [d for d in distances if 2 * d != clus_count]
    lines = [message] + [shifted(message, "clus", ring, d) for d in distances]
    plane = []
    for shift in range(mem_count):
        block = shifted(message, "mem", mem_order, shift) if shift else message
        plane.append(block)
        plane.extend(shifted(block, "sub", sub_order, turn) for turn in range(1, sub_count))

    outs = pl.pallas_call(
        lambda *refs: best_kernel(len(lines), len(one_way), mem_count, sub_count, *refs),
        out_shape=[jax.ShapeDtypeStruct((sub_count, row_count), jnp.float32)] * mem_count
        + [jax.ShapeDtypeStruct((1, row_count), jnp.float32)] * len(one_way),
        in_specs=[vmem] * (len(lines) + len(plane)),
        out_specs=[vmem] * (mem_count + len(one_way)),
        compiler_params=params,
        name="best",
    )(*plane, *lines)
    table = outs[0]
    for shift in range(1, mem_count):
        table = jnp.maximum(table, shifted(outs[shift], "mem", mem_order, -shift))
    nearest = table[0:1]
    for turn in range(1, sub_count):
        part = shifted(table[turn : turn + 1], "sub", sub_order, -turn)
        nearest = jnp.maximum(nearest, part)
    for distance, value in zip(one_way, outs[mem_count:]):
        nearest = jnp.maximum(nearest, shifted(value, "clus", ring, -distance))
    return nearest.reshape(row_count)


def solution(mesh):
    placed = (
        P(("parts", "clus", "mem", "sub"), None),
        P(("parts", "clus", "mem", "sub")),
        P(("parts", "clus", "mem", "sub")),
    )
    return jax.shard_map(
        body,
        mesh=mesh,
        in_specs=placed,
        out_specs=P(("parts", "clus", "mem", "sub")),
        check_vma=False,
    )
```

```python
import jax
import jax.numpy as jnp
from jax import lax
from jax.experimental import pallas as pl
from jax.experimental.pallas import tpu as pltpu
from jax.sharding import PartitionSpec as P

LANES = 128
SUBLANES = 8
META_ROWS = 16
DIGIT = 256
VMEM_LIMIT = 24 * 1024 * 1024
NT = (((1,), (1,)), ((), ()))
NONE = -1.0


def meta_kernel(label_ref, rank_ref, meta_ref):
    kind = lax.broadcasted_iota(jnp.int32, meta_ref.shape, 0)
    rank = rank_ref[...]
    meta = jnp.where(kind == 0, label_ref[...], 0)
    meta = jnp.where(kind == 1, rank // DIGIT, meta)
    meta = jnp.where(kind == 2, rank % DIGIT, meta)
    meta_ref[...] = meta.astype(jnp.float32).astype(jnp.bfloat16)


def pack_kernel(meta_ref, chunks_ref, message_ref, sem):
    chunk_rows = chunks_ref.shape[0]
    copy = pltpu.make_async_copy(chunks_ref, message_ref.at[pl.ds(0, chunk_rows), :], sem)
    copy.start()
    message_ref[pl.ds(chunk_rows, META_ROWS), :] = meta_ref[...]
    copy.wait()


def rows_of(message):
    rows = message.shape[1]
    chunks = message.shape[0] // rows
    return jnp.concatenate([message[c * rows : (c + 1) * rows, :] for c in range(chunks)], axis=1)


def meta_of(message):
    meta = message[message.shape[0] - META_ROWS :, :].astype(jnp.float32)
    return meta[0:1], meta[1:2] * DIGIT + meta[2:3]


def best_kernel(line_count, back_count, mem_count, sub_count, *refs):
    plane_count = mem_count * sub_count
    plane = refs[:plane_count]
    lines = refs[plane_count : plane_count + line_count]
    outs = refs[line_count + plane_count :]
    plane_outs, back_outs = outs[:mem_count], outs[mem_count:]
    rows = lines[0].shape[1]

    line_rows = jnp.concatenate([rows_of(line) for line in lines], axis=0)
    plane_rows = jnp.concatenate([rows_of(block) for block in plane], axis=0)
    metas = [part for line in lines for part in meta_of(line)]
    metas += [metas[-1]] * (-len(metas) % SUBLANES)
    columns = jnp.transpose(jnp.concatenate(metas, axis=0))
    line_label, line_rank = [
        jnp.concatenate(
            [columns[:, 2 * index + part : 2 * index + part + 1] for index in range(line_count)],
            axis=0,
        )
        for part in range(2)
    ]
    label, rank = [jnp.concatenate(parts, axis=1) for parts in zip(*map(meta_of, plane))]

    scores = lax.dot_general(line_rows, plane_rows, NT, preferred_element_type=jnp.float32)
    scores = jnp.where(line_label == label, scores, NONE)
    forward = jnp.where(line_rank < rank, scores, NONE)
    best = jnp.max(forward, axis=0, keepdims=True)
    for block in range(plane_count):
        shift, turn = block // sub_count, block % sub_count
        plane_outs[shift][turn : turn + 1, :] = best[:, block * rows : (block + 1) * rows]
    for index in range(back_count):
        piece = slice((index + 1) * rows, (index + 2) * rows)
        backward = jnp.where(line_rank[piece] > rank, scores[piece], NONE)
        back = backward[:, :rows]
        for block in range(1, plane_count):
            back = jnp.maximum(back, backward[:, block * rows : (block + 1) * rows])
        back_outs[index][...] = jnp.max(jnp.transpose(back), axis=0, keepdims=True)


def body(embeddings, labels, member_rank):
    row_count, feature_count = embeddings.shape
    clus_count = lax.axis_size("clus")
    mem_count = lax.axis_size("mem")
    sub_count = lax.axis_size("sub")
    chunk_count = feature_count // LANES
    vmem = pl.BlockSpec(memory_space=pltpu.VMEM)
    params = pltpu.CompilerParams(vmem_limit_bytes=VMEM_LIMIT)

    def shifted(value, axis, order, distance):
        count = len(order)
        pairs = [(order[i], order[(i + distance) % count]) for i in range(count)]
        return lax.ppermute(value, axis, pairs)

    half = (clus_count + 1) // 2
    ring = [z for pair in zip(range(half), range(half, 2 * half)) for z in pair if z < clus_count]
    mem_order = list(range(mem_count))
    sub_order = list(range(sub_count))

    meta = pl.pallas_call(
        meta_kernel,
        out_shape=jax.ShapeDtypeStruct((META_ROWS, row_count), jnp.bfloat16),
        in_specs=[vmem, vmem],
        out_specs=vmem,
        compiler_params=params,
        name="meta",
    )(labels.reshape(1, row_count), member_rank.reshape(1, row_count))
    meta, rows = lax.optimization_barrier((meta, embeddings))
    chunks = rows.reshape(row_count, chunk_count, LANES).transpose(1, 0, 2)
    message = pl.pallas_call(
        pack_kernel,
        out_shape=jax.ShapeDtypeStruct((chunk_count * row_count + META_ROWS, LANES), jnp.bfloat16),
        in_specs=[vmem, pl.BlockSpec(memory_space=pl.ANY)],
        out_specs=vmem,
        scratch_shapes=[pltpu.SemaphoreType.DMA(())],
        compiler_params=params,
        name="pack",
    )(meta, chunks.reshape(chunk_count * row_count, LANES))

    distances = list(range(1, clus_count // 2 + 1))
    one_way = [d for d in distances if 2 * d != clus_count]
    lines = [message] + [shifted(message, "clus", ring, d) for d in distances]
    neighbours = [shifted(message, "mem", mem_order, shift) for shift in range(1, mem_count)]
    neighbours, arrived = lax.optimization_barrier((neighbours, lines[1 + len(one_way) :]))
    lines[1 + len(one_way) :] = arrived
    plane = []
    for block in [message] + neighbours:
        plane.append(block)
        plane.extend(shifted(block, "sub", sub_order, turn) for turn in range(1, sub_count))

    outs = pl.pallas_call(
        lambda *refs: best_kernel(len(lines), len(one_way), mem_count, sub_count, *refs),
        out_shape=[jax.ShapeDtypeStruct((sub_count, row_count), jnp.float32)] * mem_count
        + [jax.ShapeDtypeStruct((1, row_count), jnp.float32)] * len(one_way),
        in_specs=[vmem] * (len(lines) + len(plane)),
        out_specs=[vmem] * (mem_count + len(one_way)),
        compiler_params=params,
        name="best",
    )(*plane, *lines)
    table = outs[0]
    for shift in range(1, mem_count):
        table = jnp.maximum(table, shifted(outs[shift], "mem", mem_order, -shift))
    nearest = table[0:1]
    for turn in range(1, sub_count):
        part = shifted(table[turn : turn + 1], "sub", sub_order, -turn)
        nearest = jnp.maximum(nearest, part)
    for distance, value in zip(one_way, outs[mem_count:]):
        nearest = jnp.maximum(nearest, shifted(value, "clus", ring, -distance))
    return nearest.reshape(row_count)


def solution(mesh):
    placed = (
        P(("parts", "clus", "mem", "sub"), None),
        P(("parts", "clus", "mem", "sub")),
        P(("parts", "clus", "mem", "sub")),
    )
    return jax.shard_map(
        body,
        mesh=mesh,
        in_specs=placed,
        out_specs=P(("parts", "clus", "mem", "sub")),
        check_vma=False,
    )
```

```python
import jax
import jax.numpy as jnp
from jax import lax
from jax.experimental import pallas as pl
from jax.experimental.pallas import tpu as pltpu
from jax.sharding import PartitionSpec as P

LANES = 128
SUBLANES = 8
META_ROWS = 16
DIGIT = 256
VMEM_LIMIT = 24 * 1024 * 1024
NT = (((1,), (1,)), ((), ()))
NONE = -1.0


def meta_kernel(label_ref, rank_ref, meta_ref):
    kind = lax.broadcasted_iota(jnp.int32, meta_ref.shape, 0)
    rank = rank_ref[...]
    meta = jnp.where(kind == 0, label_ref[...], 0)
    meta = jnp.where(kind == 1, rank // DIGIT, meta)
    meta = jnp.where(kind == 2, rank % DIGIT, meta)
    meta_ref[...] = meta.astype(jnp.float32).astype(jnp.bfloat16)


def pack_kernel(meta_ref, chunks_ref, message_ref, sem):
    chunk_rows = chunks_ref.shape[0]
    copy = pltpu.make_async_copy(chunks_ref, message_ref.at[pl.ds(0, chunk_rows), :], sem)
    copy.start()
    message_ref[pl.ds(chunk_rows, META_ROWS), :] = meta_ref[...]
    copy.wait()


def rows_of(message):
    rows = message.shape[1]
    chunks = message.shape[0] // rows
    return jnp.concatenate([message[c * rows : (c + 1) * rows, :] for c in range(chunks)], axis=1)


def meta_of(message):
    meta = message[message.shape[0] - META_ROWS :, :].astype(jnp.float32)
    return meta[0:1], meta[1:2] * DIGIT + meta[2:3]


def best_kernel(line_count, back_count, mem_count, sub_count, *refs):
    plane_count = mem_count * sub_count
    chip, refs = refs[:sub_count], refs[sub_count:]
    turned_count = (mem_count - 1) * (sub_count - 1)
    turned, refs = refs[:turned_count], refs[turned_count:]
    one_way, refs = refs[:back_count], refs[back_count:]
    straight, refs = refs[: mem_count - 1], refs[mem_count - 1 :]
    both_ways, outs = refs[: line_count - 1 - back_count], refs[line_count - 1 - back_count :]
    lines = chip[:1] + one_way + both_ways
    plane = list(chip)
    for index, block in enumerate(straight):
        plane += [block, *turned[index * (sub_count - 1) : (index + 1) * (sub_count - 1)]]
    plane_outs, back_outs = outs[:mem_count], outs[mem_count:]
    rows = lines[0].shape[1]

    line_rows = jnp.concatenate([rows_of(line) for line in lines], axis=0)
    plane_rows = jnp.concatenate([rows_of(block) for block in plane], axis=0)
    metas = [part for line in lines for part in meta_of(line)]
    metas += [metas[-1]] * (-len(metas) % SUBLANES)
    columns = jnp.transpose(jnp.concatenate(metas, axis=0))
    line_label, line_rank = [
        jnp.concatenate(
            [columns[:, 2 * index + part : 2 * index + part + 1] for index in range(line_count)],
            axis=0,
        )
        for part in range(2)
    ]
    label, rank = [jnp.concatenate(parts, axis=1) for parts in zip(*map(meta_of, plane))]

    scores = lax.dot_general(line_rows, plane_rows, NT, preferred_element_type=jnp.float32)
    scores = jnp.where(line_label == label, scores, NONE)
    forward = jnp.where(line_rank < rank, scores, NONE)
    best = jnp.max(forward, axis=0, keepdims=True)
    for block in range(plane_count):
        shift, turn = block // sub_count, block % sub_count
        plane_outs[shift][turn : turn + 1, :] = best[:, block * rows : (block + 1) * rows]
    for index in range(back_count):
        piece = slice((index + 1) * rows, (index + 2) * rows)
        backward = jnp.where(line_rank[piece] > rank, scores[piece], NONE)
        back = backward[:, :rows]
        for block in range(1, plane_count):
            back = jnp.maximum(back, backward[:, block * rows : (block + 1) * rows])
        back_outs[index][...] = jnp.max(jnp.transpose(back), axis=0, keepdims=True)


def body(embeddings, labels, member_rank):
    row_count, feature_count = embeddings.shape
    clus_count = lax.axis_size("clus")
    mem_count = lax.axis_size("mem")
    sub_count = lax.axis_size("sub")
    chunk_count = feature_count // LANES
    vmem = pl.BlockSpec(memory_space=pltpu.VMEM)
    params = pltpu.CompilerParams(vmem_limit_bytes=VMEM_LIMIT)

    def shifted(value, axis, order, distance):
        count = len(order)
        pairs = [(order[i], order[(i + distance) % count]) for i in range(count)]
        return lax.ppermute(value, axis, pairs)

    half = (clus_count + 1) // 2
    ring = [z for pair in zip(range(half), range(half, 2 * half)) for z in pair if z < clus_count]
    mem_order = list(range(mem_count))
    sub_order = list(range(sub_count))

    meta = pl.pallas_call(
        meta_kernel,
        out_shape=jax.ShapeDtypeStruct((META_ROWS, row_count), jnp.bfloat16),
        in_specs=[vmem, vmem],
        out_specs=vmem,
        compiler_params=params,
        name="meta",
    )(labels.reshape(1, row_count), member_rank.reshape(1, row_count))
    meta, rows = lax.optimization_barrier((meta, embeddings))
    chunks = rows.reshape(row_count, chunk_count, LANES).transpose(1, 0, 2)
    message = pl.pallas_call(
        pack_kernel,
        out_shape=jax.ShapeDtypeStruct((chunk_count * row_count + META_ROWS, LANES), jnp.bfloat16),
        in_specs=[vmem, pl.BlockSpec(memory_space=pl.ANY)],
        out_specs=vmem,
        scratch_shapes=[pltpu.SemaphoreType.DMA(())],
        compiler_params=params,
        name="pack",
    )(meta, chunks.reshape(chunk_count * row_count, LANES))

    distances = list(range(1, clus_count // 2 + 1))
    one_way = [d for d in distances if 2 * d != clus_count]
    lines = [message] + [shifted(message, "clus", ring, d) for d in distances]
    def from_plane(value, shift, turn):
        pairs = [
            (m * sub_count + c, (m + shift) % mem_count * sub_count + (c + turn) % sub_count)
            for m in range(mem_count)
            for c in range(sub_count)
        ]
        return lax.ppermute(value, ("mem", "sub"), pairs) if shift or turn else value

    plane = [
        from_plane(message, shift, turn)
        for shift in range(mem_count)
        for turn in range(sub_count)
    ]

    outs = pl.pallas_call(
        lambda *refs: best_kernel(len(lines), len(one_way), mem_count, sub_count, *refs),
        out_shape=[jax.ShapeDtypeStruct((sub_count, row_count), jnp.float32)] * mem_count
        + [jax.ShapeDtypeStruct((1, row_count), jnp.float32)] * len(one_way),
        in_specs=[vmem] * (len(lines) - 1 + len(plane)),
        out_specs=[vmem] * (mem_count + len(one_way)),
        compiler_params=params,
        name="best",
    )(
        *plane[:sub_count],
        *[block for index, block in enumerate(plane) if index > sub_count and index % sub_count],
        *lines[1 : 1 + len(one_way)],
        *plane[sub_count::sub_count],
        *lines[1 + len(one_way) :],
    )
    table = outs[0]
    for shift in range(1, mem_count):
        table = jnp.maximum(table, shifted(outs[shift], "mem", mem_order, -shift))
    nearest = table[0:1]
    for turn in range(1, sub_count):
        part = shifted(table[turn : turn + 1], "sub", sub_order, -turn)
        nearest = jnp.maximum(nearest, part)
    for distance, value in zip(one_way, outs[mem_count:]):
        nearest = jnp.maximum(nearest, shifted(value, "clus", ring, -distance))
    return nearest.reshape(row_count)


def solution(mesh):
    placed = (
        P(("parts", "clus", "mem", "sub"), None),
        P(("parts", "clus", "mem", "sub")),
        P(("parts", "clus", "mem", "sub")),
    )
    return jax.shard_map(
        body,
        mesh=mesh,
        in_specs=placed,
        out_specs=P(("parts", "clus", "mem", "sub")),
        check_vma=False,
    )
```

```python
import jax
import jax.numpy as jnp
from jax import lax
from jax.experimental import pallas as pl
from jax.experimental.pallas import tpu as pltpu
from jax.sharding import PartitionSpec as P

LANES = 128
SUBLANES = 8
META_ROWS = 16
DIGIT = 256
VMEM_LIMIT = 24 * 1024 * 1024
NT = (((1,), (1,)), ((), ()))
NONE = -1.0


def meta_kernel(label_ref, rank_ref, meta_ref):
    kind = lax.broadcasted_iota(jnp.int32, meta_ref.shape, 0)
    rank = rank_ref[...]
    meta = jnp.where(kind == 0, label_ref[...], 0)
    meta = jnp.where(kind == 1, rank // DIGIT, meta)
    meta = jnp.where(kind == 2, rank % DIGIT, meta)
    meta_ref[...] = meta.astype(jnp.float32).astype(jnp.bfloat16)


def pack_kernel(meta_ref, chunks_ref, message_ref, sem):
    chunk_rows = chunks_ref.shape[0]
    copy = pltpu.make_async_copy(chunks_ref, message_ref.at[pl.ds(0, chunk_rows), :], sem)
    copy.start()
    message_ref[pl.ds(chunk_rows, META_ROWS), :] = meta_ref[...]
    copy.wait()


def stage_kernel(*refs):
    half = len(refs) // 2
    for source, target in zip(refs[:half], refs[half:]):
        target[...] = source[...]


def rows_of(message):
    rows = message.shape[1]
    chunks = message.shape[0] // rows
    return jnp.concatenate([message[c * rows : (c + 1) * rows, :] for c in range(chunks)], axis=1)


def meta_of(message):
    meta = message[message.shape[0] - META_ROWS :, :].astype(jnp.float32)
    return meta[0:1], meta[1:2] * DIGIT + meta[2:3]


def best_kernel(line_count, back_count, mem_count, sub_count, *refs):
    plane_count = mem_count * sub_count
    lines = refs[line_count - 1 : line_count] + refs[: line_count - 1]
    plane = refs[line_count : line_count + plane_count]
    outs = refs[line_count + plane_count :]
    plane_outs, back_outs = outs[:mem_count], outs[mem_count:]
    rows = lines[0].shape[1]

    line_rows = jnp.concatenate([rows_of(line) for line in lines], axis=0)
    plane_rows = jnp.concatenate([rows_of(block) for block in plane], axis=0)
    metas = [part for line in lines for part in meta_of(line)]
    metas += [metas[-1]] * (-len(metas) % SUBLANES)
    columns = jnp.transpose(jnp.concatenate(metas, axis=0))
    line_label, line_rank = [
        jnp.concatenate(
            [columns[:, 2 * index + part : 2 * index + part + 1] for index in range(line_count)],
            axis=0,
        )
        for part in range(2)
    ]
    label, rank = [jnp.concatenate(parts, axis=1) for parts in zip(*map(meta_of, plane))]

    scores = lax.dot_general(line_rows, plane_rows, NT, preferred_element_type=jnp.float32)
    scores = jnp.where(line_label == label, scores, NONE)
    forward = jnp.where(line_rank < rank, scores, NONE)
    best = jnp.max(forward, axis=0, keepdims=True)
    for block in range(plane_count):
        shift, turn = block // sub_count, block % sub_count
        plane_outs[shift][turn : turn + 1, :] = best[:, block * rows : (block + 1) * rows]
    for index in range(back_count):
        piece = slice((index + 1) * rows, (index + 2) * rows)
        backward = jnp.where(line_rank[piece] > rank, scores[piece], NONE)
        back = backward[:, :rows]
        for block in range(1, plane_count):
            back = jnp.maximum(back, backward[:, block * rows : (block + 1) * rows])
        back_outs[index][...] = jnp.max(jnp.transpose(back), axis=0, keepdims=True)


def body(embeddings, labels, member_rank):
    row_count, feature_count = embeddings.shape
    clus_count = lax.axis_size("clus")
    mem_count = lax.axis_size("mem")
    sub_count = lax.axis_size("sub")
    chunk_count = feature_count // LANES
    vmem = pl.BlockSpec(memory_space=pltpu.VMEM)
    params = pltpu.CompilerParams(vmem_limit_bytes=VMEM_LIMIT)

    def shifted(value, axis, order, distance):
        count = len(order)
        pairs = [(order[i], order[(i + distance) % count]) for i in range(count)]
        return lax.ppermute(value, axis, pairs)

    half = (clus_count + 1) // 2
    ring = [z for pair in zip(range(half), range(half, 2 * half)) for z in pair if z < clus_count]
    mem_order = list(range(mem_count))
    sub_order = list(range(sub_count))

    meta = pl.pallas_call(
        meta_kernel,
        out_shape=jax.ShapeDtypeStruct((META_ROWS, row_count), jnp.bfloat16),
        in_specs=[vmem, vmem],
        out_specs=vmem,
        compiler_params=params,
        name="meta",
    )(labels.reshape(1, row_count), member_rank.reshape(1, row_count))
    meta, rows = lax.optimization_barrier((meta, embeddings))
    chunks = rows.reshape(row_count, chunk_count, LANES).transpose(1, 0, 2)
    message = pl.pallas_call(
        pack_kernel,
        out_shape=jax.ShapeDtypeStruct((chunk_count * row_count + META_ROWS, LANES), jnp.bfloat16),
        in_specs=[vmem, pl.BlockSpec(memory_space=pl.ANY)],
        out_specs=vmem,
        scratch_shapes=[pltpu.SemaphoreType.DMA(())],
        compiler_params=params,
        name="pack",
    )(meta, chunks.reshape(chunk_count * row_count, LANES))

    distances = list(range(1, clus_count // 2 + 1))
    one_way = [d for d in distances if 2 * d != clus_count]
    lines = [message] + [shifted(message, "clus", ring, d) for d in distances]
    def near_blocks(block):
        near = []
        for shift in range(mem_count):
            straight = shifted(block, "mem", mem_order, shift) if shift else block
            near.extend([straight] if shift else [])
            near.extend(shifted(straight, "sub", sub_order, t) for t in range(1, sub_count))
        return near

    near = lax.cond(
        lax.axis_index("clus") < clus_count,
        near_blocks,
        lambda block: [jnp.zeros_like(block)] * (sub_count * mem_count - 1),
        message,
    )
    near = pl.pallas_call(
        stage_kernel,
        out_shape=[jax.ShapeDtypeStruct(message.shape, message.dtype)] * len(near),
        in_specs=[vmem] * len(near),
        out_specs=[vmem] * len(near),
        compiler_params=params,
        name="stage",
    )(*near)
    plane = [message, *near]

    outs = pl.pallas_call(
        lambda *refs: best_kernel(len(lines), len(one_way), mem_count, sub_count, *refs),
        out_shape=[jax.ShapeDtypeStruct((sub_count, row_count), jnp.float32)] * mem_count
        + [jax.ShapeDtypeStruct((1, row_count), jnp.float32)] * len(one_way),
        in_specs=[vmem] * (len(lines) + len(plane)),
        out_specs=[vmem] * (mem_count + len(one_way)),
        compiler_params=params,
        name="best",
    )(*lines[1:], *lines[:1], *plane)
    table = outs[0]
    for shift in range(1, mem_count):
        table = jnp.maximum(table, shifted(outs[shift], "mem", mem_order, -shift))
    nearest = table[0:1]
    for turn in range(1, sub_count):
        part = shifted(table[turn : turn + 1], "sub", sub_order, -turn)
        nearest = jnp.maximum(nearest, part)
    for distance, value in zip(one_way, outs[mem_count:]):
        nearest = jnp.maximum(nearest, shifted(value, "clus", ring, -distance))
    return nearest.reshape(row_count)


def solution(mesh):
    placed = (
        P(("parts", "clus", "mem", "sub"), None),
        P(("parts", "clus", "mem", "sub")),
        P(("parts", "clus", "mem", "sub")),
    )
    return jax.shard_map(
        body,
        mesh=mesh,
        in_specs=placed,
        out_specs=P(("parts", "clus", "mem", "sub")),
        check_vma=False,
    )
```

```python
import jax
import jax.numpy as jnp
from jax import lax
from jax.experimental import pallas as pl
from jax.experimental.pallas import tpu as pltpu
from jax.sharding import PartitionSpec as P

LANES = 128
SUBLANES = 8
META_ROWS = 16
DIGIT = 256
VMEM_LIMIT = 24 * 1024 * 1024
NT = (((1,), (1,)), ((), ()))
NONE = -1.0


def meta_kernel(label_ref, rank_ref, meta_ref):
    kind = lax.broadcasted_iota(jnp.int32, meta_ref.shape, 0)
    rank = rank_ref[...]
    meta = jnp.where(kind == 0, label_ref[...], 0)
    meta = jnp.where(kind == 1, rank // DIGIT, meta)
    meta = jnp.where(kind == 2, rank % DIGIT, meta)
    meta_ref[...] = meta.astype(jnp.float32).astype(jnp.bfloat16)


def pack_kernel(meta_ref, chunks_ref, message_ref, sem):
    chunk_rows = chunks_ref.shape[0]
    copy = pltpu.make_async_copy(chunks_ref, message_ref.at[pl.ds(0, chunk_rows), :], sem)
    copy.start()
    message_ref[pl.ds(chunk_rows, META_ROWS), :] = meta_ref[...]
    copy.wait()


def stage_kernel(*refs):
    half = len(refs) // 2
    for source, target in zip(refs[:half], refs[half:]):
        target[...] = source[...]


def rows_of(message):
    rows = message.shape[1]
    chunks = message.shape[0] // rows
    return jnp.concatenate([message[c * rows : (c + 1) * rows, :] for c in range(chunks)], axis=1)


def meta_of(message):
    meta = message[message.shape[0] - META_ROWS :, :].astype(jnp.float32)
    return meta[0:1], meta[1:2] * DIGIT + meta[2:3]


def best_kernel(line_count, back_count, table_count, mem_count, sub_count, *refs):
    plane_count = mem_count * sub_count
    lines, refs = refs[:line_count], refs[line_count:]
    plane, refs = refs[:plane_count], refs[plane_count:]
    tables, outs = refs[:table_count], refs[table_count:]
    plane_outs, back_outs = outs[:mem_count], outs[mem_count:]
    rows = lines[0].shape[1]

    line_rows = jnp.concatenate([rows_of(line) for line in lines], axis=0)
    plane_rows = jnp.concatenate([rows_of(block) for block in plane], axis=0)
    metas = [part for line in lines for part in meta_of(line)]
    metas += [metas[-1]] * (-len(metas) % SUBLANES)
    columns = jnp.transpose(jnp.concatenate(metas, axis=0))
    line_label, line_rank = [
        jnp.concatenate(
            [columns[:, 2 * index + part : 2 * index + part + 1] for index in range(line_count)],
            axis=0,
        )
        for part in range(2)
    ]
    label, rank = [jnp.concatenate(parts, axis=1) for parts in zip(*map(meta_of, plane))]

    scores = lax.dot_general(line_rows, plane_rows, NT, preferred_element_type=jnp.float32)
    scores = jnp.where(line_label == label, scores, NONE)
    forward = jnp.where(line_rank < rank, scores, NONE)
    best = jnp.max(forward, axis=0, keepdims=True)
    for block in range(plane_count):
        shift, turn = block // sub_count, block % sub_count
        part = best[:, block * rows : (block + 1) * rows]
        if table_count:
            part = jnp.maximum(part, tables[shift][turn : turn + 1, :])
        plane_outs[shift][turn : turn + 1, :] = part
    for index in range(back_count):
        piece = slice(index * rows, (index + 1) * rows)
        backward = jnp.where(line_rank[piece] > rank, scores[piece], NONE)
        back = backward[:, :rows]
        for block in range(1, plane_count):
            back = jnp.maximum(back, backward[:, block * rows : (block + 1) * rows])
        back_outs[index][...] = jnp.max(jnp.transpose(back), axis=0, keepdims=True)


def body(embeddings, labels, member_rank):
    row_count, feature_count = embeddings.shape
    clus_count = lax.axis_size("clus")
    mem_count = lax.axis_size("mem")
    sub_count = lax.axis_size("sub")
    chunk_count = feature_count // LANES
    vmem = pl.BlockSpec(memory_space=pltpu.VMEM)
    params = pltpu.CompilerParams(vmem_limit_bytes=VMEM_LIMIT)

    def shifted(value, axis, order, distance):
        count = len(order)
        pairs = [(order[i], order[(i + distance) % count]) for i in range(count)]
        return lax.ppermute(value, axis, pairs)

    half = (clus_count + 1) // 2
    ring = [z for pair in zip(range(half), range(half, 2 * half)) for z in pair if z < clus_count]
    mem_order = list(range(mem_count))
    sub_order = list(range(sub_count))

    meta = pl.pallas_call(
        meta_kernel,
        out_shape=jax.ShapeDtypeStruct((META_ROWS, row_count), jnp.bfloat16),
        in_specs=[vmem, vmem],
        out_specs=vmem,
        compiler_params=params,
        name="meta",
    )(labels.reshape(1, row_count), member_rank.reshape(1, row_count))
    meta, rows = lax.optimization_barrier((meta, embeddings))
    chunks = rows.reshape(row_count, chunk_count, LANES).transpose(1, 0, 2)
    message = pl.pallas_call(
        pack_kernel,
        out_shape=jax.ShapeDtypeStruct((chunk_count * row_count + META_ROWS, LANES), jnp.bfloat16),
        in_specs=[vmem, pl.BlockSpec(memory_space=pl.ANY)],
        out_specs=vmem,
        scratch_shapes=[pltpu.SemaphoreType.DMA(())],
        compiler_params=params,
        name="pack",
    )(meta, chunks.reshape(chunk_count * row_count, LANES))

    distances = list(range(1, clus_count // 2 + 1))
    one_way = [d for d in distances if 2 * d != clus_count]
    lines = [message] + [shifted(message, "clus", ring, d) for d in distances]
    def near_blocks(block):
        near = []
        for shift in range(mem_count):
            straight = shifted(block, "mem", mem_order, shift) if shift else block
            near.extend([straight] if shift else [])
            near.extend(shifted(straight, "sub", sub_order, t) for t in range(1, sub_count))
        return near

    near = lax.cond(
        lax.axis_index("clus") < clus_count,
        near_blocks,
        lambda block: [jnp.zeros_like(block)] * (sub_count * mem_count - 1),
        message,
    )
    near = pl.pallas_call(
        stage_kernel,
        out_shape=[jax.ShapeDtypeStruct(message.shape, message.dtype)] * len(near),
        in_specs=[vmem] * len(near),
        out_specs=[vmem] * len(near),
        compiler_params=params,
        name="stage",
    )(*near)
    plane = [message, *near]

    def best_of(lines, back_count, tables):
        operands = [*lines, *plane, *tables]
        outs = pl.pallas_call(
            lambda *refs: best_kernel(
                len(lines), back_count, len(tables), mem_count, sub_count, *refs
            ),
            out_shape=[jax.ShapeDtypeStruct((sub_count, row_count), jnp.float32)] * mem_count
            + [jax.ShapeDtypeStruct((1, row_count), jnp.float32)] * back_count,
            in_specs=[vmem] * len(operands),
            out_specs=[vmem] * (mem_count + back_count),
            compiler_params=params,
            name="best",
        )(*operands)
        return outs[:mem_count], outs[mem_count:]

    tables, _ = best_of(lines[:1], 0, [])
    backs = []
    if one_way:
        tables, backs = best_of(lines[1 : 1 + len(one_way)], len(one_way), tables)
    if len(lines) > 1 + len(one_way):
        tables, _ = best_of(lines[1 + len(one_way) :], 0, tables)
    table = tables[0]
    for shift in range(1, mem_count):
        table = jnp.maximum(table, shifted(tables[shift], "mem", mem_order, -shift))
    nearest = table[0:1]
    for turn in range(1, sub_count):
        part = shifted(table[turn : turn + 1], "sub", sub_order, -turn)
        nearest = jnp.maximum(nearest, part)
    for distance, value in zip(one_way, backs):
        nearest = jnp.maximum(nearest, shifted(value, "clus", ring, -distance))
    return nearest.reshape(row_count)


def solution(mesh):
    placed = (
        P(("parts", "clus", "mem", "sub"), None),
        P(("parts", "clus", "mem", "sub")),
        P(("parts", "clus", "mem", "sub")),
    )
    return jax.shard_map(
        body,
        mesh=mesh,
        in_specs=placed,
        out_specs=P(("parts", "clus", "mem", "sub")),
        check_vma=False,
    )
```

```python
import jax
import jax.numpy as jnp
from jax import lax
from jax.experimental import pallas as pl
from jax.experimental.pallas import tpu as pltpu
from jax.sharding import PartitionSpec as P

LANES = 128
SUBLANES = 8
META_ROWS = 16
DIGIT = 256
VMEM_LIMIT = 24 * 1024 * 1024
NT = (((1,), (1,)), ((), ()))
NONE = -1.0


def meta_kernel(label_ref, rank_ref, meta_ref):
    kind = lax.broadcasted_iota(jnp.int32, meta_ref.shape, 0)
    rank = rank_ref[...]
    meta = jnp.where(kind == 0, label_ref[...], 0)
    meta = jnp.where(kind == 1, rank // DIGIT, meta)
    meta = jnp.where(kind == 2, rank % DIGIT, meta)
    meta_ref[...] = meta.astype(jnp.float32).astype(jnp.bfloat16)


def pack_kernel(meta_ref, chunks_ref, message_ref, sem):
    chunk_rows = chunks_ref.shape[0]
    copy = pltpu.make_async_copy(chunks_ref, message_ref.at[pl.ds(0, chunk_rows), :], sem)
    copy.start()
    message_ref[pl.ds(chunk_rows, META_ROWS), :] = meta_ref[...]
    copy.wait()


def stage_kernel(*refs):
    half = len(refs) // 2
    for source, target in zip(refs[:half], refs[half:]):
        target[...] = source[...]


def rows_of(message):
    rows = message.shape[1]
    chunks = message.shape[0] // rows
    return jnp.concatenate([message[c * rows : (c + 1) * rows, :] for c in range(chunks)], axis=1)


def meta_of(message):
    meta = message[message.shape[0] - META_ROWS :, :].astype(jnp.float32)
    return meta[0:1], meta[1:2] * DIGIT + meta[2:3]


def best_kernel(line_count, back_count, table_count, mem_count, sub_count, *refs):
    plane_count = mem_count * sub_count
    lines, refs = refs[:line_count], refs[line_count:]
    plane, refs = refs[:plane_count], refs[plane_count:]
    tables, outs = refs[:table_count], refs[table_count:]
    plane_outs, back_outs = outs[:mem_count], outs[mem_count:]
    rows = lines[0].shape[1]

    line_rows = jnp.concatenate([rows_of(line) for line in lines], axis=0)
    plane_rows = jnp.concatenate([rows_of(block) for block in plane], axis=0)
    metas = [part for line in lines for part in meta_of(line)]
    metas += [metas[-1]] * (-len(metas) % SUBLANES)
    columns = jnp.transpose(jnp.concatenate(metas, axis=0))
    line_label, line_rank = [
        jnp.concatenate(
            [columns[:, 2 * index + part : 2 * index + part + 1] for index in range(line_count)],
            axis=0,
        )
        for part in range(2)
    ]
    label, rank = [jnp.concatenate(parts, axis=1) for parts in zip(*map(meta_of, plane))]

    scores = lax.dot_general(line_rows, plane_rows, NT, preferred_element_type=jnp.float32)
    scores = jnp.where(line_label == label, scores, NONE)
    forward = jnp.where(line_rank < rank, scores, NONE)
    best = jnp.max(forward, axis=0, keepdims=True)
    for block in range(plane_count):
        shift, turn = block // sub_count, block % sub_count
        part = best[:, block * rows : (block + 1) * rows]
        if table_count:
            part = jnp.maximum(part, tables[shift][turn : turn + 1, :])
        plane_outs[shift][turn : turn + 1, :] = part
    for index in range(back_count):
        piece = slice(index * rows, (index + 1) * rows)
        backward = jnp.where(line_rank[piece] > rank, scores[piece], NONE)
        back = backward[:, :rows]
        for block in range(1, plane_count):
            back = jnp.maximum(back, backward[:, block * rows : (block + 1) * rows])
        back_outs[index][...] = jnp.max(jnp.transpose(back), axis=0, keepdims=True)


def body(embeddings, labels, member_rank):
    row_count, feature_count = embeddings.shape
    clus_count = lax.axis_size("clus")
    mem_count = lax.axis_size("mem")
    sub_count = lax.axis_size("sub")
    chunk_count = feature_count // LANES
    vmem = pl.BlockSpec(memory_space=pltpu.VMEM)
    params = pltpu.CompilerParams(vmem_limit_bytes=VMEM_LIMIT)

    def shifted(value, axis, order, distance):
        count = len(order)
        pairs = [(order[i], order[(i + distance) % count]) for i in range(count)]
        return lax.ppermute(value, axis, pairs)

    half = (clus_count + 1) // 2
    ring = [z for pair in zip(range(half), range(half, 2 * half)) for z in pair if z < clus_count]
    mem_order = list(range(mem_count))
    sub_order = list(range(sub_count))

    meta = pl.pallas_call(
        meta_kernel,
        out_shape=jax.ShapeDtypeStruct((META_ROWS, row_count), jnp.bfloat16),
        in_specs=[vmem, vmem],
        out_specs=vmem,
        compiler_params=params,
        name="meta",
    )(labels.reshape(1, row_count), member_rank.reshape(1, row_count))
    meta, rows = lax.optimization_barrier((meta, embeddings))
    chunks = rows.reshape(row_count, chunk_count, LANES).transpose(1, 0, 2)
    message = pl.pallas_call(
        pack_kernel,
        out_shape=jax.ShapeDtypeStruct((chunk_count * row_count + META_ROWS, LANES), jnp.bfloat16),
        in_specs=[vmem, pl.BlockSpec(memory_space=pl.ANY)],
        out_specs=vmem,
        scratch_shapes=[pltpu.SemaphoreType.DMA(())],
        compiler_params=params,
        name="pack",
    )(meta, chunks.reshape(chunk_count * row_count, LANES))

    distances = list(range(1, clus_count // 2 + 1))
    one_way = [d for d in distances if 2 * d != clus_count]
    lines = [message] + [shifted(message, "clus", ring, d) for d in distances]
    def near_blocks(block):
        near = []
        for shift in range(mem_count):
            straight = shifted(block, "mem", mem_order, shift) if shift else block
            near.extend([straight] if shift else [])
            near.extend(shifted(straight, "sub", sub_order, t) for t in range(1, sub_count))
        return near

    near = lax.cond(
        lax.axis_index("clus") < clus_count,
        near_blocks,
        lambda block: [jnp.zeros_like(block)] * (sub_count * mem_count - 1),
        message,
    )
    near = pl.pallas_call(
        stage_kernel,
        out_shape=[jax.ShapeDtypeStruct(message.shape, message.dtype)] * len(near),
        in_specs=[vmem] * len(near),
        out_specs=[vmem] * len(near),
        compiler_params=params,
        name="stage",
    )(*near)
    plane = [message, *near]

    def best_of(lines, back_count, tables):
        operands = [*lines, *plane, *tables]
        outs = pl.pallas_call(
            lambda *refs: best_kernel(
                len(lines), back_count, len(tables), mem_count, sub_count, *refs
            ),
            out_shape=[jax.ShapeDtypeStruct((sub_count, row_count), jnp.float32)] * mem_count
            + [jax.ShapeDtypeStruct((1, row_count), jnp.float32)] * back_count,
            in_specs=[vmem] * len(operands),
            out_specs=[vmem] * (mem_count + back_count),
            compiler_params=params,
            name="best",
        )(*operands)
        return outs[:mem_count], outs[mem_count:]

    near_lines = lines[1 : 1 + len(one_way)] + lines[:1]
    tables, backs = best_of(near_lines, len(one_way), [])
    if len(lines) > 1 + len(one_way):
        tables, _ = best_of(lines[1 + len(one_way) :], 0, tables)
    table = tables[0]
    for shift in range(1, mem_count):
        table = jnp.maximum(table, shifted(tables[shift], "mem", mem_order, -shift))
    nearest = table[0:1]
    for turn in range(1, sub_count):
        part = shifted(table[turn : turn + 1], "sub", sub_order, -turn)
        nearest = jnp.maximum(nearest, part)
    for distance, value in zip(one_way, backs):
        nearest = jnp.maximum(nearest, shifted(value, "clus", ring, -distance))
    return nearest.reshape(row_count)


def solution(mesh):
    placed = (
        P(("parts", "clus", "mem", "sub"), None),
        P(("parts", "clus", "mem", "sub")),
        P(("parts", "clus", "mem", "sub")),
    )
    return jax.shard_map(
        body,
        mesh=mesh,
        in_specs=placed,
        out_specs=P(("parts", "clus", "mem", "sub")),
        check_vma=False,
    )
```

```python
import jax
import jax.numpy as jnp
from jax import lax
from jax.experimental import pallas as pl
from jax.experimental.pallas import tpu as pltpu
from jax.sharding import PartitionSpec as P

LANES = 128
SUBLANES = 8
META_ROWS = 16
DIGIT = 256
VMEM_LIMIT = 24 * 1024 * 1024
NT = (((1,), (1,)), ((), ()))
NONE = -1.0


def meta_kernel(label_ref, rank_ref, meta_ref):
    kind = lax.broadcasted_iota(jnp.int32, meta_ref.shape, 0)
    rank = rank_ref[...]
    meta = jnp.where(kind == 0, label_ref[...], 0)
    meta = jnp.where(kind == 1, rank // DIGIT, meta)
    meta = jnp.where(kind == 2, rank % DIGIT, meta)
    meta_ref[...] = meta.astype(jnp.float32).astype(jnp.bfloat16)


def pack_kernel(meta_ref, chunks_ref, message_ref, sem):
    chunk_rows = chunks_ref.shape[0]
    copy = pltpu.make_async_copy(chunks_ref, message_ref.at[pl.ds(0, chunk_rows), :], sem)
    copy.start()
    message_ref[pl.ds(chunk_rows, META_ROWS), :] = meta_ref[...]
    copy.wait()


def rows_of(message):
    rows = message.shape[1]
    chunks = message.shape[0] // rows
    return jnp.concatenate([message[c * rows : (c + 1) * rows, :] for c in range(chunks)], axis=1)


def meta_of(message):
    meta = message[message.shape[0] - META_ROWS :, :].astype(jnp.float32)
    return meta[0:1], meta[1:2] * DIGIT + meta[2:3]


def stage_kernel(*refs):
    blocks, (rows_ref, meta_ref) = refs[:-2], refs[-2:]
    for index, block in enumerate(blocks):
        rows = block.shape[1]
        rows_ref[index * rows : (index + 1) * rows, :] = rows_of(block)
        meta_ref[:, index * rows : (index + 1) * rows] = block[block.shape[0] - META_ROWS :, :]


def best_kernel(line_count, back_count, table_count, mem_count, sub_count, *refs):
    plane_count = mem_count * sub_count
    lines, refs = refs[:line_count], refs[line_count:]
    plane, plane_meta, refs = refs[0], refs[1], refs[2:]
    tables, outs = refs[:table_count], refs[table_count:]
    plane_outs, back_outs = outs[:mem_count], outs[mem_count:]
    rows = lines[0].shape[1]

    line_rows = jnp.concatenate([rows_of(line) for line in lines], axis=0)
    plane_rows = plane[...]
    metas = [part for line in lines for part in meta_of(line)]
    metas += [metas[-1]] * (-len(metas) % SUBLANES)
    columns = jnp.transpose(jnp.concatenate(metas, axis=0))
    line_label, line_rank = [
        jnp.concatenate(
            [columns[:, 2 * index + part : 2 * index + part + 1] for index in range(line_count)],
            axis=0,
        )
        for part in range(2)
    ]
    label, rank = meta_of(plane_meta)

    scores = lax.dot_general(line_rows, plane_rows, NT, preferred_element_type=jnp.float32)
    scores = jnp.where(line_label == label, scores, NONE)
    forward = jnp.where(line_rank < rank, scores, NONE)
    best = jnp.max(forward, axis=0, keepdims=True)
    for block in range(plane_count):
        shift, turn = block // sub_count, block % sub_count
        part = best[:, block * rows : (block + 1) * rows]
        if table_count:
            part = jnp.maximum(part, tables[shift][turn : turn + 1, :])
        plane_outs[shift][turn : turn + 1, :] = part
    for index in range(back_count):
        piece = slice(index * rows, (index + 1) * rows)
        backward = jnp.where(line_rank[piece] > rank, scores[piece], NONE)
        back = backward[:, :rows]
        for block in range(1, plane_count):
            back = jnp.maximum(back, backward[:, block * rows : (block + 1) * rows])
        back_outs[index][...] = jnp.max(jnp.transpose(back), axis=0, keepdims=True)


def body(embeddings, labels, member_rank):
    row_count, feature_count = embeddings.shape
    clus_count = lax.axis_size("clus")
    mem_count = lax.axis_size("mem")
    sub_count = lax.axis_size("sub")
    chunk_count = feature_count // LANES
    vmem = pl.BlockSpec(memory_space=pltpu.VMEM)
    params = pltpu.CompilerParams(vmem_limit_bytes=VMEM_LIMIT)

    def shifted(value, axis, order, distance):
        count = len(order)
        pairs = [(order[i], order[(i + distance) % count]) for i in range(count)]
        return lax.ppermute(value, axis, pairs)

    half = (clus_count + 1) // 2
    ring = [z for pair in zip(range(half), range(half, 2 * half)) for z in pair if z < clus_count]
    mem_order = list(range(mem_count))
    sub_order = list(range(sub_count))

    meta = pl.pallas_call(
        meta_kernel,
        out_shape=jax.ShapeDtypeStruct((META_ROWS, row_count), jnp.bfloat16),
        in_specs=[vmem, vmem],
        out_specs=vmem,
        compiler_params=params,
        name="meta",
    )(labels.reshape(1, row_count), member_rank.reshape(1, row_count))
    meta, rows = lax.optimization_barrier((meta, embeddings))
    chunks = rows.reshape(row_count, chunk_count, LANES).transpose(1, 0, 2)
    message = pl.pallas_call(
        pack_kernel,
        out_shape=jax.ShapeDtypeStruct((chunk_count * row_count + META_ROWS, LANES), jnp.bfloat16),
        in_specs=[vmem, pl.BlockSpec(memory_space=pl.ANY)],
        out_specs=vmem,
        scratch_shapes=[pltpu.SemaphoreType.DMA(())],
        compiler_params=params,
        name="pack",
    )(meta, chunks.reshape(chunk_count * row_count, LANES))

    distances = list(range(1, clus_count // 2 + 1))
    one_way = [d for d in distances if 2 * d != clus_count]
    lines = [message] + [shifted(message, "clus", ring, d) for d in distances]
    def near_blocks(block):
        near = []
        for shift in range(mem_count):
            straight = shifted(block, "mem", mem_order, shift) if shift else block
            near.extend([straight] if shift else [])
            near.extend(shifted(straight, "sub", sub_order, t) for t in range(1, sub_count))
        return near

    near = lax.cond(
        lax.axis_index("clus") < clus_count,
        near_blocks,
        lambda block: [jnp.zeros_like(block)] * (sub_count * mem_count - 1),
        message,
    )
    plane_width = row_count * mem_count * sub_count
    plane = pl.pallas_call(
        stage_kernel,
        out_shape=[
            jax.ShapeDtypeStruct((plane_width, feature_count), jnp.bfloat16),
            jax.ShapeDtypeStruct((META_ROWS, plane_width), jnp.bfloat16),
        ],
        in_specs=[vmem] * (1 + len(near)),
        out_specs=[vmem, vmem],
        compiler_params=params,
        name="stage",
    )(message, *near)

    def best_of(lines, back_count, tables):
        operands = [*lines, *plane, *tables]
        outs = pl.pallas_call(
            lambda *refs: best_kernel(
                len(lines), back_count, len(tables), mem_count, sub_count, *refs
            ),
            out_shape=[jax.ShapeDtypeStruct((sub_count, row_count), jnp.float32)] * mem_count
            + [jax.ShapeDtypeStruct((1, row_count), jnp.float32)] * back_count,
            in_specs=[vmem] * len(operands),
            out_specs=[vmem] * (mem_count + back_count),
            compiler_params=params,
            name="best",
        )(*operands)
        return outs[:mem_count], outs[mem_count:]

    near_lines = lines[1 : 1 + len(one_way)] + lines[:1]
    tables, backs = best_of(near_lines, len(one_way), [])
    if len(lines) > 1 + len(one_way):
        tables, _ = best_of(lines[1 + len(one_way) :], 0, tables)
    table = tables[0]
    for shift in range(1, mem_count):
        table = jnp.maximum(table, shifted(tables[shift], "mem", mem_order, -shift))
    nearest = table[0:1]
    for turn in range(1, sub_count):
        part = shifted(table[turn : turn + 1], "sub", sub_order, -turn)
        nearest = jnp.maximum(nearest, part)
    for distance, value in zip(one_way, backs):
        nearest = jnp.maximum(nearest, shifted(value, "clus", ring, -distance))
    return nearest.reshape(row_count)


def solution(mesh):
    placed = (
        P(("parts", "clus", "mem", "sub"), None),
        P(("parts", "clus", "mem", "sub")),
        P(("parts", "clus", "mem", "sub")),
    )
    return jax.shard_map(
        body,
        mesh=mesh,
        in_specs=placed,
        out_specs=P(("parts", "clus", "mem", "sub")),
        check_vma=False,
    )
```
